32 devices in a mesh: member: 8 (over y, x, core), lon: 4 (over z).
Axes of the slice: x: 2, y: 2, z: 4, core: 2. Of those that a mesh axis runs over, the one named last changes fastest.
Arguments:
- atmos: bfloat16 [8, 96, 96, 512], P('member', None, None, 'lon'), may hold values from -6 to 6
- ocean: bfloat16 [96, 96, 512], P(None, None, 'lon'), may hold values from -6 to 6
- land_mask: int32 [96, 512], P(None, 'lon'), may hold values 0 or 1
- ice_mask: int32 [96, 512], P(None, 'lon'), may hold values 0 or 1
- atm_kernel: float32 [2, 7, 7, 96], replicated, may hold values from -0.875 to 0.875
- atm_gain: float32 [2, 96], replicated, may hold values from 0.25 to 1.75
- atm_up: bfloat16 [2, 96, 384], replicated, may hold values from -0.625 to 0.625
- atm_down: bfloat16 [2, 384, 96], replicated, may hold values from -0.3125 to 0.3125
- atm_scale: float32 [2, 96], replicated, may hold values from 0.5 to 1.5
- flux_weight: bfloat16 [96, 32], replicated, may hold values from -0.625 to 0.625
- flux_lift: bfloat16 [2, 32, 96], replicated, may hold values from -1 to 1
- ocn_kernel: float32 [7, 7, 96], replicated, may hold values from -0.875 to 0.875
- ocn_gain: float32 [96], replicated, may hold values from 0.25 to 1.75
- ocn_up: bfloat16 [96, 384], replicated, may hold values from -0.625 to 0.625
- ocn_down: bfloat16 [384, 96], replicated, may hold values from -0.3125 to 0.3125
- ocn_scale: float32 [96], replicated, may hold values from 0.5 to 1.5
- surf_weight: bfloat16 [96, 8], replicated, may hold values from -0.625 to 0.625
- back_weight: bfloat16 [8, 96], replicated, may hold values from -2 to 2
Outputs:
- atmos_out: bfloat16 [8, 96, 96, 512], P('member', None, None, 'lon')
- ocean_new: bfloat16 [96, 96, 512], P('member', None, 'lon')
The draws below stay inside these ranges and needn't reach their ends.
All inputs are finite; a program needn't handle non-finite values. No bound on the sum of `land_mask` or of `ice_mask` on one device may be relied on, other than what follows from the above.
Results may differ from the reference program's by a relative error of at most 0.017.
Values may be sent and summed in bfloat16 or wider, within the bound.
No kernel may reach another device: no remote copies, remote signals or barrier semaphores. Data moves between devices by JAX's collectives and lax.ppermute only.
A program may use at most 64 MiB of HBM per device.

```python
import jax
import jax.numpy as jnp
from jax import lax

C = 96
HID = 384
FLUX = 32
SURF = 8
LAT = 96
MEMBERS = 8
NLON = 512


def set_ends(values, rng, smallest, largest):
    index_at = [jax.random.randint(jax.random.fold_in(rng, axis), (), 0, length) for axis, length in enumerate(values.shape)]
    longest = values.shape.index(max(values.shape))
    neighbour = index_at[:longest] + [(index_at[longest] + 1) % values.shape[longest]] + index_at[longest + 1:]
    return values.at[tuple(index_at)].set(smallest).at[tuple(neighbour)].set(largest)


def block_scale(own_key, shape, shards, smallest, largest):
    def one(position, parts):
        draws = jax.random.uniform(jax.random.fold_in(jax.random.fold_in(own_key, 6), position), (parts,), jnp.float32, smallest / len(shards), largest / len(shards))
        return jnp.repeat(jnp.exp(draws), shape[position] // parts).reshape((-1,) + (1,) * (len(shape) - position - 1))

    factor_of = one(*shards[0])
    for cut in shards[1:]:
        factor_of = factor_of * one(*cut)
    return factor_of


def centred(own_key, extent, width, limit, shards=(), held_as=jnp.bfloat16):
    values = width * jax.random.normal(own_key, extent, jnp.float32)
    if shards:
        values = values * block_scale(own_key, extent, shards, -0.22, 0.18)
    return jnp.clip(values, -limit, limit).astype(held_as)


def setup_inputs(seed: int = 0) -> dict:
    keys = jax.random.split(jax.random.key(seed), 19)
    return {
        "atmos": centred(keys[0], (MEMBERS, LAT, C, NLON), 1.0, 6.0, ((0, 8), (3, 4))),
        "ocean": centred(keys[1], (LAT, C, NLON), 1.0, 6.0, ((2, 4),)),
        "land_mask": set_ends((jax.random.randint(keys[2], (LAT, NLON), 0, 10) < 3).astype(jnp.int32), jax.random.fold_in(keys[2], 1), 0, 1),
        "ice_mask": set_ends((jax.random.randint(keys[3], (LAT, NLON), 0, 4) < 1).astype(jnp.int32), jax.random.fold_in(keys[3], 1), 0, 1),
        "atm_kernel": centred(keys[4], (2, 7, 7, C), 49 ** -0.5, 0.875, (), jnp.float32),
        "atm_gain": jnp.clip(1.0 + 0.15 * jax.random.normal(keys[5], (2, C), jnp.float32), 0.25, 1.75),
        "atm_up": centred(keys[6], (2, C, HID), C ** -0.5, 0.625),
        "atm_down": centred(keys[7], (2, HID, C), HID ** -0.5, 0.3125),
        "atm_scale": jnp.clip(jax.random.uniform(keys[8], (2, C), jnp.float32, 0.5, 1.5), 0.5, 1.5),
        "flux_weight": centred(keys[9], (C, FLUX), C ** -0.5, 0.625),
        "flux_lift": centred(keys[10], (2, FLUX, C), FLUX ** -0.5, 1.0),
        "ocn_kernel": centred(keys[11], (7, 7, C), 49 ** -0.5, 0.875, (), jnp.float32),
        "ocn_gain": jnp.clip(1.0 + 0.15 * jax.random.normal(keys[12], (C,), jnp.float32), 0.25, 1.75),
        "ocn_up": centred(keys[13], (C, HID), C ** -0.5, 0.625),
        "ocn_down": centred(keys[14], (HID, C), HID ** -0.5, 0.3125),
        "ocn_scale": jnp.clip(jax.random.uniform(keys[15], (C,), jnp.float32, 0.5, 1.5), 0.5, 1.5),
        "surf_weight": centred(keys[16], (C, SURF), C ** -0.5, 0.625),
        "back_weight": centred(keys[17], (SURF, C), SURF ** -0.5, 2.0),
    }


def contract(form, left, right):
    return jnp.einsum(form, left.astype(jnp.float32), right.astype(jnp.float32))

def cycle_pad(field):
    padded = jnp.pad(field, ((3, 3), (0, 0), (0, 0)))
    return jnp.concatenate([padded[:, :, -3:], padded, padded[:, :, :3]], axis=2)

def mixer(field, padded, kernel, gain, up_proj, down_proj, scale, keep):
    rows = field.shape[0]
    cols = field.shape[2]
    acc = jnp.zeros(field.shape, jnp.float32)
    for i in range(7):
        for j in range(7):
            acc = acc + padded[i:i + rows, :, j:j + cols].astype(jnp.float32) * kernel[i, j][:, None]
    center = acc - lax.optimization_barrier(jnp.mean(acc, axis=1, keepdims=True))
    spread = lax.optimization_barrier(jnp.mean(center * center, axis=1, keepdims=True))
    normed = (center * lax.rsqrt(spread + 1e-06) * gain[:, None]).astype(jnp.bfloat16)
    hidden = jax.nn.gelu(contract('lcw,ch->lhw', normed, up_proj)).astype(jnp.bfloat16)
    branch = contract('lhw,hc->lcw', hidden, down_proj)
    result = field.astype(jnp.float32) + scale[:, None] * branch
    if keep is not None:
        result = result * keep[:, None, :]
    return result.astype(jnp.bfloat16)

def reference(atmos, ocean, land_mask, ice_mask, atm_kernel, atm_gain, atm_up, atm_down, atm_scale, flux_weight, flux_lift, ocn_kernel, ocn_gain, ocn_up, ocn_down, ocn_scale, surf_weight, back_weight):
    sea = (1 - land_mask).astype(jnp.float32)
    ice = ice_mask.astype(jnp.float32)

    def member_step(state):
        for layer in range(2):
            state = mixer(state, cycle_pad(state), atm_kernel[layer], atm_gain[layer], atm_up[layer], atm_down[layer], atm_scale[layer], None)
        flux = jax.nn.gelu(contract('lcw,cf->lfw', state, flux_weight))
        return (state, flux)
    blocks, fluxes = lax.map(member_step, atmos)
    flux_low = (lax.optimization_barrier(jnp.sum(fluxes, axis=0)) / MEMBERS).astype(jnp.bfloat16)
    open_term = contract('lfw,fc->lcw', flux_low, flux_lift[0])
    ice_term = contract('lfw,fc->lcw', flux_low, flux_lift[1])
    forcing = sea[:, None, :] * ((1.0 - ice)[:, None, :] * open_term + ice[:, None, :] * ice_term)
    ocean_mid = (ocean.astype(jnp.float32) + forcing).astype(jnp.bfloat16)
    ocean_new = mixer(ocean_mid, cycle_pad(ocean_mid), ocn_kernel, ocn_gain, ocn_up, ocn_down, ocn_scale, sea)
    surface = contract('lcw,cs->lsw', ocean_new, surf_weight).astype(jnp.bfloat16)
    coupling = sea[:, None, :] * contract('lsw,sc->lcw', surface, back_weight)

    def couple(state):
        return (state.astype(jnp.float32) + coupling).astype(jnp.bfloat16)
    atmos_out = lax.map(couple, blocks)
    return (atmos_out, ocean_new)
```

```python
import functools

import jax
import jax.numpy as jnp
from jax import lax
from jax.experimental import pallas as pl
from jax.experimental.pallas import tpu as pltpu
from jax.sharding import PartitionSpec as P

BF = jnp.bfloat16
F32 = jnp.float32
TANH_A = 0.7978845608028654
TANH_B = TANH_A * 0.044715
TAPS = 7
HALO = 3
GROUP = 16
SPAN = 16
OUT = SPAN - TAPS + 1
DEPTH = GROUP * SPAN
SLOT = 8
PACK = 16
BY_DOT = (0, 1, 5, 6)
VMEM = pl.BlockSpec(memory_space=pltpu.VMEM)
ANY = pl.BlockSpec(memory_space=pl.ANY)


def params(mib):
    return pltpu.CompilerParams(vmem_limit_bytes=mib * 2**20)


def twice_gelu(z):
    return z + z * jnp.tanh(z * (TANH_A + TANH_B * (z * z)))


def spread(row, lanes):
    return jnp.broadcast_to(row.T, (row.shape[1], lanes))


def shift_matrix(lanes):
    shape = (2 * lanes, len(BY_DOT) * lanes)
    src = lax.broadcasted_iota(jnp.int32, shape, 0)
    dst = lax.broadcasted_iota(jnp.int32, shape, 1)
    hit = jnp.zeros(shape, jnp.bool_)
    for a, j in enumerate(BY_DOT):
        want = dst - a * lanes + (j - HALO)
        want = jnp.where(want < 0, want + 2 * lanes, want)
        hit = hit | ((dst >= a * lanes) & (dst < (a + 1) * lanes) & (src == want))
    return hit.astype(BF)


def make_shifts(rows, edges, xj, at, smat):
    count, chans, lanes = rows.shape
    lane = lax.broadcasted_iota(jnp.int32, (chans, lanes), 1)
    halo = [edges if t == 0 else pltpu.roll(edges, lanes - SLOT * t, 1) for t in range(count)]
    both = jnp.concatenate(
        [rows.reshape(count * chans, lanes), jnp.concatenate(halo, axis=0)], axis=1
    )
    moved = jnp.dot(both, smat, preferred_element_type=F32)
    for a, j in enumerate(BY_DOT):
        part = moved[:, a * lanes : (a + 1) * lanes].astype(BF)
        xj[j, pl.ds(at, count)] = part.reshape(count, chans, lanes)
    for t in range(count):
        for j in range(TAPS):
            d = j - HALO
            if j in BY_DOT:
                continue
            if d == 0:
                xj[j, at + t] = rows[t]
            else:
                mask = (lane < d) if d > 0 else (lane >= lanes + d)
                xj[j, at + t] = pltpu.roll(jnp.where(mask, halo[t], rows[t]), (-d) % lanes, 1)


def pick_edges(from_left, from_right):
    lane = lax.broadcasted_iota(jnp.int32, from_left.shape, 1)
    return jnp.where(lane % SLOT < SLOT // 2, from_right, from_left)


def pack_edges(rows):
    chans, lanes = rows[0].shape
    lane = lax.broadcasted_iota(jnp.int32, (chans, lanes), 1)
    place = (lane + HALO) // SLOT % PACK
    out = rows[0]
    for t in range(1, PACK):
        if t < len(rows):
            out = jnp.where(place == t, pltpu.roll(rows[t], SLOT * t, 1), out)
    return out


def build_band(taps, band):
    chans = band.shape[0] * GROUP
    wide = TAPS * DEPTH
    t = lax.broadcasted_iota(jnp.int32, (TAPS, wide), 0)
    n = lax.broadcasted_iota(jnp.int32, (TAPS, wide), 1)
    base = jnp.zeros((chans, wide), F32)
    for i in range(TAPS):
        put = ((t == n // DEPTH) & ((n % DEPTH) // GROUP == i)).astype(BF)
        base = base + jnp.dot(taps(i).T.astype(BF), put, preferred_element_type=F32)
    r = lax.broadcasted_iota(jnp.int32, (chans, wide), 0)
    c = lax.broadcasted_iota(jnp.int32, (chans, wide), 1)
    base = jnp.where(r % GROUP == c % GROUP, base, 0.0)
    for j in range(TAPS):
        one = base[:, j * DEPTH : (j + 1) * DEPTH]
        for r in range(OUT):
            moved = (pltpu.roll(one, GROUP * r, 1) if r else one).astype(BF)
            for g in range(band.shape[0]):
                band[g, GROUP * r : GROUP * (r + 1), j * DEPTH : (j + 1) * DEPTH] = moved[
                    GROUP * g : GROUP * (g + 1)
                ]


def convolve(xj, band, acc):
    rows, chans, lanes = acc.shape
    starts = [min(OUT * i, max(rows - OUT, 0)) for i in range(-(-rows // OUT))]

    def group(g, carry):
        at = pl.ds(pl.multiple_of(GROUP * g, GROUP), GROUP)
        field = jnp.concatenate(
            [
                jnp.concatenate(
                    [xj[j, s : s + SPAN, at, :].reshape(DEPTH, lanes) for j in range(TAPS)], axis=0
                )
                for s in starts
            ],
            axis=1,
        )
        out = jnp.dot(band[g], field, preferred_element_type=F32)
        for n, s in enumerate(starts):
            take = min(OUT, rows)
            part = out[: take * GROUP, n * lanes : (n + 1) * lanes]
            acc[s : s + take, at, :] = part.reshape(take, GROUP, lanes)
        return carry

    lax.fori_loop(0, chans // GROUP, group, 0)


def pointwise(acc, at, count, gain, up_t, down_t):
    normed = []
    for r in range(count):
        a = acc[at + r]
        center = a - jnp.mean(a, axis=0, keepdims=True)
        spread_ = jnp.mean(center * center, axis=0, keepdims=True)
        normed.append((center * lax.rsqrt(spread_ + 1e-06) * gain).astype(BF))
    n = jnp.concatenate(normed, axis=1)
    z = jnp.dot(up_t, n, preferred_element_type=F32)
    h = twice_gelu(z.astype(BF))
    return jnp.dot(down_t, h, preferred_element_type=F32)


def transposed(ref_value, factor):
    return (ref_value.astype(F32).T * factor).astype(BF)


def pack_kernel(x_ref, p_ref):
    p_ref[0] = pack_edges([x_ref[t] for t in range(PACK)])


def pack(x):
    rows, chans, lanes = x.shape
    return pl.pallas_call(
        pack_kernel,
        grid=(rows // PACK,),
        out_shape=jax.ShapeDtypeStruct((rows // PACK, chans, lanes), BF),
        in_specs=[pl.BlockSpec((PACK, chans, lanes), lambda i: (i, 0, 0))],
        out_specs=pl.BlockSpec((1, chans, lanes), lambda i: (i, 0, 0)),
        name="pack_edges",
    )(x)


def layer_kernel(layer, members, *refs):
    x_ref, left_ref, right_ref, k_ref, g_ref, up_ref, dn_ref, s_ref = refs[:8]
    if layer == 0:
        y_ref, p_ref, xj, acc, band, up_t, dn_t = refs[8:]
    else:
        fw_ref, y_ref = refs[8:10]
        flux_refs = refs[10 : 10 + members]
        xj, acc, band, up_t, dn_t, flux = refs[10 + members :]
    rows, chans, lanes = x_ref.shape
    blank = jnp.zeros((HALO, chans, lanes), BF)
    for j in range(TAPS):
        xj[j, 0:HALO] = blank
        xj[j, rows + HALO : rows + 2 * HALO] = blank
    smat = shift_matrix(lanes)

    def prep(q, carry):
        at = q * PACK
        edges = pick_edges(left_ref[q], right_ref[q])
        make_shifts(x_ref[pl.ds(at, PACK)], edges, xj, at + HALO, smat)
        return carry

    lax.fori_loop(0, rows // PACK, prep, 0)
    build_band(lambda i: k_ref[layer, i], band)
    up_t[...] = transposed(up_ref[layer], 1.0)
    dn_t[...] = transposed(dn_ref[layer], 0.5)
    gain = spread(g_ref[layer : layer + 1], lanes)
    scale = spread(s_ref[layer : layer + 1], lanes)
    convolve(xj, band, acc)
    if layer == 1:
        fw_t = transposed(fw_ref[...], 1.0)
        flux[0:HALO] = jnp.zeros((HALO,) + flux.shape[1:], BF)
        flux[rows + HALO : rows + 2 * HALO] = jnp.zeros((HALO,) + flux.shape[1:], BF)

    def mlp(q, carry):
        at = q * PACK
        branch = pointwise(acc, at, PACK, gain, up_t[...], dn_t[...])
        made = []
        for t in range(PACK):
            y = x_ref[at + t].astype(F32) + scale * branch[:, t * lanes : (t + 1) * lanes]
            made.append(y.astype(BF))
            y_ref[at + t] = made[t]
        if layer == 0:
            p_ref[q] = pack_edges(made)
        else:
            z = jnp.dot(fw_t, jnp.concatenate(made, axis=1), preferred_element_type=F32)
            f = (0.5 * twice_gelu(z)).astype(BF)
            for t in range(PACK):
                flux[at + HALO + t] = f[:, t * lanes : (t + 1) * lanes]
        return carry

    lax.fori_loop(0, rows // PACK, mlp, 0)
    if layer == 1:
        share = rows // members
        rank = lax.axis_index("member")
        for s in range(members):
            dst = lax.rem(rank + s, members)
            flux_refs[s][...] = flux[pl.ds(dst * share, share + 2 * HALO)]


def run_layer(layer, members, x, left, right, kernel, gain, up, down, scale, flux_weight=None):
    rows, chans, lanes = x.shape
    hid = up.shape[2]
    out = [jax.ShapeDtypeStruct(x.shape, BF)]
    args = [x, left, right, kernel, gain, up, down, scale]
    scratch = [
        pltpu.VMEM((TAPS, rows + 2 * HALO, chans, lanes), BF),
        pltpu.VMEM((rows, chans, lanes), F32),
        pltpu.VMEM((chans // GROUP, GROUP * OUT, TAPS * DEPTH), BF),
        pltpu.VMEM((hid, chans), BF),
        pltpu.VMEM((chans, hid), BF),
    ]
    if layer == 0:
        out.append(jax.ShapeDtypeStruct(left.shape, BF))
    else:
        args.append(flux_weight)
        flux = flux_weight.shape[1]
        share = rows // members
        out += [jax.ShapeDtypeStruct((share + 2 * HALO, flux, lanes), BF)] * members
        scratch.append(pltpu.VMEM((rows + 2 * HALO, flux, lanes), BF))
    return pl.pallas_call(
        functools.partial(layer_kernel, layer, members),
        out_shape=out,
        in_specs=[VMEM] * len(args),
        out_specs=[VMEM] * len(out),
        scratch_shapes=scratch,
        compiler_params=params(56),
        name="atmos_block",
    )(*args)


def force_kernel(members, *refs):
    flux_refs = refs[:members]
    ocean_ref, land_ref, ice_ref, lift_ref, mid_ref, p_ref, win, sem = refs[members:]
    span, flux, lanes = flux_refs[0].shape
    rows = land_ref.shape[0]
    chans = mid_ref.shape[1]
    share = rows // members
    first = lax.axis_index("member") * share - HALO
    start = jnp.clip(first, 0, rows - span)
    copy = pltpu.make_async_copy(ocean_ref.at[pl.ds(start, span)], win, sem)
    copy.start()
    total = flux_refs[0][...].astype(F32)
    for ref in flux_refs[1:]:
        total = total + ref[...].astype(F32)
    low = (total / members).astype(BF)
    lift = jnp.concatenate([transposed(lift_ref[0], 1.0), transposed(lift_ref[1], 1.0)], axis=0)
    terms = jnp.dot(
        lift, jnp.concatenate([low[r] for r in range(span)], axis=1), preferred_element_type=F32
    )
    copy.wait()
    for r in range(span, mid_ref.shape[0]):
        mid_ref[r] = jnp.zeros((chans, lanes), BF)
    for r in range(span):
        row = first + r
        safe = jnp.clip(row, 0, rows - 1)
        sea = (1 - land_ref[pl.ds(safe, 1), :]).astype(F32)
        ice = ice_ref[pl.ds(safe, 1), :].astype(F32)
        at = slice(r * lanes, (r + 1) * lanes)
        forcing = sea * ((1.0 - ice) * terms[:chans, at] + ice * terms[chans:, at])
        mid = win[jnp.clip(row - start, 0, span - 1)].astype(F32) + forcing
        inside = (row >= 0) & (row < rows)
        mid_ref[r] = jnp.where(inside, mid, 0.0).astype(BF)
    for q in range(mid_ref.shape[0] // PACK):
        p_ref[q] = pack_edges([mid_ref[q * PACK + t] for t in range(PACK)])


def run_force(members, chunks, ocean, land, ice, lift):
    span, _, lanes = chunks[0].shape
    chans = ocean.shape[1]
    tall = max(-(-span // PACK) * PACK, 2 * PACK)
    return pl.pallas_call(
        functools.partial(force_kernel, members),
        out_shape=[
            jax.ShapeDtypeStruct((tall, chans, lanes), BF),
            jax.ShapeDtypeStruct((tall // PACK, chans, lanes), BF),
        ],
        in_specs=[VMEM] * members + [ANY, VMEM, VMEM, VMEM],
        out_specs=[VMEM] * 2,
        scratch_shapes=[pltpu.VMEM((span, chans, lanes), BF), pltpu.SemaphoreType.DMA(())],
        compiler_params=params(40),
        name="ocean_forcing",
    )(*chunks, ocean, land, ice, lift)


def ocean_kernel(members, mid_ref, left_ref, right_ref, land_ref, k_ref, g_ref, up_ref, dn_ref, s_ref, sw_ref, new_ref, surf_ref, xj, acc, band):
    tall, chans, lanes = mid_ref.shape
    share = new_ref.shape[0]
    smat = shift_matrix(lanes)

    def prep(q, carry):
        at = q * PACK
        edges = pick_edges(left_ref[q], right_ref[q])
        make_shifts(mid_ref[pl.ds(at, PACK)], edges, xj, at, smat)
        return carry

    lax.fori_loop(0, tall // PACK, prep, 0)
    build_band(lambda i: k_ref[i], band)
    gain = spread(g_ref[...], lanes)
    scale = spread(s_ref[...], lanes)
    convolve(xj, band, acc)
    branch = pointwise(
        acc, 0, share, gain, transposed(up_ref[...], 1.0), transposed(dn_ref[...], 0.5)
    )
    first = lax.axis_index("member") * share
    made = []
    for r in range(share):
        sea = (1 - land_ref[pl.ds(first + r, 1), :]).astype(F32)
        y = mid_ref[HALO + r].astype(F32) + scale * branch[:, r * lanes : (r + 1) * lanes]
        made.append((y * sea).astype(BF))
        new_ref[r] = made[r]
    surf = jnp.dot(
        transposed(sw_ref[...], 1.0), jnp.concatenate(made, axis=1), preferred_element_type=F32
    )
    for r in range(share):
        surf_ref[r] = surf[:, r * lanes : (r + 1) * lanes].astype(BF)


def run_ocean(members, mid, left, right, land, kernel, gain, up, down, scale, surf_weight):
    tall, chans, lanes = mid.shape
    share = land.shape[0] // members
    return pl.pallas_call(
        functools.partial(ocean_kernel, members),
        out_shape=[
            jax.ShapeDtypeStruct((share, chans, lanes), BF),
            jax.ShapeDtypeStruct((share, surf_weight.shape[1], lanes), BF),
        ],
        in_specs=[VMEM] * 10,
        out_specs=[VMEM] * 2,
        scratch_shapes=[
            pltpu.VMEM((TAPS, tall, chans, lanes), BF),
            pltpu.VMEM((share, chans, lanes), F32),
            pltpu.VMEM((chans // GROUP, GROUP * OUT, TAPS * DEPTH), BF),
        ],
        compiler_params=params(40),
        name="ocean_block",
    )(mid, left, right, land, kernel, gain[None], up, down, scale[None], surf_weight)


def couple_kernel(y_ref, surf_ref, land_ref, bw_ref, o_ref):
    share, chans, lanes = y_ref.shape
    surf = jnp.concatenate([surf_ref[0, r] for r in range(share)], axis=1)
    back = jnp.dot(transposed(bw_ref[...], 1.0), surf, preferred_element_type=F32)
    first = pl.program_id(0) * share
    for r in range(share):
        sea = (1 - land_ref[pl.ds(first + r, 1), :]).astype(F32)
        out = y_ref[r].astype(F32) + sea * back[:, r * lanes : (r + 1) * lanes]
        o_ref[r] = out.astype(BF)


def couple(y, surface, land, back_weight):
    members, share, surf, lanes = surface.shape
    chans = y.shape[1]
    rows = pl.BlockSpec((share, chans, lanes), lambda i: (i, 0, 0))
    return pl.pallas_call(
        couple_kernel,
        grid=(members,),
        out_shape=jax.ShapeDtypeStruct(y.shape, BF),
        in_specs=[
            rows,
            pl.BlockSpec((1, share, surf, lanes), lambda i: (i, 0, 0, 0)),
            VMEM,
            VMEM,
        ],
        out_specs=rows,
        compiler_params=params(32),
        name="couple",
    )(y, surface, land, back_weight)


def neighbours(packed):
    count = lax.axis_size("lon")
    left = lax.ppermute(packed, "lon", [(i, (i + 1) % count) for i in range(count)])
    right = lax.ppermute(packed, "lon", [((i + 1) % count, i) for i in range(count)])
    return left, right


def local(
    atmos,
    ocean,
    land_mask,
    ice_mask,
    atm_kernel,
    atm_gain,
    atm_up,
    atm_down,
    atm_scale,
    flux_weight,
    flux_lift,
    ocn_kernel,
    ocn_gain,
    ocn_up,
    ocn_down,
    ocn_scale,
    surf_weight,
    back_weight,
):
    members = lax.axis_size("member")
    state = atmos[0]
    atm = (atm_kernel, atm_gain, atm_up, atm_down, atm_scale)
    left, right = neighbours(pack(state))
    state, packed = run_layer(0, members, state, left, right, *atm)
    left, right = neighbours(packed)
    state, *chunks = run_layer(1, members, state, left, right, *atm, flux_weight)
    for s in range(1, members):
        chunks[s] = lax.ppermute(
            chunks[s], "member", [(i, (i + s) % members) for i in range(members)]
        )
    mid, packed = run_force(members, chunks, ocean, land_mask, ice_mask, flux_lift)
    left, right = neighbours(packed)
    ocean_rows, surface = run_ocean(
        members, mid, left, right, land_mask, ocn_kernel, ocn_gain, ocn_up, ocn_down, ocn_scale, surf_weight
    )
    surface = lax.all_gather(surface, "member")
    out = couple(state, surface, land_mask, back_weight)
    return (out[None], ocean_rows)


def solution(mesh):
    in_specs = (
        P("member", None, None, "lon"),
        P(None, None, "lon"),
        P(None, "lon"),
        P(None, "lon"),
    ) + (P(),) * 14
    out_specs = (P("member", None, None, "lon"), P("member", None, "lon"))
    return jax.shard_map(local, mesh=mesh, in_specs=in_specs, out_specs=out_specs, check_vma=False)
```

```python
import functools

import jax
import jax.numpy as jnp
from jax import lax
from jax.experimental import pallas as pl
from jax.experimental.pallas import tpu as pltpu
from jax.sharding import PartitionSpec as P

BF = jnp.bfloat16
F32 = jnp.float32
TANH_A = 0.7978845608028654
TANH_B = TANH_A * 0.044715
TAPS = 7
HALO = 3
GROUP = 16
SPAN = 16
OUT = SPAN - TAPS + 1
DEPTH = GROUP * SPAN
SLOT = 8
SLOTS = 16
BY_DOT = (0, 1, 5, 6)
VMEM = pl.BlockSpec(memory_space=pltpu.VMEM)
ANY = pl.BlockSpec(memory_space=pl.ANY)


def params(mib):
    return pltpu.CompilerParams(vmem_limit_bytes=mib * 2**20)


def cost(gflop):
    return pl.CostEstimate(flops=int(gflop * 1e9), bytes_accessed=0, transcendentals=0)


def twice_gelu(z):
    return z + z * jnp.tanh(z * (TANH_A + TANH_B * (z * z)))


def transposed(value, factor):
    return (value.astype(F32).T * factor).astype(BF)


def spread(row, lanes):
    return jnp.broadcast_to(row.T, (row.shape[1], lanes))


def edge_lanes(shape):
    lane = lax.broadcasted_iota(jnp.int32, shape, len(shape) - 1)
    return (lane < HALO) | (lane >= shape[-1] - HALO)


def pack_kernel(x_ref, p_ref):
    step = pl.program_id(0)
    count, chans, lanes = x_ref.shape
    blocks = p_ref.shape[0]
    keep = edge_lanes((chans, lanes)).astype(F32).astype(BF)
    for q in range(blocks):
        total = None
        for c in range(count // blocks):
            slot = step * (count // blocks) + c
            moved = pltpu.roll(x_ref[c * blocks + q] * keep, SLOT * slot, 1)
            total = moved if total is None else total + moved
        if count // blocks < SLOTS:

            @pl.when(step == 0)
            def _():
                p_ref[q] = total

            @pl.when(step > 0)
            def _():
                p_ref[q] = p_ref[q] + total

        else:
            p_ref[q] = total


def pack(x, step):
    rows, chans, lanes = x.shape
    blocks = rows // SLOTS
    return pl.pallas_call(
        pack_kernel,
        grid=(rows // step,),
        out_shape=jax.ShapeDtypeStruct((blocks, chans, lanes), BF),
        in_specs=[pl.BlockSpec((step, chans, lanes), lambda i: (i, 0, 0))],
        out_specs=pl.BlockSpec((blocks, chans, lanes), lambda i: (0, 0, 0)),
        compiler_params=params(16),
        name="pack_edges",
    )(x)


def neighbours(packed):
    count = lax.axis_size("lon")
    left = lax.ppermute(packed, "lon", [(i, (i + 1) % count) for i in range(count)])
    right = lax.ppermute(packed, "lon", [((i + 1) % count, i) for i in range(count)])
    return left, right


def shift_matrix(lanes):
    shape = (lanes, len(BY_DOT) * lanes)
    src = lax.broadcasted_iota(jnp.int32, shape, 0)
    dst = lax.broadcasted_iota(jnp.int32, shape, 1)
    hit = jnp.zeros(shape, jnp.bool_)
    for a, j in enumerate(BY_DOT):
        hit = hit | ((dst >= a * lanes) & (dst < (a + 1) * lanes) & (src == dst - a * lanes + j - HALO))
    return hit.astype(F32).astype(BF)


def fill_base(taps, base):
    groups, _, wide = base.shape
    chans = groups * GROUP
    t = lax.broadcasted_iota(jnp.int32, (TAPS, wide), 0)
    n = lax.broadcasted_iota(jnp.int32, (TAPS, wide), 1)
    total = jnp.zeros((chans, wide), F32)
    for i in range(TAPS):
        put = ((t == n // DEPTH) & ((n % DEPTH) // GROUP == i)).astype(F32).astype(BF)
        total = total + jnp.dot(taps(i).T.astype(BF), put, preferred_element_type=F32)
    r = lax.broadcasted_iota(jnp.int32, (chans, wide), 0)
    c = lax.broadcasted_iota(jnp.int32, (chans, wide), 1)
    total = jnp.where(r % GROUP == c % GROUP, total, 0.0)
    for g in range(groups):
        base[g] = total[GROUP * g : GROUP * (g + 1)]


def conv_kernel(layer, pad, x_ref, k_ref, a_ref, band_ref, base, smat, xj, band):
    g = pl.program_id(0)
    count, _, lanes = x_ref.shape
    rows = a_ref.shape[0]
    tall = xj.shape[1]

    @pl.when(g == 0)
    def _():
        fill_base(lambda i: k_ref[layer, i] if layer is not None else k_ref[i], base)
        smat[...] = shift_matrix(lanes)
        for j in range(TAPS):
            if pad:
                xj[j, :pad] = jnp.zeros((pad, GROUP, lanes), BF)
            if tall > pad + count:
                xj[j, pad + count :] = jnp.zeros((tall - pad - count, GROUP, lanes), BF)

    for j in range(TAPS):
        one = base[g, :, j * DEPTH : (j + 1) * DEPTH]
        for r in range(OUT):
            moved = pltpu.roll(one, GROUP * r, 1) if r else one
            band[GROUP * r : GROUP * (r + 1), j * DEPTH : (j + 1) * DEPTH] = moved.astype(BF)
    band_ref[0] = band[: band_ref.shape[1]]

    x = x_ref[...]
    moved = jnp.dot(x.reshape(count * GROUP, lanes), smat[...], preferred_element_type=F32)
    for a, j in enumerate(BY_DOT):
        part = moved[:, a * lanes : (a + 1) * lanes].astype(BF)
        xj[j, pad : pad + count] = part.reshape(count, GROUP, lanes)
    lane = lax.broadcasted_iota(jnp.int32, (GROUP, lanes), 1)
    for j in range(TAPS):
        d = j - HALO
        if j in BY_DOT:
            continue
        if d == 0:
            xj[j, pad : pad + count] = x
        else:
            keep = ((lane < lanes - d) if d > 0 else (lane >= -d)).astype(F32).astype(BF)
            xj[j, pad : pad + count] = pltpu.roll(x, (-d) % lanes, 2) * keep[None]

    starts = [min(OUT * i, max(rows - OUT, 0)) for i in range(-(-rows // OUT))]
    field = jnp.concatenate(
        [
            jnp.concatenate([xj[j, s : s + SPAN].reshape(DEPTH, lanes) for j in range(TAPS)], axis=0)
            for s in starts
        ],
        axis=1,
    )
    out = jnp.dot(band[...], field, preferred_element_type=F32)
    take = min(OUT, rows)
    for n, s in enumerate(starts):
        part = out[: take * GROUP, n * lanes : (n + 1) * lanes]
        a_ref[s : s + take] = part.reshape(take, GROUP, lanes)


def convolve(layer, x, taps, pad, blocks):
    count, chans, lanes = x.shape
    rows = count + 2 * pad - 2 * HALO
    groups = chans // GROUP
    wide = TAPS * DEPTH
    tall = max(count + 2 * pad, SPAN)
    return pl.pallas_call(
        functools.partial(conv_kernel, layer, pad),
        grid=(groups,),
        out_shape=[
            jax.ShapeDtypeStruct((rows, chans, lanes), F32),
            jax.ShapeDtypeStruct((groups, blocks * GROUP, wide), BF),
        ],
        in_specs=[pl.BlockSpec((count, GROUP, lanes), lambda g: (0, g, 0)), VMEM],
        out_specs=[
            pl.BlockSpec((rows, GROUP, lanes), lambda g: (0, g, 0)),
            pl.BlockSpec((1, blocks * GROUP, wide), lambda g: (g, 0, 0)),
        ],
        scratch_shapes=[
            pltpu.VMEM((groups, GROUP, wide), F32),
            pltpu.VMEM((lanes, len(BY_DOT) * lanes), BF),
            pltpu.VMEM((TAPS, tall, GROUP, lanes), BF),
            pltpu.VMEM((GROUP * OUT, wide), BF),
        ],
        compiler_params=params(32),
        cost_estimate=cost(8 * rows / 96),
        name="conv",
    )(x, taps)


def halo_matrix(lanes):
    side = [j for j in range(TAPS) if j != HALO]
    shape = (2 * lanes, len(side) * lanes)
    src = lax.broadcasted_iota(jnp.int32, shape, 0)
    dst = lax.broadcasted_iota(jnp.int32, shape, 1)
    hit = jnp.zeros(shape, jnp.bool_)
    to = dst % lanes
    for a, j in enumerate(side):
        d = j - HALO
        here = (dst >= a * lanes) & (dst < (a + 1) * lanes)
        from_ = (to + d + lanes) % lanes
        if d > 0:
            ok = (src == from_) & (src % SLOT < HALO) & (to % SLOT >= SLOT - HALO)
        else:
            ok = (src == from_ + lanes) & (src % SLOT >= SLOT - HALO) & (to % SLOT < HALO)
        hit = hit | (here & ok)
    return hit.astype(F32).astype(BF)


def halo_conv(left, right, band, wrapped, xe, halo):
    blocks, chans, lanes = halo.shape
    wide = TAPS * DEPTH
    both = [jnp.concatenate([right[q], left[q]], axis=1) for q in range(blocks)]
    lane = lax.broadcasted_iota(jnp.int32, (chans, lanes), 1)
    slot = (lane + HALO) // SLOT % SLOTS

    def turned(value, shift, drop):
        keep = (slot != drop).astype(F32).astype(BF)
        parts = [pltpu.roll(value[:, n * lanes : (n + 1) * lanes], shift, 1) * keep for n in range(2)]
        return jnp.concatenate(parts, axis=1)

    if wrapped:
        tall = (
            [turned(both[q], SLOT, 0) for q in range(blocks - HALO, blocks)]
            + both
            + [turned(both[q], lanes - SLOT, SLOTS - 1) for q in range(HALO)]
        )
    else:
        tall = both + [turned(both[q], lanes - SLOT, SLOTS - 1) for q in range(2 * HALO)]
    field = jnp.concatenate(tall, axis=0)
    moved = jnp.dot(field, halo_matrix(lanes), preferred_element_type=F32)
    count = len(tall)
    for a in range(TAPS - 1):
        part = moved[:, a * lanes : (a + 1) * lanes].astype(BF)
        xe[a, :count] = part.reshape(count, chans, lanes)
        xe[a, count:] = jnp.zeros((SPAN - count, chans, lanes), BF)
    low = HALO * DEPTH
    for g in range(chans // GROUP):
        at = slice(GROUP * g, GROUP * (g + 1))
        rhs = jnp.concatenate([xe[a, :, at, :].reshape(DEPTH, lanes) for a in range(TAPS - 1)], axis=0)
        lhs = jnp.concatenate([band[g, :, :low], band[g, :, low + DEPTH : wide]], axis=1)
        out = jnp.dot(lhs, rhs, preferred_element_type=F32)
        halo[:, at, :] = out.reshape(blocks, GROUP, lanes)


def branch_of(a_ref, halo, slot0, gain, up_t, down_t):
    count, chans, lanes = a_ref.shape
    blocks = halo.shape[0]
    edge = edge_lanes((chans, lanes))
    normed = []
    for r in range(count):
        shift = lax.rem(lanes - SLOT * (slot0 + r // blocks), lanes)
        a = a_ref[r] + jnp.where(edge, pltpu.roll(halo[r % blocks], shift, 1), 0.0)
        center = a - jnp.mean(a, axis=0, keepdims=True)
        var = jnp.mean(center * center, axis=0, keepdims=True)
        normed.append((center * lax.rsqrt(var + 1e-06) * gain).astype(BF))
    z = jnp.dot(up_t, jnp.concatenate(normed, axis=1), preferred_element_type=F32)
    h = twice_gelu(z.astype(BF))
    return jnp.dot(down_t, h, preferred_element_type=F32)


def first_kernel(x_ref, a_ref, left_ref, right_ref, band_ref, g_ref, up_ref, dn_ref, s_ref, y_ref, p_ref, xe, halo, up_t, dn_t, gain, scale):
    step = pl.program_id(0)
    count, chans, lanes = x_ref.shape
    blocks = halo.shape[0]

    @pl.when(step == 0)
    def _():
        halo_conv(left_ref, right_ref, band_ref, True, xe, halo)
        up_t[...] = transposed(up_ref[0], 1.0)
        dn_t[...] = transposed(dn_ref[0], 0.5)
        gain[...] = spread(g_ref[0:1], lanes)
        scale[...] = spread(s_ref[0:1], lanes)
        p_ref[...] = jnp.zeros(p_ref.shape, BF)

    slot0 = step * (count // blocks)
    branch = branch_of(a_ref, halo, slot0, gain[...], up_t[...], dn_t[...])
    keep = edge_lanes((chans, lanes)).astype(F32).astype(BF)
    for r in range(count):
        y = x_ref[r].astype(F32) + scale[...] * branch[:, r * lanes : (r + 1) * lanes]
        y = y.astype(BF)
        y_ref[r] = y
        moved = pltpu.roll(y * keep, SLOT * (slot0 + r // blocks), 1)
        p_ref[r % blocks] = p_ref[r % blocks] + moved


def first_block(x, a, left, right, band, gain, up, down, scale, step):
    rows, chans, lanes = x.shape
    blocks = rows // SLOTS
    hid = up.shape[2]
    part = pl.BlockSpec((step, chans, lanes), lambda i: (i, 0, 0))
    return pl.pallas_call(
        first_kernel,
        grid=(rows // step,),
        out_shape=[
            jax.ShapeDtypeStruct(x.shape, BF),
            jax.ShapeDtypeStruct((blocks, chans, lanes), BF),
        ],
        in_specs=[part, part] + [VMEM] * 7,
        out_specs=[part, pl.BlockSpec((blocks, chans, lanes), lambda i: (0, 0, 0))],
        scratch_shapes=[
            pltpu.VMEM((TAPS - 1, SPAN, chans, lanes), BF),
            pltpu.VMEM((blocks, chans, lanes), F32),
            pltpu.VMEM((hid, chans), BF),
            pltpu.VMEM((chans, hid), BF),
            pltpu.VMEM((chans, lanes), F32),
            pltpu.VMEM((chans, lanes), F32),
        ],
        compiler_params=params(40),
        cost_estimate=cost(8),
        name="first_block",
    )(x, a, left, right, band, gain, up, down, scale)


def second_kernel(near, members, at_ref, *refs):
    x_ref, a_ref, left_ref, right_ref, band_ref, g_ref, up_ref, dn_ref, s_ref, fw_ref = refs[:10]
    refs = refs[10:]
    if near:
        old_ref = refs[1]
        refs = refs[2:]
    y_ref, refs = refs[0], refs[1:]
    half = members // 2
    chunk_refs, refs = refs[:half], refs[half:]
    flux, xe, halo, up_t, dn_t, fw_t, gain, scale = refs
    step = pl.program_id(0)
    count, chans, lanes = x_ref.shape
    blocks = halo.shape[0]
    tall = flux.shape[0]

    @pl.when(step == 0)
    def _():
        halo_conv(left_ref, right_ref, band_ref, True, xe, halo)
        up_t[...] = transposed(up_ref[1], 1.0)
        dn_t[...] = transposed(dn_ref[1], 0.5)
        fw_t[...] = transposed(fw_ref[...], 1.0)
        gain[...] = spread(g_ref[1:2], lanes)
        scale[...] = spread(s_ref[1:2], lanes)
        if near:
            flux[...] = old_ref[...]
        else:
            flux[0:HALO] = jnp.zeros((HALO,) + flux.shape[1:], BF)
            flux[tall - HALO : tall] = jnp.zeros((HALO,) + flux.shape[1:], BF)

    row0 = (at_ref[0] + step) * count
    slot0 = (at_ref[0] + step) * (count // blocks)
    branch = branch_of(a_ref, halo, slot0, gain[...], up_t[...], dn_t[...])
    made = []
    for r in range(count):
        y = x_ref[r].astype(F32) + scale[...] * branch[:, r * lanes : (r + 1) * lanes]
        made.append(y.astype(BF))
        y_ref[r] = made[r]
    z = jnp.dot(fw_t[...], jnp.concatenate(made, axis=1), preferred_element_type=F32)
    f = (0.5 * twice_gelu(z)).astype(BF)
    for r in range(count):
        flux[row0 + HALO + r] = f[:, r * lanes : (r + 1) * lanes]

    @pl.when(step == pl.num_programs(0) - 1)
    def _():
        rank = lax.axis_index("member")
        share = (tall - 2 * HALO) // members
        for k in range(half):
            dst = rank ^ (k if near else half + k)
            chunk_refs[k][...] = flux[pl.ds(dst * share, share + 2 * HALO)]


def second_block(near, members, at, x, a, left, right, band, gain, up, down, scale, flux_weight, earlier, step, steps):
    rows, chans, lanes = x.shape
    blocks = rows // SLOTS
    hid = up.shape[2]
    flux = flux_weight.shape[1]
    half = members // 2
    share = rows // members
    part = pl.BlockSpec((step, chans, lanes), lambda i, s: (s[0] + i, 0, 0))
    args = [at, x, a, left, right, band, gain, up, down, scale, flux_weight]
    in_specs = [part, part] + [VMEM] * 8
    alias = {}
    if near:
        alias = {len(args): 0}
        args += earlier
        in_specs += [ANY, VMEM]
    outs = [jax.ShapeDtypeStruct(x.shape, BF)]
    outs += [jax.ShapeDtypeStruct((share + 2 * HALO, flux, lanes), BF)] * half
    out_specs = [part] + [VMEM] * half
    scratch = [
        pltpu.VMEM((TAPS - 1, SPAN, chans, lanes), BF),
        pltpu.VMEM((blocks, chans, lanes), F32),
        pltpu.VMEM((hid, chans), BF),
        pltpu.VMEM((chans, hid), BF),
        pltpu.VMEM((flux, chans), BF),
        pltpu.VMEM((chans, lanes), F32),
        pltpu.VMEM((chans, lanes), F32),
    ]
    field = (rows + 2 * HALO, flux, lanes)
    if near:
        scratch = [pltpu.VMEM(field, BF)] + scratch
    else:
        outs.append(jax.ShapeDtypeStruct(field, BF))
        out_specs.append(VMEM)
    return pl.pallas_call(
        functools.partial(second_kernel, near, members),
        out_shape=outs,
        grid_spec=pltpu.PrefetchScalarGridSpec(
            num_scalar_prefetch=1,
            grid=(steps,),
            in_specs=in_specs,
            out_specs=out_specs,
            scratch_shapes=scratch,
        ),
        input_output_aliases=alias,
        compiler_params=params(40),
        cost_estimate=cost(8 * steps * step / rows),
        name="second_block",
    )(*args)


def force_kernel(members, *refs):
    flux_refs = refs[:members]
    ocean_ref, land_ref, ice_ref, lift_ref, mid_ref, p_ref, win, sem = refs[members:]
    span, flux, lanes = flux_refs[0].shape
    rows = land_ref.shape[0]
    chans = mid_ref.shape[1]
    share = rows // members
    blocks = p_ref.shape[0]
    first = lax.axis_index("member") * share - HALO
    start = jnp.clip(first, 0, rows - span)
    copy = pltpu.make_async_copy(ocean_ref.at[pl.ds(start, span)], win, sem)
    copy.start()
    total = flux_refs[0][...].astype(F32)
    for ref in flux_refs[1:]:
        total = total + ref[...].astype(F32)
    low = (total / members).astype(BF)
    lift = jnp.concatenate([transposed(lift_ref[0], 1.0), transposed(lift_ref[1], 1.0)], axis=0)
    terms = jnp.dot(
        lift, jnp.concatenate([low[r] for r in range(span)], axis=1), preferred_element_type=F32
    )
    keep = edge_lanes((chans, lanes)).astype(F32).astype(BF)
    packed = [None] * blocks
    copy.wait()
    for r in range(span):
        row = first + r
        safe = jnp.clip(row, 0, rows - 1)
        sea = (1 - land_ref[pl.ds(safe, 1), :]).astype(F32)
        ice = ice_ref[pl.ds(safe, 1), :].astype(F32)
        at = slice(r * lanes, (r + 1) * lanes)
        forcing = sea * ((1.0 - ice) * terms[:chans, at] + ice * terms[chans:, at])
        mid = win[jnp.clip(row - start, 0, span - 1)].astype(F32) + forcing
        inside = (row >= 0) & (row < rows)
        mid = jnp.where(inside, mid, 0.0).astype(BF)
        mid_ref[r] = mid
        q, slot = r % blocks, r // blocks
        moved = mid * keep
        if slot:
            moved = pltpu.roll(moved, SLOT * slot, 1)
        packed[q] = moved if packed[q] is None else packed[q] + moved
    for q in range(blocks):
        p_ref[q] = packed[q]


def force(members, chunks, ocean, land, ice, lift):
    span, _, lanes = chunks[0].shape
    rows, chans, _ = ocean.shape
    return pl.pallas_call(
        functools.partial(force_kernel, members),
        out_shape=[
            jax.ShapeDtypeStruct((span, chans, lanes), BF),
            jax.ShapeDtypeStruct((rows // SLOTS, chans, lanes), BF),
        ],
        in_specs=[VMEM] * members + [ANY, VMEM, VMEM, VMEM],
        out_specs=[VMEM] * 2,
        scratch_shapes=[pltpu.VMEM((span, chans, lanes), BF), pltpu.SemaphoreType.DMA(())],
        compiler_params=params(24),
        name="ocean_forcing",
    )(*chunks, ocean, land, ice, lift)


def ocean_kernel(mid_ref, a_ref, left_ref, right_ref, band_ref, land_ref, g_ref, up_ref, dn_ref, s_ref, sw_ref, new_ref, surf_ref, xe, halo):
    share, chans, lanes = new_ref.shape
    halo_conv(left_ref, right_ref, band_ref, False, xe, halo)
    gain = spread(g_ref[...], lanes)
    scale = spread(s_ref[...], lanes)
    branch = branch_of(
        a_ref, halo, 0, gain, transposed(up_ref[...], 1.0), transposed(dn_ref[...], 0.5)
    )
    first = lax.axis_index("member") * share
    made = []
    for r in range(share):
        sea = (1 - land_ref[pl.ds(first + r, 1), :]).astype(F32)
        y = mid_ref[HALO + r].astype(F32) + scale * branch[:, r * lanes : (r + 1) * lanes]
        made.append((y * sea).astype(BF))
        new_ref[r] = made[r]
    surf = jnp.dot(
        transposed(sw_ref[...], 1.0), jnp.concatenate(made, axis=1), preferred_element_type=F32
    )
    for r in range(share):
        surf_ref[r] = surf[:, r * lanes : (r + 1) * lanes].astype(BF)


def ocean_block(mid, a, left, right, band, land, gain, up, down, scale, surf_weight):
    share, chans, lanes = a.shape
    blocks = left.shape[0]
    return pl.pallas_call(
        ocean_kernel,
        out_shape=[
            jax.ShapeDtypeStruct((share, chans, lanes), BF),
            jax.ShapeDtypeStruct((share, surf_weight.shape[1], lanes), BF),
        ],
        in_specs=[VMEM] * 11,
        out_specs=[VMEM] * 2,
        scratch_shapes=[
            pltpu.VMEM((TAPS - 1, SPAN, chans, lanes), BF),
            pltpu.VMEM((blocks, chans, lanes), F32),
        ],
        compiler_params=params(24),
        name="ocean_block",
    )(mid, a, left, right, band, land, gain[None], up, down, scale[None], surf_weight)


def couple_kernel(y_ref, surf_ref, land_ref, bw_ref, o_ref):
    share, chans, lanes = y_ref.shape
    surf = jnp.concatenate([surf_ref[0, r] for r in range(share)], axis=1)
    back = jnp.dot(transposed(bw_ref[...], 1.0), surf, preferred_element_type=F32)
    first = pl.program_id(0) * share
    for r in range(share):
        sea = (1 - land_ref[pl.ds(first + r, 1), :]).astype(F32)
        out = y_ref[r].astype(F32) + sea * back[:, r * lanes : (r + 1) * lanes]
        o_ref[r] = out.astype(BF)


def couple(y, surface, land, back_weight):
    members, share, surf, lanes = surface.shape
    chans = y.shape[1]
    rows = pl.BlockSpec((share, chans, lanes), lambda i: (i, 0, 0))
    return pl.pallas_call(
        couple_kernel,
        grid=(members,),
        out_shape=jax.ShapeDtypeStruct(y.shape, BF),
        in_specs=[
            rows,
            pl.BlockSpec((1, share, surf, lanes), lambda i: (i, 0, 0, 0)),
            VMEM,
            VMEM,
        ],
        out_specs=rows,
        compiler_params=params(24),
        name="couple",
    )(y, surface, land, back_weight)


def local(
    atmos,
    ocean,
    land_mask,
    ice_mask,
    atm_kernel,
    atm_gain,
    atm_up,
    atm_down,
    atm_scale,
    flux_weight,
    flux_lift,
    ocn_kernel,
    ocn_gain,
    ocn_up,
    ocn_down,
    ocn_scale,
    surf_weight,
    back_weight,
):
    members = lax.axis_size("member")
    rank = lax.axis_index("member")
    half = members // 2
    state = atmos[0]
    rows = state.shape[0]
    blocks = rows // SLOTS
    big, small = 4 * blocks, 2 * blocks
    atm = (atm_gain, atm_up, atm_down, atm_scale)

    left, right = neighbours(pack(state, big))
    a, band = convolve(0, state, atm_kernel, HALO, blocks)
    state, packed = first_block(state, a, left, right, band, *atm, big)

    left, right = neighbours(packed)
    a, band = convolve(1, state, atm_kernel, HALO, blocks)
    near_steps = (rows // 2 - small) // small
    far_steps = rows // small - near_steps
    upper = rank >= half
    far_at = jnp.where(upper, 0, near_steps).astype(jnp.int32)[None]
    near_at = jnp.where(upper, far_steps, 0).astype(jnp.int32)[None]
    shared = (state, a, left, right, band, *atm, flux_weight)
    partly, *chunks, flux = second_block(False, members, far_at, *shared, [], small, far_steps)
    sent = [
        lax.ppermute(chunk, "member", [(i, i ^ (half + k)) for i in range(members)])
        for k, chunk in enumerate(chunks)
    ]
    state, *chunks = second_block(True, members, near_at, *shared, [partly, flux], small, near_steps)
    sent += [
        lax.ppermute(chunks[k], "member", [(i, i ^ k) for i in range(members)])
        for k in range(half - 1, 0, -1)
    ]
    sent.append(chunks[0])

    mid, packed = force(members, sent, ocean, land_mask, ice_mask, flux_lift)
    left, right = neighbours(packed)
    a, band = convolve(None, mid, ocn_kernel, 0, blocks)
    ocean_rows, surface = ocean_block(
        mid, a, left, right, band, land_mask, ocn_gain, ocn_up, ocn_down, ocn_scale, surf_weight
    )
    surface = lax.all_gather(surface, "member")
    out = couple(state, surface, land_mask, back_weight)
    return (out[None], ocean_rows)


def solution(mesh):
    in_specs = (
        P("member", None, None, "lon"),
        P(None, None, "lon"),
        P(None, "lon"),
        P(None, "lon"),
    ) + (P(),) * 14
    out_specs = (P("member", None, None, "lon"), P("member", None, "lon"))
    return jax.shard_map(local, mesh=mesh, in_specs=in_specs, out_specs=out_specs, check_vma=False)
```

```python
import functools

import jax
import jax.numpy as jnp
from jax import lax
from jax.experimental import pallas as pl
from jax.experimental.pallas import tpu as pltpu
from jax.sharding import PartitionSpec as P

BF = jnp.bfloat16
F32 = jnp.float32
TANH_A = 0.7978845608028654
TANH_B = TANH_A * 0.044715
TAPS = 7
HALO = 3
GROUP = 16
SPAN = 16
OUT = SPAN - TAPS + 1
DEPTH = GROUP * SPAN
SLOT = 8
SLOTS = 16
OCEAN_BLOCKS = 2
BY_DOT = (0, 1, 5, 6)
VMEM = pl.BlockSpec(memory_space=pltpu.VMEM)
ANY = pl.BlockSpec(memory_space=pl.ANY)


def params(mib):
    return pltpu.CompilerParams(vmem_limit_bytes=mib * 2**20)


def cost(gflop):
    return pl.CostEstimate(flops=int(gflop * 1e9), bytes_accessed=0, transcendentals=0)


def twice_gelu(z):
    return z + z * jnp.tanh(z * (TANH_A + TANH_B * (z * z)))


def transposed(value):
    return value.astype(F32).T.astype(BF)


def halved(value):
    return (0.5 * value.astype(F32)).astype(BF)


def spread(row, lanes):
    return jnp.broadcast_to(row.T, (row.shape[1], lanes))


def edge_lanes(shape):
    lane = lax.broadcasted_iota(jnp.int32, shape, len(shape) - 1)
    return (lane < HALO) | (lane >= shape[-1] - HALO)


def pack_kernel(x_ref, p_ref):
    step = pl.program_id(0)
    count, chans, lanes = x_ref.shape
    blocks = p_ref.shape[0]
    keep = edge_lanes((chans, lanes)).astype(F32).astype(BF)
    for q in range(blocks):
        total = None
        for c in range(count // blocks):
            slot = step * (count // blocks) + c
            moved = pltpu.roll(x_ref[c * blocks + q] * keep, SLOT * slot, 1)
            total = moved if total is None else total + moved
        if count // blocks < SLOTS:

            @pl.when(step == 0)
            def _():
                p_ref[q] = total

            @pl.when(step > 0)
            def _():
                p_ref[q] = p_ref[q] + total

        else:
            p_ref[q] = total


def pack(x, step):
    rows, chans, lanes = x.shape
    blocks = rows // SLOTS
    return pl.pallas_call(
        pack_kernel,
        grid=(rows // step,),
        out_shape=jax.ShapeDtypeStruct((blocks, chans, lanes), BF),
        in_specs=[pl.BlockSpec((step, chans, lanes), lambda i: (i, 0, 0))],
        out_specs=pl.BlockSpec((blocks, chans, lanes), lambda i: (0, 0, 0)),
        compiler_params=params(24),
        name="pack_edges",
    )(x)


def neighbours(packed):
    count = lax.axis_size("lon")
    left = lax.ppermute(packed, "lon", [(i, (i + 1) % count) for i in range(count)])
    right = lax.ppermute(packed, "lon", [((i + 1) % count, i) for i in range(count)])
    return left, right


def shift_matrix(lanes):
    shape = (lanes, len(BY_DOT) * lanes)
    src = lax.broadcasted_iota(jnp.int32, shape, 0)
    dst = lax.broadcasted_iota(jnp.int32, shape, 1)
    hit = jnp.zeros(shape, jnp.bool_)
    for a, j in enumerate(BY_DOT):
        hit = hit | ((dst >= a * lanes) & (dst < (a + 1) * lanes) & (src == dst - a * lanes + j - HALO))
    return hit.astype(F32).astype(BF)


def fill_base(taps, base):
    groups, _, wide = base.shape
    chans = groups * GROUP
    t = lax.broadcasted_iota(jnp.int32, (TAPS, wide), 0)
    n = lax.broadcasted_iota(jnp.int32, (TAPS, wide), 1)
    total = jnp.zeros((chans, wide), F32)
    for i in range(TAPS):
        put = ((t == n // DEPTH) & ((n % DEPTH) // GROUP == i)).astype(F32).astype(BF)
        total = total + jnp.dot(taps(i).T.astype(BF), put, preferred_element_type=F32)
    r = lax.broadcasted_iota(jnp.int32, (chans, wide), 0)
    c = lax.broadcasted_iota(jnp.int32, (chans, wide), 1)
    total = jnp.where(r % GROUP == c % GROUP, total, 0.0)
    for g in range(groups):
        base[g] = total[GROUP * g : GROUP * (g + 1)]


def conv_kernel(layer, pad, x_ref, k_ref, a_ref, band_ref, base, smat, xj, band):
    g = pl.program_id(0)
    count, _, lanes = x_ref.shape
    rows = a_ref.shape[0]
    tall = xj.shape[1]

    @pl.when(g == 0)
    def _():
        fill_base(lambda i: k_ref[i, :, layer, :] if layer is not None else k_ref[i], base)
        smat[...] = shift_matrix(lanes)
        for j in range(TAPS):
            if pad:
                xj[j, :pad] = jnp.zeros((pad, GROUP, lanes), BF)
            if tall > pad + count:
                xj[j, pad + count :] = jnp.zeros((tall - pad - count, GROUP, lanes), BF)

    for j in range(TAPS):
        one = base[g, :, j * DEPTH : (j + 1) * DEPTH]
        for r in range(OUT):
            moved = pltpu.roll(one, GROUP * r, 1) if r else one
            band[GROUP * r : GROUP * (r + 1), j * DEPTH : (j + 1) * DEPTH] = moved.astype(BF)
    band_ref[0] = band[: band_ref.shape[1]]

    x = x_ref[...]
    moved = jnp.dot(x.reshape(count * GROUP, lanes), smat[...], preferred_element_type=F32)
    for a, j in enumerate(BY_DOT):
        part = moved[:, a * lanes : (a + 1) * lanes].astype(BF)
        xj[j, pad : pad + count] = part.reshape(count, GROUP, lanes)
    lane = lax.broadcasted_iota(jnp.int32, (GROUP, lanes), 1)
    for j in range(TAPS):
        d = j - HALO
        if j in BY_DOT:
            continue
        if d == 0:
            xj[j, pad : pad + count] = x
        else:
            keep = ((lane < lanes - d) if d > 0 else (lane >= -d)).astype(F32).astype(BF)
            xj[j, pad : pad + count] = pltpu.roll(x, (-d) % lanes, 2) * keep[None]

    starts = [min(OUT * i, max(rows - OUT, 0)) for i in range(-(-rows // OUT))]
    field = jnp.concatenate(
        [
            jnp.concatenate([xj[j, s : s + SPAN].reshape(DEPTH, lanes) for j in range(TAPS)], axis=0)
            for s in starts
        ],
        axis=1,
    )
    out = jnp.dot(band[...], field, preferred_element_type=F32)
    take = min(OUT, rows)
    for n, s in enumerate(starts):
        part = out[: take * GROUP, n * lanes : (n + 1) * lanes]
        a_ref[s : s + take] = part.reshape(take, GROUP, lanes)


def convolve(layer, x, taps, pad, blocks):
    count, chans, lanes = x.shape
    rows = count + 2 * pad - 2 * HALO
    groups = chans // GROUP
    wide = TAPS * DEPTH
    tall = max(count + 2 * pad, SPAN)
    return pl.pallas_call(
        functools.partial(conv_kernel, layer, pad),
        grid=(groups,),
        out_shape=[
            jax.ShapeDtypeStruct((rows, chans, lanes), F32),
            jax.ShapeDtypeStruct((groups, blocks * GROUP, wide), BF),
        ],
        in_specs=[pl.BlockSpec((count, GROUP, lanes), lambda g: (0, g, 0)), VMEM],
        out_specs=[
            pl.BlockSpec((rows, GROUP, lanes), lambda g: (0, g, 0)),
            pl.BlockSpec((1, blocks * GROUP, wide), lambda g: (g, 0, 0)),
        ],
        scratch_shapes=[
            pltpu.VMEM((groups, GROUP, wide), F32),
            pltpu.VMEM((lanes, len(BY_DOT) * lanes), BF),
            pltpu.VMEM((TAPS, tall, GROUP, lanes), BF),
            pltpu.VMEM((GROUP * OUT, wide), BF),
        ],
        compiler_params=params(24),
        cost_estimate=cost(8 * rows / 96),
        name="conv",
    )(x, taps)


def halo_matrix(lanes):
    side = [j for j in range(TAPS) if j != HALO]
    shape = (2 * lanes, len(side) * lanes)
    src = lax.broadcasted_iota(jnp.int32, shape, 0)
    dst = lax.broadcasted_iota(jnp.int32, shape, 1)
    hit = jnp.zeros(shape, jnp.bool_)
    to = dst % lanes
    for a, j in enumerate(side):
        d = j - HALO
        here = (dst >= a * lanes) & (dst < (a + 1) * lanes)
        from_ = (to + d + lanes) % lanes
        if d > 0:
            ok = (src == from_) & (src % SLOT < HALO) & (to % SLOT >= SLOT - HALO)
        else:
            ok = (src == from_ + lanes) & (src % SLOT >= SLOT - HALO) & (to % SLOT < HALO)
        hit = hit | (here & ok)
    return hit.astype(F32).astype(BF)


def halo_conv(left, right, band, wrapped, xe, halo):
    blocks, chans, lanes = halo.shape
    wide = TAPS * DEPTH
    both = [jnp.concatenate([right[q], left[q]], axis=1) for q in range(blocks)]
    lane = lax.broadcasted_iota(jnp.int32, (chans, lanes), 1)
    slot = (lane + HALO) // SLOT % SLOTS

    def turned(value, shift, drop):
        parts = [pltpu.roll(value[:, n * lanes : (n + 1) * lanes], shift, 1) for n in range(2)]
        if drop >= 0:
            keep = (slot != drop).astype(F32).astype(BF)
            parts = [part * keep for part in parts]
        return jnp.concatenate(parts, axis=1)

    if wrapped:
        tall = (
            [turned(both[q], SLOT, 0) for q in range(blocks - HALO, blocks)]
            + both
            + [turned(both[q], lanes - SLOT, SLOTS - 1) for q in range(HALO)]
        )
    else:
        tall = both + [
            turned(both[e % blocks], lanes - SLOT * (e // blocks), -1)
            for e in range(blocks, blocks + 2 * HALO)
        ]
    field = jnp.concatenate(tall, axis=0)
    moved = jnp.dot(field, halo_matrix(lanes), preferred_element_type=F32)
    count = len(tall)
    for a in range(TAPS - 1):
        part = moved[:, a * lanes : (a + 1) * lanes].astype(BF)
        xe[a, :count] = part.reshape(count, chans, lanes)
        xe[a, count:] = jnp.zeros((SPAN - count, chans, lanes), BF)
    low = HALO * DEPTH
    for g in range(chans // GROUP):
        at = slice(GROUP * g, GROUP * (g + 1))
        rhs = jnp.concatenate([xe[a, :, at, :].reshape(DEPTH, lanes) for a in range(TAPS - 1)], axis=0)
        lhs = jnp.concatenate([band[g, :, :low], band[g, :, low + DEPTH : wide]], axis=1)
        out = jnp.dot(lhs, rhs, preferred_element_type=F32)
        halo[:, at, :] = out.reshape(blocks, GROUP, lanes)


def branch_of(a_ref, halo, slot0, gain, up_t, down_t):
    count, chans, lanes = a_ref.shape
    blocks = halo.shape[0]
    edge = edge_lanes((chans, lanes))
    normed = []
    for r in range(count):
        shift = lax.rem(lanes - SLOT * (slot0 + r // blocks), lanes)
        a = a_ref[r] + jnp.where(edge, pltpu.roll(halo[r % blocks], shift, 1), 0.0)
        center = a - jnp.mean(a, axis=0, keepdims=True)
        var = jnp.mean(center * center, axis=0, keepdims=True)
        normed.append((center * lax.rsqrt(var + 1e-06) * gain).astype(BF))
    z = jnp.dot(up_t, jnp.concatenate(normed, axis=1), preferred_element_type=F32)
    h = twice_gelu(z.astype(BF))
    return jnp.dot(down_t, h, preferred_element_type=F32)


def first_kernel(x_ref, a_ref, left_ref, right_ref, band_ref, g_ref, up_ref, dn_ref, s_ref, y_ref, p_ref, xe, halo, up_t, dn_t, gain, scale):
    step = pl.program_id(0)
    count, chans, lanes = x_ref.shape
    blocks = halo.shape[0]

    @pl.when(step == 0)
    def _():
        halo_conv(left_ref, right_ref, band_ref, True, xe, halo)
        up_t[...] = transposed(up_ref[0])
        dn_t[...] = halved(dn_ref[0])
        gain[...] = spread(g_ref[0:1], lanes)
        scale[...] = spread(s_ref[0:1], lanes)
        p_ref[...] = jnp.zeros(p_ref.shape, BF)

    slot0 = step * (count // blocks)
    branch = branch_of(a_ref, halo, slot0, gain[...], up_t[...], dn_t[...])
    keep = edge_lanes((chans, lanes)).astype(F32).astype(BF)
    for r in range(count):
        y = x_ref[r].astype(F32) + scale[...] * branch[:, r * lanes : (r + 1) * lanes]
        y = y.astype(BF)
        y_ref[r] = y
        moved = pltpu.roll(y * keep, SLOT * (slot0 + r // blocks), 1)
        p_ref[r % blocks] = p_ref[r % blocks] + moved


def first_block(x, a, left, right, band, gain, up, down, scale, step):
    rows, chans, lanes = x.shape
    blocks = rows // SLOTS
    hid = up.shape[2]
    part = pl.BlockSpec((step, chans, lanes), lambda i: (i, 0, 0))
    return pl.pallas_call(
        first_kernel,
        grid=(rows // step,),
        out_shape=[
            jax.ShapeDtypeStruct(x.shape, BF),
            jax.ShapeDtypeStruct((blocks, chans, lanes), BF),
        ],
        in_specs=[part, part] + [VMEM] * 7,
        out_specs=[part, pl.BlockSpec((blocks, chans, lanes), lambda i: (0, 0, 0))],
        scratch_shapes=[
            pltpu.VMEM((TAPS - 1, SPAN, chans, lanes), BF),
            pltpu.VMEM((blocks, chans, lanes), F32),
            pltpu.VMEM((hid, chans), BF),
            pltpu.VMEM((chans, hid), BF),
            pltpu.VMEM((chans, lanes), F32),
            pltpu.VMEM((chans, lanes), F32),
        ],
        compiler_params=params(24),
        cost_estimate=cost(8),
        name="first_block",
    )(x, a, left, right, band, gain, up, down, scale)


def second_kernel(near, members, at_ref, *refs):
    x_ref, a_ref, left_ref, right_ref, band_ref, g_ref, up_ref, dn_ref, s_ref, fw_ref = refs[:10]
    refs = refs[10:]
    if near:
        old_ref = refs[1]
        refs = refs[2:]
    y_ref, refs = refs[0], refs[1:]
    half = members // 2
    chunk_refs, refs = refs[:half], refs[half:]
    flux, xe, halo, up_t, dn_t, gain, scale = refs
    step = pl.program_id(0)
    count, chans, lanes = x_ref.shape
    blocks = halo.shape[0]
    tall = flux.shape[0]

    @pl.when(step == 0)
    def _():
        halo_conv(left_ref, right_ref, band_ref, True, xe, halo)
        up_t[...] = transposed(up_ref[1])
        dn_t[...] = halved(dn_ref[1])
        gain[...] = spread(g_ref[1:2], lanes)
        scale[...] = spread(s_ref[1:2], lanes)
        if near:
            flux[...] = old_ref[...]
        else:
            flux[0:HALO] = jnp.zeros((HALO,) + flux.shape[1:], BF)
            flux[tall - HALO : tall] = jnp.zeros((HALO,) + flux.shape[1:], BF)

    row0 = (at_ref[0] + step) * count
    slot0 = (at_ref[0] + step) * (count // blocks)
    branch = branch_of(a_ref, halo, slot0, gain[...], up_t[...], dn_t[...])
    made = []
    for r in range(count):
        y = x_ref[r].astype(F32) + scale[...] * branch[:, r * lanes : (r + 1) * lanes]
        made.append(y.astype(BF))
        y_ref[r] = made[r]
    z = jnp.dot(fw_ref[...], jnp.concatenate(made, axis=1), preferred_element_type=F32)
    f = (0.5 * twice_gelu(z)).astype(BF)
    for r in range(count):
        flux[row0 + HALO + r] = f[:, r * lanes : (r + 1) * lanes]

    @pl.when(step == pl.num_programs(0) - 1)
    def _():
        rank = lax.axis_index("member")
        share = (tall - 2 * HALO) // members
        for k in range(half):
            dst = rank ^ (k if near else half + k)
            chunk_refs[k][...] = flux[pl.ds(dst * share, share + 2 * HALO)]


def second_block(near, members, at, x, a, left, right, band, gain, up, down, scale, flux_weight, earlier, step, steps):
    rows, chans, lanes = x.shape
    blocks = rows // SLOTS
    hid = up.shape[2]
    flux = flux_weight.shape[0]
    half = members // 2
    share = rows // members
    part = pl.BlockSpec((step, chans, lanes), lambda i, s: (s[0] + i, 0, 0))
    args = [at, x, a, left, right, band, gain, up, down, scale, flux_weight]
    in_specs = [part, part] + [VMEM] * 8
    alias = {}
    if near:
        alias = {len(args): 0}
        args += earlier
        in_specs += [ANY, VMEM]
    outs = [jax.ShapeDtypeStruct(x.shape, BF)]
    outs += [jax.ShapeDtypeStruct((share + 2 * HALO, flux, lanes), BF)] * half
    out_specs = [part] + [VMEM] * half
    scratch = [
        pltpu.VMEM((TAPS - 1, SPAN, chans, lanes), BF),
        pltpu.VMEM((blocks, chans, lanes), F32),
        pltpu.VMEM((hid, chans), BF),
        pltpu.VMEM((chans, hid), BF),
        pltpu.VMEM((chans, lanes), F32),
        pltpu.VMEM((chans, lanes), F32),
    ]
    field = (rows + 2 * HALO, flux, lanes)
    if near:
        scratch = [pltpu.VMEM(field, BF)] + scratch
    else:
        outs.append(jax.ShapeDtypeStruct(field, BF))
        out_specs.append(VMEM)
    return pl.pallas_call(
        functools.partial(second_kernel, near, members),
        out_shape=outs,
        grid_spec=pltpu.PrefetchScalarGridSpec(
            num_scalar_prefetch=1,
            grid=(steps,),
            in_specs=in_specs,
            out_specs=out_specs,
            scratch_shapes=scratch,
        ),
        input_output_aliases=alias,
        compiler_params=params(24),
        cost_estimate=cost(8 * steps * step / rows),
        name="second_block",
    )(*args)


def force_kernel(members, *refs):
    flux_refs = refs[:members]
    ocean_ref, land_ref, ice_ref, lift_ref, mid_ref, p_ref, win, sem = refs[members:]
    span, flux, lanes = flux_refs[0].shape
    rows = land_ref.shape[0]
    chans = mid_ref.shape[1]
    share = rows // members
    blocks = p_ref.shape[0]
    first = lax.axis_index("member") * share - HALO
    start = jnp.clip(first, 0, rows - span)
    copy = pltpu.make_async_copy(ocean_ref.at[pl.ds(start, span)], win, sem)
    copy.start()
    total = flux_refs[0][...].astype(F32)
    for ref in flux_refs[1:]:
        total = total + ref[...].astype(F32)
    low = (total / members).astype(BF)
    lift = jnp.concatenate([transposed(lift_ref[0]), transposed(lift_ref[1])], axis=0)
    terms = jnp.dot(
        lift, jnp.concatenate([low[r] for r in range(span)], axis=1), preferred_element_type=F32
    )
    keep = edge_lanes((chans, lanes)).astype(F32).astype(BF)
    packed = [None] * blocks
    copy.wait()
    for r in range(span):
        row = first + r
        safe = jnp.clip(row, 0, rows - 1)
        sea = (1 - land_ref[pl.ds(safe, 1), :]).astype(F32)
        ice = ice_ref[pl.ds(safe, 1), :].astype(F32)
        at = slice(r * lanes, (r + 1) * lanes)
        forcing = sea * ((1.0 - ice) * terms[:chans, at] + ice * terms[chans:, at])
        mid = win[jnp.clip(row - start, 0, span - 1)].astype(F32) + forcing
        inside = (row >= 0) & (row < rows)
        mid = jnp.where(inside, mid, 0.0).astype(BF)
        mid_ref[r] = mid
        q, slot = r % blocks, r // blocks
        moved = mid * keep
        if slot:
            moved = pltpu.roll(moved, SLOT * slot, 1)
        packed[q] = moved if packed[q] is None else packed[q] + moved
    for q in range(blocks):
        p_ref[q] = packed[q]


def force(members, chunks, ocean, land, ice, lift):
    span, _, lanes = chunks[0].shape
    rows, chans, _ = ocean.shape
    return pl.pallas_call(
        functools.partial(force_kernel, members),
        out_shape=[
            jax.ShapeDtypeStruct((span, chans, lanes), BF),
            jax.ShapeDtypeStruct((OCEAN_BLOCKS, chans, lanes), BF),
        ],
        in_specs=[VMEM] * members + [ANY, VMEM, VMEM, VMEM],
        out_specs=[VMEM] * 2,
        scratch_shapes=[pltpu.VMEM((span, chans, lanes), BF), pltpu.SemaphoreType.DMA(())],
        compiler_params=params(24),
        name="ocean_forcing",
    )(*chunks, ocean, land, ice, lift)


def ocean_kernel(mid_ref, a_ref, left_ref, right_ref, band_ref, land_ref, g_ref, up_ref, dn_ref, s_ref, sw_ref, new_ref, surf_ref, xe, halo):
    share, chans, lanes = new_ref.shape
    halo_conv(left_ref, right_ref, band_ref, False, xe, halo)
    gain = spread(g_ref[...], lanes)
    scale = spread(s_ref[...], lanes)
    branch = branch_of(
        a_ref, halo, 0, gain, transposed(up_ref[...]), halved(dn_ref[...])
    )
    first = lax.axis_index("member") * share
    made = []
    for r in range(share):
        sea = (1 - land_ref[pl.ds(first + r, 1), :]).astype(F32)
        y = mid_ref[HALO + r].astype(F32) + scale * branch[:, r * lanes : (r + 1) * lanes]
        made.append((y * sea).astype(BF))
        new_ref[r] = made[r]
    surf = jnp.dot(
        sw_ref[...], jnp.concatenate(made, axis=1), preferred_element_type=F32
    )
    for r in range(share):
        surf_ref[r] = surf[:, r * lanes : (r + 1) * lanes].astype(BF)


def ocean_block(mid, a, left, right, band, land, gain, up, down, scale, surf_weight):
    share, chans, lanes = a.shape
    blocks = left.shape[0]
    return pl.pallas_call(
        ocean_kernel,
        out_shape=[
            jax.ShapeDtypeStruct((share, chans, lanes), BF),
            jax.ShapeDtypeStruct((share, surf_weight.shape[0], lanes), BF),
        ],
        in_specs=[VMEM] * 11,
        out_specs=[VMEM] * 2,
        scratch_shapes=[
            pltpu.VMEM((TAPS - 1, SPAN, chans, lanes), BF),
            pltpu.VMEM((blocks, chans, lanes), F32),
        ],
        compiler_params=params(24),
        name="ocean_block",
    )(mid, a, left, right, band, land, gain[None], up, down, scale[None], surf_weight)


def couple_kernel(y_ref, surf_ref, land_ref, bw_ref, o_ref):
    share, chans, lanes = y_ref.shape
    surf = jnp.concatenate([surf_ref[0, r] for r in range(share)], axis=1)
    back = jnp.dot(transposed(bw_ref[...]), surf, preferred_element_type=F32)
    first = pl.program_id(0) * share
    for r in range(share):
        sea = (1 - land_ref[pl.ds(first + r, 1), :]).astype(F32)
        out = y_ref[r].astype(F32) + sea * back[:, r * lanes : (r + 1) * lanes]
        o_ref[r] = out.astype(BF)


def couple(y, surface, land, back_weight):
    members, share, surf, lanes = surface.shape
    chans = y.shape[1]
    rows = pl.BlockSpec((share, chans, lanes), lambda i: (i, 0, 0))
    return pl.pallas_call(
        couple_kernel,
        grid=(members,),
        out_shape=jax.ShapeDtypeStruct(y.shape, BF),
        in_specs=[
            rows,
            pl.BlockSpec((1, share, surf, lanes), lambda i: (i, 0, 0, 0)),
            VMEM,
            VMEM,
        ],
        out_specs=rows,
        compiler_params=params(24),
        name="couple",
    )(y, surface, land, back_weight)


def local(
    atmos,
    ocean,
    land_mask,
    ice_mask,
    atm_kernel,
    atm_gain,
    atm_up,
    atm_down,
    atm_scale,
    flux_weight,
    flux_lift,
    ocn_kernel,
    ocn_gain,
    ocn_up,
    ocn_down,
    ocn_scale,
    surf_weight,
    back_weight,
):
    members = lax.axis_size("member")
    rank = lax.axis_index("member")
    half = members // 2
    state = atmos[0]
    rows = state.shape[0]
    blocks = rows // SLOTS
    big, small = 4 * blocks, 2 * blocks
    atm = (atm_gain, atm_up, atm_down.transpose(0, 2, 1), atm_scale)
    taps = atm_kernel.transpose(1, 2, 0, 3)

    left, right = neighbours(pack(state, big))
    a, band = convolve(0, state, taps, HALO, blocks)
    state, packed = first_block(state, a, left, right, band, *atm, big)

    left, right = neighbours(packed)
    a, band = convolve(1, state, taps, HALO, blocks)
    near_steps = (rows // 2 - small) // small
    far_steps = rows // small - near_steps
    upper = rank >= half
    far_at = jnp.where(upper, 0, near_steps).astype(jnp.int32)[None]
    near_at = jnp.where(upper, far_steps, 0).astype(jnp.int32)[None]
    shared = (state, a, left, right, band, *atm, flux_weight.T)
    partly, *chunks, flux = second_block(False, members, far_at, *shared, [], small, far_steps)
    sent = [
        lax.ppermute(chunk, "member", [(i, i ^ (half + k)) for i in range(members)])
        for k, chunk in enumerate(chunks)
    ]
    state, *chunks = second_block(True, members, near_at, *shared, [partly, flux], small, near_steps)
    sent += [
        lax.ppermute(chunks[k], "member", [(i, i ^ k) for i in range(members)])
        for k in range(half - 1, 0, -1)
    ]
    sent.append(chunks[0])

    mid, packed = force(members, sent, ocean, land_mask, ice_mask, flux_lift)
    left, right = neighbours(packed)
    a, band = convolve(None, mid, ocn_kernel, 0, OCEAN_BLOCKS)
    ocean_rows, surface = ocean_block(
        mid, a, left, right, band, land_mask, ocn_gain, ocn_up, ocn_down.T, ocn_scale, surf_weight.T
    )
    surface = lax.all_gather(surface, "member")
    out = couple(state, surface, land_mask, back_weight)
    return (out[None], ocean_rows)


def solution(mesh):
    in_specs = (
        P("member", None, None, "lon"),
        P(None, None, "lon"),
        P(None, "lon"),
        P(None, "lon"),
    ) + (P(),) * 14
    out_specs = (P("member", None, None, "lon"), P("member", None, "lon"))
    return jax.shard_map(local, mesh=mesh, in_specs=in_specs, out_specs=out_specs, check_vma=False)
```

```python
import functools

import jax
import jax.numpy as jnp
from jax import lax
from jax.experimental import pallas as pl
from jax.experimental.pallas import tpu as pltpu
from jax.sharding import PartitionSpec as P

BF = jnp.bfloat16
F32 = jnp.float32
TANH_A = 0.7978845608028654
TANH_B = TANH_A * 0.044715
TAPS = 7
HALO = 3
GROUP = 16
SPAN = 16
OUT = SPAN - TAPS + 1
DEPTH = GROUP * SPAN
SLOT = 8
SLOTS = 16
OCEAN_BLOCKS = 2
BY_DOT = (0, 1, 5, 6)
VMEM = pl.BlockSpec(memory_space=pltpu.VMEM)
ANY = pl.BlockSpec(memory_space=pl.ANY)
HBM = pl.BlockSpec(memory_space=pltpu.HBM)


def params(mib):
    return pltpu.CompilerParams(vmem_limit_bytes=mib * 2**20)


def cost(gflop):
    return pl.CostEstimate(flops=int(gflop * 1e9), bytes_accessed=0, transcendentals=0)


def twice_gelu(z):
    return z + z * jnp.tanh(z * (TANH_A + TANH_B * (z * z)))


def transposed(value):
    return value.astype(F32).T.astype(BF)


def halved(value):
    return (0.5 * value.astype(F32)).astype(BF)


def spread(row, lanes):
    return jnp.broadcast_to(row.T, (row.shape[1], lanes))


def edge_lanes(shape):
    lane = lax.broadcasted_iota(jnp.int32, shape, len(shape) - 1)
    return (lane < HALO) | (lane >= shape[-1] - HALO)


def pack_kernel(step, src_ref, x_ref, p_ref, sems):
    rows, chans, lanes = x_ref.shape
    blocks = p_ref.shape[0]
    copies = []
    for n in range(rows // step):
        at = slice(n * step, (n + 1) * step)
        copies.append(pltpu.make_async_copy(src_ref.at[at], x_ref.at[at], sems.at[n]))
        copies[n].start()
    keep = edge_lanes((chans, lanes)).astype(F32).astype(BF)
    for n in range(rows // step):
        copies[n].wait()
        for q in range(blocks):
            total = None if n == 0 else p_ref[q]
            for slot in range(n * step // blocks, (n + 1) * step // blocks):
                moved = x_ref[slot * blocks + q] * keep
                if slot:
                    moved = pltpu.roll(moved, SLOT * slot, 1)
                total = moved if total is None else total + moved
            p_ref[q] = total


def pack(x, step):
    rows, chans, lanes = x.shape
    return pl.pallas_call(
        functools.partial(pack_kernel, step),
        out_shape=[
            jax.ShapeDtypeStruct(x.shape, BF),
            jax.ShapeDtypeStruct((rows // SLOTS, chans, lanes), BF),
        ],
        in_specs=[HBM],
        out_specs=[VMEM, VMEM],
        scratch_shapes=[pltpu.SemaphoreType.DMA((rows // step,))],
        compiler_params=params(24),
        name="pack_edges",
    )(x)


def neighbours(packed):
    count = lax.axis_size("lon")
    left = lax.ppermute(packed, "lon", [(i, (i + 1) % count) for i in range(count)])
    right = lax.ppermute(packed, "lon", [((i + 1) % count, i) for i in range(count)])
    return left, right


def shift_matrix(lanes):
    shape = (lanes, len(BY_DOT) * lanes)
    src = lax.broadcasted_iota(jnp.int32, shape, 0)
    dst = lax.broadcasted_iota(jnp.int32, shape, 1)
    hit = jnp.zeros(shape, jnp.bool_)
    for a, j in enumerate(BY_DOT):
        hit = hit | ((dst >= a * lanes) & (dst < (a + 1) * lanes) & (src == dst - a * lanes + j - HALO))
    return hit.astype(F32).astype(BF)


def fill_base(taps, base):
    groups, _, wide = base.shape
    chans = groups * GROUP
    t = lax.broadcasted_iota(jnp.int32, (TAPS, wide), 0)
    n = lax.broadcasted_iota(jnp.int32, (TAPS, wide), 1)
    total = jnp.zeros((chans, wide), F32)
    for i in range(TAPS):
        put = ((t == n // DEPTH) & ((n % DEPTH) // GROUP == i)).astype(F32).astype(BF)
        total = total + jnp.dot(taps(i).T.astype(BF), put, preferred_element_type=F32)
    r = lax.broadcasted_iota(jnp.int32, (chans, wide), 0)
    c = lax.broadcasted_iota(jnp.int32, (chans, wide), 1)
    total = jnp.where(r % GROUP == c % GROUP, total, 0.0)
    for g in range(groups):
        base[g] = total[GROUP * g : GROUP * (g + 1)]


def fill_band(base, g, band):
    for j in range(TAPS):
        one = base[g, :, j * DEPTH : (j + 1) * DEPTH]
        for r in range(OUT):
            moved = pltpu.roll(one, GROUP * r, 1) if r else one
            band[GROUP * r : GROUP * (r + 1), j * DEPTH : (j + 1) * DEPTH] = moved.astype(BF)


def fill_shifts(x, pad, smat, xj):
    count, _, lanes = x.shape
    moved = jnp.dot(x.reshape(count * GROUP, lanes), smat, preferred_element_type=F32)
    for a, j in enumerate(BY_DOT):
        part = moved[:, a * lanes : (a + 1) * lanes].astype(BF)
        xj[j, pad : pad + count] = part.reshape(count, GROUP, lanes)
    lane = lax.broadcasted_iota(jnp.int32, (GROUP, lanes), 1)
    for j in range(TAPS):
        d = j - HALO
        if j in BY_DOT:
            continue
        if d == 0:
            xj[j, pad : pad + count] = x
        else:
            keep = ((lane < lanes - d) if d > 0 else (lane >= -d)).astype(F32).astype(BF)
            xj[j, pad : pad + count] = pltpu.roll(x, (-d) % lanes, 2) * keep[None]


def clear_pads(pad, count, xj):
    tall, _, lanes = xj.shape[1:]
    for j in range(TAPS):
        if pad:
            xj[j, :pad] = jnp.zeros((pad, GROUP, lanes), BF)
        if tall > pad + count:
            xj[j, pad + count :] = jnp.zeros((tall - pad - count, GROUP, lanes), BF)


def apply_band(band, xj, a_ref):
    rows, _, lanes = a_ref.shape
    starts = [min(OUT * i, max(rows - OUT, 0)) for i in range(-(-rows // OUT))]
    field = jnp.concatenate(
        [
            jnp.concatenate([xj[j, s : s + SPAN].reshape(DEPTH, lanes) for j in range(TAPS)], axis=0)
            for s in starts
        ],
        axis=1,
    )
    out = jnp.dot(band, field, preferred_element_type=F32)
    take = min(OUT, rows)
    for n, s in enumerate(starts):
        part = out[: take * GROUP, n * lanes : (n + 1) * lanes]
        a_ref[s : s + take] = part.reshape(take, GROUP, lanes)


def conv_kernel(layer, x_ref, k_ref, a_ref, band_ref, base, smat, xj, band):
    g = pl.program_id(0)
    count, _, lanes = x_ref.shape

    @pl.when(g == 0)
    def _():
        fill_base(lambda i: k_ref[i, :, layer, :], base)
        smat[...] = shift_matrix(lanes)
        clear_pads(HALO, count, xj)

    fill_band(base, g, band)
    band_ref[0] = band[: band_ref.shape[1]]
    fill_shifts(x_ref[...], HALO, smat[...], xj)
    apply_band(band[...], xj, a_ref)


def convolve(layer, x, taps, blocks):
    rows, chans, lanes = x.shape
    groups = chans // GROUP
    wide = TAPS * DEPTH
    part = pl.BlockSpec((rows, GROUP, lanes), lambda g: (0, g, 0))
    return pl.pallas_call(
        functools.partial(conv_kernel, layer),
        grid=(groups,),
        out_shape=[
            jax.ShapeDtypeStruct((rows, chans, lanes), F32),
            jax.ShapeDtypeStruct((groups, blocks * GROUP, wide), BF),
        ],
        in_specs=[part, VMEM],
        out_specs=[part, pl.BlockSpec((1, blocks * GROUP, wide), lambda g: (g, 0, 0))],
        scratch_shapes=[
            pltpu.VMEM((groups, GROUP, wide), F32),
            pltpu.VMEM((lanes, len(BY_DOT) * lanes), BF),
            pltpu.VMEM((TAPS, rows + 2 * HALO, GROUP, lanes), BF),
            pltpu.VMEM((GROUP * OUT, wide), BF),
        ],
        compiler_params=params(24),
        cost_estimate=cost(8),
        name="conv",
    )(x, taps)


def band_kernel(k_ref, band_ref, base):
    fill_base(lambda i: k_ref[i], base)
    for g in range(base.shape[0]):
        fill_band(base, g, band_ref.at[g])


def ocean_band(taps):
    groups = taps.shape[2] // GROUP
    wide = TAPS * DEPTH
    return pl.pallas_call(
        band_kernel,
        out_shape=jax.ShapeDtypeStruct((groups, GROUP * OUT, wide), BF),
        in_specs=[VMEM],
        out_specs=VMEM,
        scratch_shapes=[pltpu.VMEM((groups, GROUP, wide), F32)],
        compiler_params=params(24),
        cost_estimate=cost(3),
        name="ocean_band",
    )(taps)


def ocean_conv_kernel(x_ref, band_ref, a_ref, xj):
    count, chans, lanes = x_ref.shape
    smat = shift_matrix(lanes)
    clear_pads(0, count, xj)
    for g in range(chans // GROUP):
        at = slice(GROUP * g, GROUP * (g + 1))
        fill_shifts(x_ref[:, at, :], 0, smat, xj)
        apply_band(band_ref[g], xj, a_ref.at[:, at, :])


def ocean_conv(x, band):
    count, chans, lanes = x.shape
    return pl.pallas_call(
        ocean_conv_kernel,
        out_shape=jax.ShapeDtypeStruct((count - 2 * HALO, chans, lanes), F32),
        in_specs=[VMEM, VMEM],
        out_specs=VMEM,
        scratch_shapes=[pltpu.VMEM((TAPS, max(count, SPAN), GROUP, lanes), BF)],
        compiler_params=params(24),
        cost_estimate=cost(2),
        name="ocean_conv",
    )(x, band)


def halo_matrix(lanes):
    side = [j for j in range(TAPS) if j != HALO]
    shape = (2 * lanes, len(side) * lanes)
    src = lax.broadcasted_iota(jnp.int32, shape, 0)
    dst = lax.broadcasted_iota(jnp.int32, shape, 1)
    hit = jnp.zeros(shape, jnp.bool_)
    to = dst % lanes
    for a, j in enumerate(side):
        d = j - HALO
        here = (dst >= a * lanes) & (dst < (a + 1) * lanes)
        from_ = (to + d + lanes) % lanes
        if d > 0:
            ok = (src == from_) & (src % SLOT < HALO) & (to % SLOT >= SLOT - HALO)
        else:
            ok = (src == from_ + lanes) & (src % SLOT >= SLOT - HALO) & (to % SLOT < HALO)
        hit = hit | (here & ok)
    return hit.astype(F32).astype(BF)


def halo_conv(left, right, band, wrapped, xe, halo):
    blocks, chans, lanes = halo.shape
    wide = TAPS * DEPTH
    both = [jnp.concatenate([right[q], left[q]], axis=1) for q in range(blocks)]
    lane = lax.broadcasted_iota(jnp.int32, (chans, lanes), 1)
    slot = (lane + HALO) // SLOT % SLOTS

    def turned(value, shift, drop):
        parts = [pltpu.roll(value[:, n * lanes : (n + 1) * lanes], shift, 1) for n in range(2)]
        if drop >= 0:
            keep = (slot != drop).astype(F32).astype(BF)
            parts = [part * keep for part in parts]
        return jnp.concatenate(parts, axis=1)

    if wrapped:
        tall = (
            [turned(both[q], SLOT, 0) for q in range(blocks - HALO, blocks)]
            + both
            + [turned(both[q], lanes - SLOT, SLOTS - 1) for q in range(HALO)]
        )
    else:
        tall = both + [
            turned(both[e % blocks], lanes - SLOT * (e // blocks), -1)
            for e in range(blocks, blocks + 2 * HALO)
        ]
    field = jnp.concatenate(tall, axis=0)
    moved = jnp.dot(field, halo_matrix(lanes), preferred_element_type=F32)
    count = len(tall)
    for a in range(TAPS - 1):
        part = moved[:, a * lanes : (a + 1) * lanes].astype(BF)
        xe[a, :count] = part.reshape(count, chans, lanes)
        xe[a, count:] = jnp.zeros((SPAN - count, chans, lanes), BF)
    low = HALO * DEPTH
    for g in range(chans // GROUP):
        at = slice(GROUP * g, GROUP * (g + 1))
        rhs = jnp.concatenate([xe[a, :, at, :].reshape(DEPTH, lanes) for a in range(TAPS - 1)], axis=0)
        tops = slice(0, blocks * GROUP)
        lhs = jnp.concatenate([band[g, tops, :low], band[g, tops, low + DEPTH : wide]], axis=1)
        out = jnp.dot(lhs, rhs, preferred_element_type=F32)
        halo[:, at, :] = out.reshape(blocks, GROUP, lanes)


def branch_of(a_ref, halo, slot0, gain, up_t, down_t):
    count, chans, lanes = a_ref.shape
    blocks = halo.shape[0]
    edge = edge_lanes((chans, lanes))
    normed = []
    for r in range(count):
        shift = lax.rem(lanes - SLOT * (slot0 + r // blocks), lanes)
        a = a_ref[r] + jnp.where(edge, pltpu.roll(halo[r % blocks], shift, 1), 0.0)
        center = a - jnp.mean(a, axis=0, keepdims=True)
        var = jnp.mean(center * center, axis=0, keepdims=True)
        normed.append((center * lax.rsqrt(var + 1e-06) * gain).astype(BF))
    z = jnp.dot(up_t, jnp.concatenate(normed, axis=1), preferred_element_type=F32)
    h = twice_gelu(z.astype(BF))
    return jnp.dot(down_t, h, preferred_element_type=F32)


def first_kernel(x_ref, a_ref, left_ref, right_ref, band_ref, g_ref, up_ref, dn_ref, s_ref, y_ref, p_ref, xe, halo, up_t, dn_t, gain, scale):
    step = pl.program_id(0)
    count, chans, lanes = x_ref.shape
    blocks = halo.shape[0]

    @pl.when(step == 0)
    def _():
        halo_conv(left_ref, right_ref, band_ref, True, xe, halo)
        up_t[...] = transposed(up_ref[0])
        dn_t[...] = halved(dn_ref[0])
        gain[...] = spread(g_ref[0:1], lanes)
        scale[...] = spread(s_ref[0:1], lanes)
        p_ref[...] = jnp.zeros(p_ref.shape, BF)

    slot0 = step * (count // blocks)
    branch = branch_of(a_ref, halo, slot0, gain[...], up_t[...], dn_t[...])
    keep = edge_lanes((chans, lanes)).astype(F32).astype(BF)
    for r in range(count):
        y = x_ref[r].astype(F32) + scale[...] * branch[:, r * lanes : (r + 1) * lanes]
        y = y.astype(BF)
        y_ref[r] = y
        moved = pltpu.roll(y * keep, SLOT * (slot0 + r // blocks), 1)
        p_ref[r % blocks] = p_ref[r % blocks] + moved


def first_block(x, a, left, right, band, gain, up, down, scale, step):
    rows, chans, lanes = x.shape
    blocks = rows // SLOTS
    hid = up.shape[2]
    part = pl.BlockSpec((step, chans, lanes), lambda i: (i, 0, 0))
    return pl.pallas_call(
        first_kernel,
        grid=(rows // step,),
        out_shape=[
            jax.ShapeDtypeStruct(x.shape, BF),
            jax.ShapeDtypeStruct((blocks, chans, lanes), BF),
        ],
        in_specs=[part, part] + [VMEM] * 7,
        out_specs=[part, pl.BlockSpec((blocks, chans, lanes), lambda i: (0, 0, 0))],
        scratch_shapes=[
            pltpu.VMEM((TAPS - 1, SPAN, chans, lanes), BF),
            pltpu.VMEM((blocks, chans, lanes), F32),
            pltpu.VMEM((hid, chans), BF),
            pltpu.VMEM((chans, hid), BF),
            pltpu.VMEM((chans, lanes), F32),
            pltpu.VMEM((chans, lanes), F32),
        ],
        compiler_params=params(24),
        cost_estimate=cost(8),
        name="first_block",
    )(x, a, left, right, band, gain, up, down, scale)


def second_kernel(near, members, at_ref, *refs):
    x_ref, a_ref, g_ref, up_ref, dn_ref, s_ref, fw_ref = refs[:7]
    refs = refs[7:]
    if near:
        _, old_ref, halo = refs[:3]
        refs = refs[3:]
    else:
        left_ref, right_ref, band_ref = refs[:3]
        refs = refs[3:]
    y_ref, keep_ref, give_ref = refs[:3]
    if near:
        flux, up_t, dn_t, gain, scale = refs[3:]
    else:
        flux, halo, xe, up_t, dn_t, gain, scale = refs[3:]
    half = members // 2
    step = pl.program_id(0)
    count, chans, lanes = x_ref.shape
    blocks = halo.shape[0]
    tall = flux.shape[0]

    @pl.when(step == 0)
    def _():
        up_t[...] = transposed(up_ref[1])
        dn_t[...] = halved(dn_ref[1])
        gain[...] = spread(g_ref[1:2], lanes)
        scale[...] = spread(s_ref[1:2], lanes)
        if near:
            flux[...] = old_ref[...]
        else:
            halo_conv(left_ref, right_ref, band_ref, True, xe, halo)
            flux[0:HALO] = jnp.zeros((HALO,) + flux.shape[1:], BF)
            flux[tall - HALO : tall] = jnp.zeros((HALO,) + flux.shape[1:], BF)

    row0 = (at_ref[0] + step) * count
    slot0 = (at_ref[0] + step) * (count // blocks)
    branch = branch_of(a_ref, halo, slot0, gain[...], up_t[...], dn_t[...])
    made = []
    for r in range(count):
        y = x_ref[r].astype(F32) + scale[...] * branch[:, r * lanes : (r + 1) * lanes]
        made.append(y.astype(BF))
        y_ref[r] = made[r]
    z = jnp.dot(fw_ref[...], jnp.concatenate(made, axis=1), preferred_element_type=F32)
    f = (0.5 * twice_gelu(z)).astype(BF)
    for r in range(count):
        flux[row0 + HALO + r] = f[:, r * lanes : (r + 1) * lanes]

    @pl.when(step == pl.num_programs(0) - 1)
    def _():
        rank = lax.axis_index("member")
        share = (tall - 2 * HALO) // members
        for k in range(half):
            dst = rank ^ (k if near else half + k)
            chunk = flux[pl.ds(dst * share, share + 2 * HALO)]
            if k % 2:
                give_ref[k // 2] = chunk
            else:
                keep_ref[k // 2] = chunk


def second_block(near, members, at, x, a, weights, others, step, steps):
    rows, chans, lanes = x.shape
    blocks = rows // SLOTS
    gain, up, down, scale, flux_weight = weights
    hid = up.shape[2]
    flux = flux_weight.shape[0]
    share = rows // members
    part = pl.BlockSpec((step, chans, lanes), lambda i, s: (s[0] + i, 0, 0))
    chunks = jax.ShapeDtypeStruct((members // 4, share + 2 * HALO, flux, lanes), BF)
    field = jax.ShapeDtypeStruct((rows + 2 * HALO, flux, lanes), BF)
    halo = jax.ShapeDtypeStruct((blocks, chans, lanes), F32)
    args = [at, x, a, gain, up, down, scale, flux_weight, *others]
    outs = [jax.ShapeDtypeStruct(x.shape, BF), chunks, chunks]
    scratch = [
        pltpu.VMEM((hid, chans), BF),
        pltpu.VMEM((chans, hid), BF),
        pltpu.VMEM((chans, lanes), F32),
        pltpu.VMEM((chans, lanes), F32),
    ]
    if near:
        scratch = [pltpu.VMEM(field.shape, BF)] + scratch
        other_specs = [ANY, VMEM, VMEM]
    else:
        scratch = [pltpu.VMEM((TAPS - 1, SPAN, chans, lanes), BF)] + scratch
        outs += [field, halo]
        other_specs = [VMEM] * 3
    return pl.pallas_call(
        functools.partial(second_kernel, near, members),
        out_shape=outs,
        grid_spec=pltpu.PrefetchScalarGridSpec(
            num_scalar_prefetch=1,
            grid=(steps,),
            in_specs=[part, part] + [VMEM] * 5 + other_specs,
            out_specs=[part] + [VMEM] * (len(outs) - 1),
            scratch_shapes=scratch,
        ),
        input_output_aliases={8: 0} if near else {},
        compiler_params=params(24),
        cost_estimate=cost(8 * steps * step / rows),
        name="second_block",
    )(*args)


def add_kernel(keep_ref, got_ref, *out_refs):
    for n, ref in enumerate(out_refs):
        k = n + keep_ref.shape[0] - len(out_refs)
        ref[...] = (keep_ref[k].astype(F32) + got_ref[k].astype(F32)).astype(BF)


def add_pairs(keep, got, skip):
    count = keep.shape[0] - skip
    return pl.pallas_call(
        add_kernel,
        out_shape=[jax.ShapeDtypeStruct(keep.shape[1:], BF)] * count,
        in_specs=[VMEM] * 2,
        out_specs=[VMEM] * count,
        compiler_params=params(24),
        name="add_pairs",
    )(keep, got)


def send_xor(value, bits):
    members = lax.axis_size("member")
    return lax.ppermute(value, "member", [(i, i ^ bits) for i in range(members)])


def force_kernel(members, *refs):
    near_refs, flux_refs = refs[:2], refs[2 : members // 2 + 1]
    ocean_ref, land_ref, ice_ref, lift_ref, mid_ref, p_ref, win, sem = refs[members // 2 + 1 :]
    span, flux, lanes = flux_refs[0].shape
    rows = land_ref.shape[0]
    chans = mid_ref.shape[1]
    share = rows // members
    blocks = p_ref.shape[0]
    first = lax.axis_index("member") * share - HALO
    start = jnp.clip(first, 0, rows - span)
    copy = pltpu.make_async_copy(ocean_ref.at[pl.ds(start, span)], win, sem)
    copy.start()
    total = near_refs[0][0].astype(F32) + near_refs[1][0].astype(F32)
    for ref in flux_refs:
        total = total + ref[...].astype(F32)
    low = (total / members).astype(BF)
    lift = jnp.concatenate([transposed(lift_ref[0]), transposed(lift_ref[1])], axis=0)
    terms = jnp.dot(
        lift, jnp.concatenate([low[r] for r in range(span)], axis=1), preferred_element_type=F32
    )
    keep = edge_lanes((chans, lanes)).astype(F32).astype(BF)
    packed = [None] * blocks
    copy.wait()
    for r in range(span):
        row = first + r
        safe = jnp.clip(row, 0, rows - 1)
        sea = (1 - land_ref[pl.ds(safe, 1), :]).astype(F32)
        ice = ice_ref[pl.ds(safe, 1), :].astype(F32)
        at = slice(r * lanes, (r + 1) * lanes)
        forcing = sea * ((1.0 - ice) * terms[:chans, at] + ice * terms[chans:, at])
        mid = win[jnp.clip(row - start, 0, span - 1)].astype(F32) + forcing
        inside = (row >= 0) & (row < rows)
        mid = jnp.where(inside, mid, 0.0).astype(BF)
        mid_ref[r] = mid
        q, slot = r % blocks, r // blocks
        moved = mid * keep
        if slot:
            moved = pltpu.roll(moved, SLOT * slot, 1)
        packed[q] = moved if packed[q] is None else packed[q] + moved
    for q in range(blocks):
        p_ref[q] = packed[q]


def force(members, chunks, ocean, land, ice, lift):
    span, _, lanes = chunks[-1].shape
    rows, chans, _ = ocean.shape
    return pl.pallas_call(
        functools.partial(force_kernel, members),
        out_shape=[
            jax.ShapeDtypeStruct((span, chans, lanes), BF),
            jax.ShapeDtypeStruct((OCEAN_BLOCKS, chans, lanes), BF),
        ],
        in_specs=[VMEM] * len(chunks) + [HBM, VMEM, VMEM, VMEM],
        out_specs=[VMEM] * 2,
        scratch_shapes=[pltpu.VMEM((span, chans, lanes), BF), pltpu.SemaphoreType.DMA(())],
        compiler_params=params(24),
        name="ocean_forcing",
    )(*chunks, ocean, land, ice, lift)


def ocean_kernel(mid_ref, a_ref, left_ref, right_ref, band_ref, land_ref, g_ref, up_ref, dn_ref, s_ref, sw_ref, new_ref, surf_ref, xe, halo):
    share, chans, lanes = new_ref.shape
    halo_conv(left_ref, right_ref, band_ref, False, xe, halo)
    gain = spread(g_ref[...], lanes)
    scale = spread(s_ref[...], lanes)
    branch = branch_of(
        a_ref, halo, 0, gain, transposed(up_ref[...]), halved(dn_ref[...])
    )
    first = lax.axis_index("member") * share
    made = []
    for r in range(share):
        sea = (1 - land_ref[pl.ds(first + r, 1), :]).astype(F32)
        y = mid_ref[HALO + r].astype(F32) + scale * branch[:, r * lanes : (r + 1) * lanes]
        made.append((y * sea).astype(BF))
        new_ref[r] = made[r]
    surf = jnp.dot(
        sw_ref[...], jnp.concatenate(made, axis=1), preferred_element_type=F32
    )
    for r in range(share):
        surf_ref[r] = surf[:, r * lanes : (r + 1) * lanes].astype(BF)


def ocean_block(mid, a, left, right, band, land, gain, up, down, scale, surf_weight):
    share, chans, lanes = a.shape
    blocks = left.shape[0]
    return pl.pallas_call(
        ocean_kernel,
        out_shape=[
            jax.ShapeDtypeStruct((share, chans, lanes), BF),
            jax.ShapeDtypeStruct((share, surf_weight.shape[0], lanes), BF),
        ],
        in_specs=[VMEM] * 11,
        out_specs=[VMEM] * 2,
        scratch_shapes=[
            pltpu.VMEM((TAPS - 1, SPAN, chans, lanes), BF),
            pltpu.VMEM((blocks, chans, lanes), F32),
        ],
        compiler_params=params(24),
        name="ocean_block",
    )(mid, a, left, right, band, land, gain[None], up, down, scale[None], surf_weight)


def couple_kernel(y_ref, surf_ref, land_ref, bw_ref, o_ref):
    share, chans, lanes = y_ref.shape
    surf = jnp.concatenate([surf_ref[0, r] for r in range(share)], axis=1)
    back = jnp.dot(transposed(bw_ref[...]), surf, preferred_element_type=F32)
    first = pl.program_id(0) * share
    for r in range(share):
        sea = (1 - land_ref[pl.ds(first + r, 1), :]).astype(F32)
        out = y_ref[r].astype(F32) + sea * back[:, r * lanes : (r + 1) * lanes]
        o_ref[r] = out.astype(BF)


def couple(y, surface, land, back_weight):
    members, share, surf, lanes = surface.shape
    chans = y.shape[1]
    rows = pl.BlockSpec((share, chans, lanes), lambda i: (i, 0, 0))
    return pl.pallas_call(
        couple_kernel,
        grid=(members,),
        out_shape=jax.ShapeDtypeStruct(y.shape, BF),
        in_specs=[
            rows,
            pl.BlockSpec((1, share, surf, lanes), lambda i: (i, 0, 0, 0)),
            VMEM,
            VMEM,
        ],
        out_specs=rows,
        compiler_params=params(24),
        name="couple",
    )(y, surface, land, back_weight)


def local(
    atmos,
    ocean,
    land_mask,
    ice_mask,
    atm_kernel,
    atm_gain,
    atm_up,
    atm_down,
    atm_scale,
    flux_weight,
    flux_lift,
    ocn_kernel,
    ocn_gain,
    ocn_up,
    ocn_down,
    ocn_scale,
    surf_weight,
    back_weight,
):
    members = lax.axis_size("member")
    rank = lax.axis_index("member")
    half = members // 2
    state = atmos[0]
    rows = state.shape[0]
    blocks = rows // SLOTS
    big, small = 4 * blocks, 2 * blocks
    atm = (atm_gain, atm_up, atm_down.transpose(0, 2, 1), atm_scale)
    taps = atm_kernel.transpose(1, 2, 0, 3)

    state, packed = pack(state, big)
    left, right = neighbours(packed)
    a, band = convolve(0, state, taps, blocks)
    state, packed = first_block(state, a, left, right, band, *atm, big)

    left, right = neighbours(packed)
    a, band = convolve(1, state, taps, blocks)
    near_steps = (rows // 2 - small) // small
    far_steps = rows // small - near_steps
    upper = rank >= half
    far_at = jnp.where(upper, 0, near_steps).astype(jnp.int32)[None]
    near_at = jnp.where(upper, far_steps, 0).astype(jnp.int32)[None]
    weights = (*atm, flux_weight.T)
    partly, keep, give, flux, halo = second_block(
        False, members, far_at, state, a, weights, [left, right, band], small, far_steps
    )
    got = send_xor(give, 1)
    state, near_keep, near_give = second_block(
        True, members, near_at, state, a, weights, [partly, flux, halo], small, near_steps
    )
    near_got = send_xor(near_give, 1)
    got, near_keep, taps = lax.optimization_barrier((got, near_keep, ocn_kernel))
    sums = add_pairs(keep, got, 0)
    sent = [send_xor(part, half + 2 * k) for k, part in enumerate(sums)]
    sums = add_pairs(near_keep, near_got, 1)
    sent += [send_xor(part, 2 * k + 2) for k, part in enumerate(sums)]
    sent = [near_keep, near_got] + sent
    band = ocean_band(taps)

    mid, packed = force(members, sent, ocean, land_mask, ice_mask, flux_lift)
    left, right = neighbours(packed)
    a = ocean_conv(mid, band)
    ocean_rows, surface = ocean_block(
        mid, a, left, right, band, land_mask, ocn_gain, ocn_up, ocn_down.T, ocn_scale, surf_weight.T
    )
    surface = lax.all_gather(surface, "member")
    out = couple(state, surface, land_mask, back_weight)
    return (out[None], ocean_rows)


def solution(mesh):
    in_specs = (
        P("member", None, None, "lon"),
        P(None, None, "lon"),
        P(None, "lon"),
        P(None, "lon"),
    ) + (P(),) * 14
    out_specs = (P("member", None, None, "lon"), P("member", None, "lon"))
    return jax.shard_map(local, mesh=mesh, in_specs=in_specs, out_specs=out_specs, check_vma=False)
```

```python
import functools

import jax
import jax.numpy as jnp
from jax import lax
from jax.experimental import pallas as pl
from jax.experimental.pallas import tpu as pltpu
from jax.sharding import PartitionSpec as P

BF = jnp.bfloat16
F32 = jnp.float32
TANH_A = 0.7978845608028654
TANH_B = TANH_A * 0.044715
TAPS = 7
HALO = 3
GROUP = 16
SPAN = 16
OUT = SPAN - TAPS + 1
DEPTH = GROUP * SPAN
SLOT = 8
SLOTS = 16
OCEAN_BLOCKS = 2
BIG = 32
BY_DOT = (0, 1, 5, 6)
VMEM = pl.BlockSpec(memory_space=pltpu.VMEM)
ANY = pl.BlockSpec(memory_space=pl.ANY)
HBM = pl.BlockSpec(memory_space=pltpu.HBM)


def params(mib):
    return pltpu.CompilerParams(vmem_limit_bytes=mib * 2**20)


def cost(gflop):
    return pl.CostEstimate(flops=int(gflop * 1e9), bytes_accessed=0, transcendentals=0)


def twice_gelu(z):
    return z + z * jnp.tanh(z * (TANH_A + TANH_B * (z * z)))


def transposed(value):
    return value.astype(F32).T.astype(BF)


def halved(value):
    return (0.5 * value.astype(F32)).astype(BF)


def spread(row, lanes):
    return jnp.broadcast_to(row.T, (row.shape[1], lanes))


def edge_lanes(shape):
    lane = lax.broadcasted_iota(jnp.int32, shape, len(shape) - 1)
    return (lane < HALO) | (lane >= shape[-1] - HALO)


def pack_kernel(step, src_ref, x_ref, p_ref, sems):
    rows, chans, lanes = x_ref.shape
    blocks = p_ref.shape[0]
    copies = []
    for n in range(rows // step):
        at = slice(n * step, (n + 1) * step)
        copies.append(pltpu.make_async_copy(src_ref.at[at], x_ref.at[at], sems.at[n]))
        copies[n].start()
    keep = edge_lanes((chans, lanes)).astype(F32).astype(BF)
    for n in range(rows // step):
        copies[n].wait()
        for q in range(blocks):
            total = None if n == 0 else p_ref[q]
            for slot in range(n * step // blocks, (n + 1) * step // blocks):
                moved = x_ref[slot * blocks + q] * keep
                if slot:
                    moved = pltpu.roll(moved, SLOT * slot, 1)
                total = moved if total is None else total + moved
            p_ref[q] = total


def pack(x, step):
    rows, chans, lanes = x.shape
    return pl.pallas_call(
        functools.partial(pack_kernel, step),
        out_shape=[
            jax.ShapeDtypeStruct(x.shape, BF),
            jax.ShapeDtypeStruct((rows // SLOTS, chans, lanes), BF),
        ],
        in_specs=[HBM],
        out_specs=[VMEM, VMEM],
        scratch_shapes=[pltpu.SemaphoreType.DMA((rows // step,))],
        compiler_params=params(24),
        name="pack_edges",
    )(x)


def neighbours(packed):
    count = lax.axis_size("lon")
    left = lax.ppermute(packed, "lon", [(i, (i + 1) % count) for i in range(count)])
    right = lax.ppermute(packed, "lon", [((i + 1) % count, i) for i in range(count)])
    return left, right


def shift_matrix(lanes):
    shape = (lanes, len(BY_DOT) * lanes)
    src = lax.broadcasted_iota(jnp.int32, shape, 0)
    dst = lax.broadcasted_iota(jnp.int32, shape, 1)
    hit = jnp.zeros(shape, jnp.bool_)
    for a, j in enumerate(BY_DOT):
        hit = hit | ((dst >= a * lanes) & (dst < (a + 1) * lanes) & (src == dst - a * lanes + j - HALO))
    return hit.astype(F32).astype(BF)


def fill_base(taps, base):
    groups, _, wide = base.shape
    chans = groups * GROUP
    t = lax.broadcasted_iota(jnp.int32, (TAPS, wide), 0)
    n = lax.broadcasted_iota(jnp.int32, (TAPS, wide), 1)
    total = jnp.zeros((chans, wide), F32)
    for i in range(TAPS):
        put = ((t == n // DEPTH) & ((n % DEPTH) // GROUP == i)).astype(F32).astype(BF)
        total = total + jnp.dot(taps(i).T.astype(BF), put, preferred_element_type=F32)
    r = lax.broadcasted_iota(jnp.int32, (chans, wide), 0)
    c = lax.broadcasted_iota(jnp.int32, (chans, wide), 1)
    total = jnp.where(r % GROUP == c % GROUP, total, 0.0)
    for g in range(groups):
        base[g] = total[GROUP * g : GROUP * (g + 1)]


def fill_band(base, g, band):
    for j in range(TAPS):
        one = base[g, :, j * DEPTH : (j + 1) * DEPTH]
        for r in range(OUT):
            moved = pltpu.roll(one, GROUP * r, 1) if r else one
            band[GROUP * r : GROUP * (r + 1), j * DEPTH : (j + 1) * DEPTH] = moved.astype(BF)


def fill_shifts(x, pad, smat, xj):
    count, _, lanes = x.shape
    moved = jnp.dot(x.reshape(count * GROUP, lanes), smat, preferred_element_type=F32)
    for a, j in enumerate(BY_DOT):
        part = moved[:, a * lanes : (a + 1) * lanes].astype(BF)
        xj[j, pad : pad + count] = part.reshape(count, GROUP, lanes)
    lane = lax.broadcasted_iota(jnp.int32, (GROUP, lanes), 1)
    for j in range(TAPS):
        d = j - HALO
        if j in BY_DOT:
            continue
        if d == 0:
            xj[j, pad : pad + count] = x
        else:
            keep = ((lane < lanes - d) if d > 0 else (lane >= -d)).astype(F32).astype(BF)
            xj[j, pad : pad + count] = pltpu.roll(x, (-d) % lanes, 2) * keep[None]


def clear_pads(pad, count, xj):
    tall, _, lanes = xj.shape[1:]
    for j in range(TAPS):
        if pad:
            xj[j, :pad] = jnp.zeros((pad, GROUP, lanes), BF)
        if tall > pad + count:
            xj[j, pad + count :] = jnp.zeros((tall - pad - count, GROUP, lanes), BF)


def apply_band(band, xj, a_ref):
    rows, _, lanes = a_ref.shape
    starts = [min(OUT * i, max(rows - OUT, 0)) for i in range(-(-rows // OUT))]
    field = jnp.concatenate(
        [
            jnp.concatenate([xj[j, s : s + SPAN].reshape(DEPTH, lanes) for j in range(TAPS)], axis=0)
            for s in starts
        ],
        axis=1,
    )
    out = jnp.dot(band, field, preferred_element_type=F32)
    take = min(OUT, rows)
    for n, s in enumerate(starts):
        part = out[: take * GROUP, n * lanes : (n + 1) * lanes]
        a_ref[s : s + take] = part.reshape(take, GROUP, lanes)


def conv_kernel(layer, x_ref, k_ref, a_ref, band_ref, base, xj, band):
    rows, chans, lanes = x_ref.shape
    fill_base(lambda i: k_ref[i, :, layer, :], base)
    smat = shift_matrix(lanes)
    clear_pads(HALO, rows, xj)

    def group(g, carry):
        at = pl.ds(pl.multiple_of(GROUP * g, GROUP), GROUP)
        fill_band(base, g, band)
        band_ref[g] = band[: band_ref.shape[1]]
        fill_shifts(x_ref[:, at, :], HALO, smat, xj)
        apply_band(band[...], xj, a_ref.at[:, at, :])
        return carry

    lax.fori_loop(0, chans // GROUP, group, 0)


def convolve(layer, x, taps, blocks):
    rows, chans, lanes = x.shape
    groups = chans // GROUP
    wide = TAPS * DEPTH
    return pl.pallas_call(
        functools.partial(conv_kernel, layer),
        out_shape=[
            jax.ShapeDtypeStruct((rows, chans, lanes), F32),
            jax.ShapeDtypeStruct((groups, blocks * GROUP, wide), BF),
        ],
        in_specs=[VMEM, VMEM],
        out_specs=[VMEM, VMEM],
        scratch_shapes=[
            pltpu.VMEM((groups, GROUP, wide), F32),
            pltpu.VMEM((TAPS, rows + 2 * HALO, GROUP, lanes), BF),
            pltpu.VMEM((GROUP * OUT, wide), BF),
        ],
        compiler_params=params(BIG),
        cost_estimate=cost(8),
        name="conv",
    )(x, taps)


def band_kernel(k_ref, band_ref, base):
    fill_base(lambda i: k_ref[i], base)
    for g in range(base.shape[0]):
        fill_band(base, g, band_ref.at[g])


def ocean_band(taps):
    groups = taps.shape[2] // GROUP
    wide = TAPS * DEPTH
    return pl.pallas_call(
        band_kernel,
        out_shape=jax.ShapeDtypeStruct((groups, GROUP * OUT, wide), BF),
        in_specs=[VMEM],
        out_specs=VMEM,
        scratch_shapes=[pltpu.VMEM((groups, GROUP, wide), F32)],
        compiler_params=params(24),
        cost_estimate=cost(3),
        name="ocean_band",
    )(taps)


def ocean_conv_kernel(x_ref, band_ref, a_ref, xj):
    count, chans, lanes = x_ref.shape
    smat = shift_matrix(lanes)
    clear_pads(0, count, xj)
    for g in range(chans // GROUP):
        at = slice(GROUP * g, GROUP * (g + 1))
        fill_shifts(x_ref[:, at, :], 0, smat, xj)
        apply_band(band_ref[g], xj, a_ref.at[:, at, :])


def ocean_conv(x, band):
    count, chans, lanes = x.shape
    return pl.pallas_call(
        ocean_conv_kernel,
        out_shape=jax.ShapeDtypeStruct((count - 2 * HALO, chans, lanes), F32),
        in_specs=[VMEM, VMEM],
        out_specs=VMEM,
        scratch_shapes=[pltpu.VMEM((TAPS, max(count, SPAN), GROUP, lanes), BF)],
        compiler_params=params(24),
        cost_estimate=cost(2),
        name="ocean_conv",
    )(x, band)


def halo_matrix(lanes):
    side = [j for j in range(TAPS) if j != HALO]
    shape = (2 * lanes, len(side) * lanes)
    src = lax.broadcasted_iota(jnp.int32, shape, 0)
    dst = lax.broadcasted_iota(jnp.int32, shape, 1)
    hit = jnp.zeros(shape, jnp.bool_)
    to = dst % lanes
    for a, j in enumerate(side):
        d = j - HALO
        here = (dst >= a * lanes) & (dst < (a + 1) * lanes)
        from_ = (to + d + lanes) % lanes
        if d > 0:
            ok = (src == from_) & (src % SLOT < HALO) & (to % SLOT >= SLOT - HALO)
        else:
            ok = (src == from_ + lanes) & (src % SLOT >= SLOT - HALO) & (to % SLOT < HALO)
        hit = hit | (here & ok)
    return hit.astype(F32).astype(BF)


def halo_conv(left, right, band, wrapped, xe, halo):
    blocks, chans, lanes = halo.shape
    wide = TAPS * DEPTH
    both = [jnp.concatenate([right[q], left[q]], axis=1) for q in range(blocks)]
    lane = lax.broadcasted_iota(jnp.int32, (chans, lanes), 1)
    slot = (lane + HALO) // SLOT % SLOTS

    def turned(value, shift, drop):
        parts = [pltpu.roll(value[:, n * lanes : (n + 1) * lanes], shift, 1) for n in range(2)]
        if drop >= 0:
            keep = (slot != drop).astype(F32).astype(BF)
            parts = [part * keep for part in parts]
        return jnp.concatenate(parts, axis=1)

    if wrapped:
        tall = (
            [turned(both[q], SLOT, 0) for q in range(blocks - HALO, blocks)]
            + both
            + [turned(both[q], lanes - SLOT, SLOTS - 1) for q in range(HALO)]
        )
    else:
        tall = both + [
            turned(both[e % blocks], lanes - SLOT * (e // blocks), -1)
            for e in range(blocks, blocks + 2 * HALO)
        ]
    field = jnp.concatenate(tall, axis=0)
    moved = jnp.dot(field, halo_matrix(lanes), preferred_element_type=F32)
    count = len(tall)
    for a in range(TAPS - 1):
        part = moved[:, a * lanes : (a + 1) * lanes].astype(BF)
        xe[a, :count] = part.reshape(count, chans, lanes)
        xe[a, count:] = jnp.zeros((SPAN - count, chans, lanes), BF)
    low = HALO * DEPTH
    for g in range(chans // GROUP):
        at = slice(GROUP * g, GROUP * (g + 1))
        rhs = jnp.concatenate([xe[a, :, at, :].reshape(DEPTH, lanes) for a in range(TAPS - 1)], axis=0)
        tops = slice(0, blocks * GROUP)
        lhs = jnp.concatenate([band[g, tops, :low], band[g, tops, low + DEPTH : wide]], axis=1)
        out = jnp.dot(lhs, rhs, preferred_element_type=F32)
        halo[:, at, :] = out.reshape(blocks, GROUP, lanes)


def branch_of(a_ref, row0, count, halo, slot0, gain, up_t, down_t):
    _, chans, lanes = a_ref.shape
    blocks = halo.shape[0]
    edge = edge_lanes((chans, lanes))
    normed = []
    for r in range(count):
        shift = lax.rem(lanes - SLOT * (slot0 + r // blocks), lanes)
        a = a_ref[row0 + r] + jnp.where(edge, pltpu.roll(halo[r % blocks], shift, 1), 0.0)
        center = a - jnp.mean(a, axis=0, keepdims=True)
        var = jnp.mean(center * center, axis=0, keepdims=True)
        normed.append((center * lax.rsqrt(var + 1e-06) * gain).astype(BF))
    z = jnp.dot(up_t, jnp.concatenate(normed, axis=1), preferred_element_type=F32)
    h = twice_gelu(z.astype(BF))
    return jnp.dot(down_t, h, preferred_element_type=F32)


def first_kernel(count, x_ref, a_ref, left_ref, right_ref, band_ref, g_ref, up_ref, dn_ref, s_ref, y_ref, p_ref, xe, halo):
    rows, chans, lanes = x_ref.shape
    blocks = halo.shape[0]
    halo_conv(left_ref, right_ref, band_ref, True, xe, halo)
    up_t = transposed(up_ref[0])
    dn_t = halved(dn_ref[0])
    gain = spread(g_ref[0:1], lanes)
    scale = spread(s_ref[0:1], lanes)
    keep = edge_lanes((chans, lanes)).astype(F32).astype(BF)
    p_ref[...] = jnp.zeros(p_ref.shape, BF)

    def part(step, carry):
        row0 = step * count
        slot0 = step * (count // blocks)
        branch = branch_of(a_ref, row0, count, halo, slot0, gain, up_t, dn_t)
        for r in range(count):
            y = x_ref[row0 + r].astype(F32) + scale * branch[:, r * lanes : (r + 1) * lanes]
            y = y.astype(BF)
            y_ref[row0 + r] = y
            moved = pltpu.roll(y * keep, SLOT * (slot0 + r // blocks), 1)
            p_ref[r % blocks] = p_ref[r % blocks] + moved
        return carry

    lax.fori_loop(0, rows // count, part, 0)


def first_block(x, a, left, right, band, gain, up, down, scale, step):
    rows, chans, lanes = x.shape
    blocks = rows // SLOTS
    return pl.pallas_call(
        functools.partial(first_kernel, step),
        out_shape=[
            jax.ShapeDtypeStruct(x.shape, BF),
            jax.ShapeDtypeStruct((blocks, chans, lanes), BF),
        ],
        in_specs=[VMEM] * 9,
        out_specs=[VMEM] * 2,
        scratch_shapes=[
            pltpu.VMEM((TAPS - 1, SPAN, chans, lanes), BF),
            pltpu.VMEM((blocks, chans, lanes), F32),
        ],
        compiler_params=params(BIG),
        cost_estimate=cost(8),
        name="first_block",
    )(x, a, left, right, band, gain, up, down, scale)


def second_kernel(near, members, count, steps, x_ref, a_ref, g_ref, up_ref, dn_ref, s_ref, fw_ref, *refs):
    if near:
        _, old_ref, halo, y_ref, keep_ref, give_ref, flux = refs
    else:
        left_ref, right_ref, band_ref, y_ref, keep_ref, give_ref, flux, halo, xe = refs
    half = members // 2
    rows, chans, lanes = x_ref.shape
    blocks = halo.shape[0]
    rank = lax.axis_index("member")
    at = jnp.where(rank >= half, rows // count - steps, 0)
    if not near:
        at = rows // count - steps - at
    if near:
        flux[...] = old_ref[...]
    else:
        halo_conv(left_ref, right_ref, band_ref, True, xe, halo)
        blank = jnp.zeros((HALO,) + flux.shape[1:], BF)
        flux[0:HALO] = blank
        flux[rows + HALO : rows + 2 * HALO] = blank
    up_t = transposed(up_ref[1])
    dn_t = halved(dn_ref[1])
    gain = spread(g_ref[1:2], lanes)
    scale = spread(s_ref[1:2], lanes)

    def part(step, carry):
        row0 = (at + step) * count
        slot0 = (at + step) * (count // blocks)
        branch = branch_of(a_ref, row0, count, halo, slot0, gain, up_t, dn_t)
        made = []
        for r in range(count):
            y = x_ref[row0 + r].astype(F32) + scale * branch[:, r * lanes : (r + 1) * lanes]
            made.append(y.astype(BF))
            y_ref[row0 + r] = made[r]
        z = jnp.dot(fw_ref[...], jnp.concatenate(made, axis=1), preferred_element_type=F32)
        f = (0.5 * twice_gelu(z)).astype(BF)
        for r in range(count):
            flux[row0 + HALO + r] = f[:, r * lanes : (r + 1) * lanes]
        return carry

    lax.fori_loop(0, steps, part, 0)
    share = rows // members
    for k in range(half):
        dst = rank ^ (k if near else half + k)
        chunk = flux[pl.ds(dst * share, share + 2 * HALO)]
        if k % 2:
            give_ref[k // 2] = chunk
        else:
            keep_ref[k // 2] = chunk


def second_block(near, members, x, a, weights, others, step, steps):
    rows, chans, lanes = x.shape
    blocks = rows // SLOTS
    flux = weights[-1].shape[0]
    share = rows // members
    chunks = jax.ShapeDtypeStruct((members // 4, share + 2 * HALO, flux, lanes), BF)
    field = jax.ShapeDtypeStruct((rows + 2 * HALO, flux, lanes), BF)
    halo = jax.ShapeDtypeStruct((blocks, chans, lanes), F32)
    args = [x, a, *weights, *others]
    outs = [jax.ShapeDtypeStruct(x.shape, BF), chunks, chunks]
    if near:
        scratch = [pltpu.VMEM(field.shape, BF)]
    else:
        scratch = [pltpu.VMEM((TAPS - 1, SPAN, chans, lanes), BF)]
        outs += [field, halo]
    return pl.pallas_call(
        functools.partial(second_kernel, near, members, step, steps),
        out_shape=outs,
        in_specs=[VMEM] * len(args),
        out_specs=[VMEM] * len(outs),
        scratch_shapes=scratch,
        input_output_aliases={7: 0} if near else {},
        compiler_params=params(BIG),
        cost_estimate=cost(8 * steps * step / rows),
        name="second_block",
    )(*args)


def add_kernel(keep_ref, got_ref, *out_refs):
    for n, ref in enumerate(out_refs):
        k = n + keep_ref.shape[0] - len(out_refs)
        ref[...] = (keep_ref[k].astype(F32) + got_ref[k].astype(F32)).astype(BF)


def add_pairs(keep, got, skip):
    count = keep.shape[0] - skip
    return pl.pallas_call(
        add_kernel,
        out_shape=[jax.ShapeDtypeStruct(keep.shape[1:], BF)] * count,
        in_specs=[VMEM] * 2,
        out_specs=[VMEM] * count,
        compiler_params=params(24),
        name="add_pairs",
    )(keep, got)


def send_xor(value, bits):
    members = lax.axis_size("member")
    return lax.ppermute(value, "member", [(i, i ^ bits) for i in range(members)])


def force_kernel(members, *refs):
    near_refs, flux_refs = refs[:2], refs[2 : members // 2 + 1]
    ocean_ref, land_ref, ice_ref, lift_ref, mid_ref, p_ref, win, sem = refs[members // 2 + 1 :]
    span, flux, lanes = flux_refs[0].shape
    rows = land_ref.shape[0]
    chans = mid_ref.shape[1]
    share = rows // members
    blocks = p_ref.shape[0]
    first = lax.axis_index("member") * share - HALO
    start = jnp.clip(first, 0, rows - span)
    copy = pltpu.make_async_copy(ocean_ref.at[pl.ds(start, span)], win, sem)
    copy.start()
    total = near_refs[0][0].astype(F32) + near_refs[1][0].astype(F32)
    for ref in flux_refs:
        total = total + ref[...].astype(F32)
    low = (total / members).astype(BF)
    lift = jnp.concatenate([transposed(lift_ref[0]), transposed(lift_ref[1])], axis=0)
    terms = jnp.dot(
        lift, jnp.concatenate([low[r] for r in range(span)], axis=1), preferred_element_type=F32
    )
    keep = edge_lanes((chans, lanes)).astype(F32).astype(BF)
    packed = [None] * blocks
    copy.wait()
    for r in range(span):
        row = first + r
        safe = jnp.clip(row, 0, rows - 1)
        sea = (1 - land_ref[pl.ds(safe, 1), :]).astype(F32)
        ice = ice_ref[pl.ds(safe, 1), :].astype(F32)
        at = slice(r * lanes, (r + 1) * lanes)
        forcing = sea * ((1.0 - ice) * terms[:chans, at] + ice * terms[chans:, at])
        mid = win[jnp.clip(row - start, 0, span - 1)].astype(F32) + forcing
        inside = (row >= 0) & (row < rows)
        mid = jnp.where(inside, mid, 0.0).astype(BF)
        mid_ref[r] = mid
        q, slot = r % blocks, r // blocks
        moved = mid * keep
        if slot:
            moved = pltpu.roll(moved, SLOT * slot, 1)
        packed[q] = moved if packed[q] is None else packed[q] + moved
    for q in range(blocks):
        p_ref[q] = packed[q]


def force(members, chunks, ocean, land, ice, lift):
    span, _, lanes = chunks[-1].shape
    rows, chans, _ = ocean.shape
    return pl.pallas_call(
        functools.partial(force_kernel, members),
        out_shape=[
            jax.ShapeDtypeStruct((span, chans, lanes), BF),
            jax.ShapeDtypeStruct((OCEAN_BLOCKS, chans, lanes), BF),
        ],
        in_specs=[VMEM] * len(chunks) + [HBM, VMEM, VMEM, VMEM],
        out_specs=[VMEM] * 2,
        scratch_shapes=[pltpu.VMEM((span, chans, lanes), BF), pltpu.SemaphoreType.DMA(())],
        compiler_params=params(24),
        name="ocean_forcing",
    )(*chunks, ocean, land, ice, lift)


def ocean_kernel(mid_ref, a_ref, left_ref, right_ref, band_ref, land_ref, g_ref, up_ref, dn_ref, s_ref, sw_ref, new_ref, surf_ref, xe, halo):
    share, chans, lanes = new_ref.shape
    halo_conv(left_ref, right_ref, band_ref, False, xe, halo)
    gain = spread(g_ref[...], lanes)
    scale = spread(s_ref[...], lanes)
    branch = branch_of(
        a_ref, 0, share, halo, 0, gain, transposed(up_ref[...]), halved(dn_ref[...])
    )
    first = lax.axis_index("member") * share
    made = []
    for r in range(share):
        sea = (1 - land_ref[pl.ds(first + r, 1), :]).astype(F32)
        y = mid_ref[HALO + r].astype(F32) + scale * branch[:, r * lanes : (r + 1) * lanes]
        made.append((y * sea).astype(BF))
        new_ref[r] = made[r]
    surf = jnp.dot(
        sw_ref[...], jnp.concatenate(made, axis=1), preferred_element_type=F32
    )
    for r in range(share):
        surf_ref[r] = surf[:, r * lanes : (r + 1) * lanes].astype(BF)


def ocean_block(mid, a, left, right, band, land, gain, up, down, scale, surf_weight):
    share, chans, lanes = a.shape
    blocks = left.shape[0]
    return pl.pallas_call(
        ocean_kernel,
        out_shape=[
            jax.ShapeDtypeStruct((share, chans, lanes), BF),
            jax.ShapeDtypeStruct((share, surf_weight.shape[0], lanes), BF),
        ],
        in_specs=[VMEM] * 11,
        out_specs=[VMEM] * 2,
        scratch_shapes=[
            pltpu.VMEM((TAPS - 1, SPAN, chans, lanes), BF),
            pltpu.VMEM((blocks, chans, lanes), F32),
        ],
        compiler_params=params(24),
        name="ocean_block",
    )(mid, a, left, right, band, land, gain[None], up, down, scale[None], surf_weight)


def couple_kernel(count, y_ref, surf_ref, land_ref, bw_ref, o_ref):
    rows, chans, lanes = y_ref.shape
    share = surf_ref.shape[1]
    first = pl.program_id(0) * count
    owner = pl.program_id(0) * (count // share)
    surf = [surf_ref[owner + r // share, r % share] for r in range(count)]
    back = jnp.dot(bw_ref[...], jnp.concatenate(surf, axis=1), preferred_element_type=F32)
    sea = (1 - land_ref[pl.ds(pl.multiple_of(first, SLOT), count), :]).astype(F32)
    for r in range(count):
        out = y_ref[first + r].astype(F32) + sea[r : r + 1] * back[:, r * lanes : (r + 1) * lanes]
        o_ref[r] = out.astype(BF)


def couple(y, surface, land, back_weight, count):
    rows, chans, lanes = y.shape
    return pl.pallas_call(
        functools.partial(couple_kernel, count),
        grid=(rows // count,),
        out_shape=jax.ShapeDtypeStruct(y.shape, BF),
        in_specs=[VMEM] * 4,
        out_specs=pl.BlockSpec((count, chans, lanes), lambda i: (i, 0, 0)),
        compiler_params=params(24),
        name="couple",
    )(y, surface, land, back_weight)


def local(
    atmos,
    ocean,
    land_mask,
    ice_mask,
    atm_kernel,
    atm_gain,
    atm_up,
    atm_down,
    atm_scale,
    flux_weight,
    flux_lift,
    ocn_kernel,
    ocn_gain,
    ocn_up,
    ocn_down,
    ocn_scale,
    surf_weight,
    back_weight,
):
    members = lax.axis_size("member")
    half = members // 2
    state = atmos[0]
    rows = state.shape[0]
    blocks = rows // SLOTS
    big, small = 4 * blocks, 2 * blocks
    atm = (atm_gain, atm_up, atm_down.transpose(0, 2, 1), atm_scale)
    taps = atm_kernel.transpose(1, 2, 0, 3)

    state, packed = pack(state, big)
    left, right = neighbours(packed)
    a, band = convolve(0, state, taps, blocks)
    state, packed = first_block(state, a, left, right, band, *atm, big)

    left, right = neighbours(packed)
    a, band = convolve(1, state, taps, blocks)
    near_steps = (rows // 2 - small) // small
    far_steps = rows // small - near_steps
    weights = (*atm, flux_weight.T)
    partly, keep, give, flux, halo = second_block(
        False, members, state, a, weights, [left, right, band], small, far_steps
    )
    got = send_xor(give, 1)
    state, near_keep, near_give = second_block(
        True, members, state, a, weights, [partly, flux, halo], small, near_steps
    )
    near_got = send_xor(near_give, 1)
    got, near_keep, taps = lax.optimization_barrier((got, near_keep, ocn_kernel))
    sums = add_pairs(keep, got, 0)
    sent = [send_xor(part, half + 2 * k) for k, part in enumerate(sums)]
    sums = add_pairs(near_keep, near_got, 1)
    sent += [send_xor(part, 2 * k + 2) for k, part in enumerate(sums)]
    sent = [near_keep, near_got] + sent
    band = ocean_band(taps)

    mid, packed = force(members, sent, ocean, land_mask, ice_mask, flux_lift)
    left, right = neighbours(packed)
    a = ocean_conv(mid, band)
    ocean_rows, surface = ocean_block(
        mid, a, left, right, band, land_mask, ocn_gain, ocn_up, ocn_down.T, ocn_scale, surf_weight.T
    )
    surface = lax.all_gather(surface, "member")
    out = couple(state, surface, land_mask, back_weight.T, big)
    return (out[None], ocean_rows)


def solution(mesh):
    in_specs = (
        P("member", None, None, "lon"),
        P(None, None, "lon"),
        P(None, "lon"),
        P(None, "lon"),
    ) + (P(),) * 14
    out_specs = (P("member", None, None, "lon"), P("member", None, "lon"))
    return jax.shard_map(local, mesh=mesh, in_specs=in_specs, out_specs=out_specs, check_vma=False)
```

```python
import functools

import jax
import jax.numpy as jnp
from jax import lax
from jax.experimental import pallas as pl
from jax.experimental.pallas import tpu as pltpu
from jax.sharding import PartitionSpec as P

BF = jnp.bfloat16
F32 = jnp.float32
TANH_A = 0.7978845608028654
TANH_B = TANH_A * 0.044715
TAPS = 7
HALO = 3
GROUP = 16
SPAN = 16
OUT = SPAN - TAPS + 1
DEPTH = GROUP * SPAN
SLOT = 8
SLOTS = 16
OCEAN_BLOCKS = 2
BIG = 32
VMEM = pl.BlockSpec(memory_space=pltpu.VMEM)
ANY = pl.BlockSpec(memory_space=pl.ANY)
HBM = pl.BlockSpec(memory_space=pltpu.HBM)


def params(mib):
    return pltpu.CompilerParams(vmem_limit_bytes=mib * 2**20)


def cost(gflop):
    return pl.CostEstimate(flops=int(gflop * 1e9), bytes_accessed=0, transcendentals=0)


def twice_gelu(z):
    return z + z * jnp.tanh(z * (TANH_A + TANH_B * (z * z)))


def transposed(value):
    return value.astype(F32).T.astype(BF)


def halved(value):
    return (0.5 * value.astype(F32)).astype(BF)


def spread(row, lanes):
    return jnp.broadcast_to(row.T, (row.shape[1], lanes))


def edge_lanes(shape):
    lane = lax.broadcasted_iota(jnp.int32, shape, len(shape) - 1)
    return (lane < HALO) | (lane >= shape[-1] - HALO)


def pack_kernel(step, src_ref, p_ref, x_ref, sems):
    rows, chans, lanes = x_ref.shape
    blocks = p_ref.shape[0]
    copies = []
    for n in range(rows // step):
        at = slice(n * step, (n + 1) * step)
        copies.append(pltpu.make_async_copy(src_ref.at[at], x_ref.at[at], sems.at[n]))
        copies[n].start()
    keep = edge_lanes((chans, lanes)).astype(F32).astype(BF)
    for n in range(rows // step):
        copies[n].wait()
        for q in range(blocks):
            total = None if n == 0 else p_ref[q]
            for slot in range(n * step // blocks, (n + 1) * step // blocks):
                moved = x_ref[slot * blocks + q] * keep
                if slot:
                    moved = pltpu.roll(moved, SLOT * slot, 1)
                total = moved if total is None else total + moved
            p_ref[q] = total


def pack(x, step):
    rows, chans, lanes = x.shape
    return pl.pallas_call(
        functools.partial(pack_kernel, step),
        out_shape=jax.ShapeDtypeStruct((rows // SLOTS, chans, lanes), BF),
        in_specs=[HBM],
        out_specs=VMEM,
        scratch_shapes=[pltpu.VMEM(x.shape, BF), pltpu.SemaphoreType.DMA((rows // step,))],
        compiler_params=params(60),
        name="pack_edges",
    )(x)


def neighbours(packed):
    count = lax.axis_size("lon")
    left = lax.ppermute(packed, "lon", [(i, (i + 1) % count) for i in range(count)])
    right = lax.ppermute(packed, "lon", [((i + 1) % count, i) for i in range(count)])
    return left, right


def fill_base(taps, base):
    groups, _, wide = base.shape
    chans = groups * GROUP
    t = lax.broadcasted_iota(jnp.int32, (TAPS, wide), 0)
    n = lax.broadcasted_iota(jnp.int32, (TAPS, wide), 1)
    total = jnp.zeros((chans, wide), F32)
    for i in range(TAPS):
        put = ((t == n // DEPTH) & ((n % DEPTH) // GROUP == i)).astype(F32).astype(BF)
        total = total + jnp.dot(taps(i).T.astype(BF), put, preferred_element_type=F32)
    r = lax.broadcasted_iota(jnp.int32, (chans, wide), 0)
    c = lax.broadcasted_iota(jnp.int32, (chans, wide), 1)
    total = jnp.where(r % GROUP == c % GROUP, total, 0.0)
    for g in range(groups):
        base[g] = total[GROUP * g : GROUP * (g + 1)]


def fill_band(base, g, band):
    for j in range(TAPS):
        one = base[g, :, j * DEPTH : (j + 1) * DEPTH]
        for r in range(OUT):
            moved = pltpu.roll(one, GROUP * r, 1) if r else one
            band[GROUP * r : GROUP * (r + 1), j * DEPTH : (j + 1) * DEPTH] = moved.astype(BF)


def fill_shifts(x, pad, xj):
    count, _, lanes = x.shape
    lane = lax.broadcasted_iota(jnp.int32, (GROUP, lanes), 1)
    for j in range(TAPS):
        d = j - HALO
        if d:
            keep = ((lane < lanes - d) if d > 0 else (lane >= -d)).astype(F32).astype(BF)
            xj[j, pad : pad + count] = pltpu.roll(x, (-d) % lanes, 2) * keep[None]
        else:
            xj[j, pad : pad + count] = x


def clear_pads(pad, count, xj):
    tall, _, lanes = xj.shape[1:]
    for j in range(TAPS):
        if pad:
            xj[j, :pad] = jnp.zeros((pad, GROUP, lanes), BF)
        if tall > pad + count:
            xj[j, pad + count :] = jnp.zeros((tall - pad - count, GROUP, lanes), BF)


def apply_band(band, xj, a_ref):
    rows, _, lanes = a_ref.shape
    starts = [min(OUT * i, max(rows - OUT, 0)) for i in range(-(-rows // OUT))]
    field = jnp.concatenate(
        [
            jnp.concatenate([xj[j, s : s + SPAN].reshape(DEPTH, lanes) for j in range(TAPS)], axis=0)
            for s in starts
        ],
        axis=1,
    )
    out = jnp.dot(band, field, preferred_element_type=F32)
    take = min(OUT, rows)
    for n, s in enumerate(starts):
        part = out[: take * GROUP, n * lanes : (n + 1) * lanes]
        a_ref[s : s + take] = part.reshape(take, GROUP, lanes)


def conv_kernel(layer, x_ref, k_ref, a_ref, band_ref, base, even_xj, odd_xj, even_band, odd_band):
    rows, chans, lanes = x_ref.shape
    groups = chans // GROUP
    fill_base(lambda i: k_ref[i, :, layer, :], base)
    clear_pads(HALO, rows, even_xj)
    clear_pads(HALO, rows, odd_xj)

    def at(g):
        return pl.ds(pl.multiple_of(GROUP * g, GROUP), GROUP)

    def prepare(g, xj, band):
        fill_band(base, g, band)
        band_ref[g] = band[: band_ref.shape[1]]
        fill_shifts(x_ref[:, at(g), :], HALO, xj)

    prepare(0, even_xj, even_band)

    def pair(i, carry):
        prepare(2 * i + 1, odd_xj, odd_band)
        apply_band(even_band[...], even_xj, a_ref.at[:, at(2 * i), :])
        prepare(jnp.minimum(2 * i + 2, groups - 1), even_xj, even_band)
        apply_band(odd_band[...], odd_xj, a_ref.at[:, at(2 * i + 1), :])
        return carry

    lax.fori_loop(0, groups // 2, pair, 0)


def convolve(layer, x, taps, blocks):
    rows, chans, lanes = x.shape
    groups = chans // GROUP
    wide = TAPS * DEPTH
    return pl.pallas_call(
        functools.partial(conv_kernel, layer),
        out_shape=[
            jax.ShapeDtypeStruct((rows, chans, lanes), F32),
            jax.ShapeDtypeStruct((groups, blocks * GROUP, wide), BF),
        ],
        in_specs=[VMEM, VMEM],
        out_specs=[VMEM, VMEM],
        scratch_shapes=[
            pltpu.VMEM((groups, GROUP, wide), F32),
        ]
        + [pltpu.VMEM((TAPS, rows + 2 * HALO, GROUP, lanes), BF)] * 2
        + [pltpu.VMEM((GROUP * OUT, wide), BF)] * 2,
        compiler_params=params(BIG),
        cost_estimate=cost(8),
        name="conv",
    )(x, taps)


def band_kernel(k_ref, _, band_ref, base):
    fill_base(lambda i: k_ref[i], base)
    for g in range(base.shape[0]):
        fill_band(base, g, band_ref.at[g])


def ocean_band(taps, after):
    groups = taps.shape[2] // GROUP
    wide = TAPS * DEPTH
    return pl.pallas_call(
        band_kernel,
        out_shape=jax.ShapeDtypeStruct((groups, GROUP * OUT, wide), BF),
        in_specs=[VMEM, ANY],
        out_specs=VMEM,
        scratch_shapes=[pltpu.VMEM((groups, GROUP, wide), F32)],
        compiler_params=params(24),
        cost_estimate=cost(3),
        name="ocean_band",
    )(taps, after)


def ocean_conv_kernel(x_ref, band_ref, a_ref, xj):
    count, chans, lanes = x_ref.shape
    for g in range(chans // GROUP):
        at = slice(GROUP * g, GROUP * (g + 1))
        clear_pads(0, count, xj.at[g])
        fill_shifts(x_ref[:, at, :], 0, xj.at[g])
        apply_band(band_ref[g], xj.at[g], a_ref.at[:, at, :])


def ocean_conv(x, band):
    count, chans, lanes = x.shape
    return pl.pallas_call(
        ocean_conv_kernel,
        out_shape=jax.ShapeDtypeStruct((count - 2 * HALO, chans, lanes), F32),
        in_specs=[VMEM, VMEM],
        out_specs=VMEM,
        scratch_shapes=[pltpu.VMEM((chans // GROUP, TAPS, max(count, SPAN), GROUP, lanes), BF)],
        compiler_params=params(24),
        cost_estimate=cost(2),
        name="ocean_conv",
    )(x, band)


def halo_matrix(lanes):
    side = [j for j in range(TAPS) if j != HALO]
    shape = (2 * lanes, len(side) * lanes)
    src = lax.broadcasted_iota(jnp.int32, shape, 0)
    dst = lax.broadcasted_iota(jnp.int32, shape, 1)
    hit = jnp.zeros(shape, jnp.bool_)
    to = dst % lanes
    for a, j in enumerate(side):
        d = j - HALO
        here = (dst >= a * lanes) & (dst < (a + 1) * lanes)
        from_ = (to + d + lanes) % lanes
        if d > 0:
            ok = (src == from_) & (src % SLOT < HALO) & (to % SLOT >= SLOT - HALO)
        else:
            ok = (src == from_ + lanes) & (src % SLOT >= SLOT - HALO) & (to % SLOT < HALO)
        hit = hit | (here & ok)
    return hit.astype(F32).astype(BF)


def halo_conv(left, right, band, wrapped, xe, halo):
    blocks, chans, lanes = halo.shape
    wide = TAPS * DEPTH
    both = [jnp.concatenate([right[q], left[q]], axis=1) for q in range(blocks)]
    lane = lax.broadcasted_iota(jnp.int32, (chans, lanes), 1)
    slot = (lane + HALO) // SLOT % SLOTS

    def turned(value, shift, drop):
        parts = [pltpu.roll(value[:, n * lanes : (n + 1) * lanes], shift, 1) for n in range(2)]
        if drop >= 0:
            keep = (slot != drop).astype(F32).astype(BF)
            parts = [part * keep for part in parts]
        return jnp.concatenate(parts, axis=1)

    if wrapped:
        tall = (
            [turned(both[q], SLOT, 0) for q in range(blocks - HALO, blocks)]
            + both
            + [turned(both[q], lanes - SLOT, SLOTS - 1) for q in range(HALO)]
        )
    else:
        tall = both + [
            turned(both[e % blocks], lanes - SLOT * (e // blocks), -1)
            for e in range(blocks, blocks + 2 * HALO)
        ]
    field = jnp.concatenate(tall, axis=0)
    moved = jnp.dot(field, halo_matrix(lanes), preferred_element_type=F32)
    count = len(tall)
    for a in range(TAPS - 1):
        part = moved[:, a * lanes : (a + 1) * lanes].astype(BF)
        xe[a, :count] = part.reshape(count, chans, lanes)
        xe[a, count:] = jnp.zeros((SPAN - count, chans, lanes), BF)
    low = HALO * DEPTH
    for g in range(chans // GROUP):
        at = slice(GROUP * g, GROUP * (g + 1))
        rhs = jnp.concatenate([xe[a, :, at, :].reshape(DEPTH, lanes) for a in range(TAPS - 1)], axis=0)
        tops = slice(0, blocks * GROUP)
        lhs = jnp.concatenate([band[g, tops, :low], band[g, tops, low + DEPTH : wide]], axis=1)
        out = jnp.dot(lhs, rhs, preferred_element_type=F32)
        halo[:, at, :] = out.reshape(blocks, GROUP, lanes)


def norm_rows(a_ref, row0, count, halo, gain, out):
    _, chans, lanes = a_ref.shape
    blocks = halo.shape[0]
    edge = edge_lanes((chans, lanes))
    for r in range(count):
        q, slot = (row0 + r) % blocks, (row0 + r) // blocks
        extra = pltpu.roll(halo[q], lanes - SLOT * slot, 1) if slot else halo[q]
        a = a_ref[row0 + r] + jnp.where(edge, extra, 0.0)
        center = a - jnp.mean(a, axis=0, keepdims=True)
        var = jnp.mean(center * center, axis=0, keepdims=True)
        normed = (center * lax.rsqrt(var + 1e-06) * gain).astype(BF)
        out[:, r * lanes : (r + 1) * lanes] = normed


def branch_of(normed, up_t, down_t):
    z = jnp.dot(up_t, normed, preferred_element_type=F32)
    h = twice_gelu(z.astype(BF))
    return jnp.dot(down_t, h, preferred_element_type=F32)


def atmos_kernel(layer, members, count, *refs):
    x_ref, a_ref, left_ref, right_ref, band_ref, g_ref, up_ref, dn_ref, s_ref = refs[:9]
    if layer == 0:
        y_ref, p_ref = refs[9:11]
    else:
        fw_ref, y_ref, keep_ref, give_ref, flux = refs[9:14]
    xe, halo, even, odd = refs[-4:]
    rows, chans, lanes = x_ref.shape
    blocks = halo.shape[0]
    halo_conv(left_ref, right_ref, band_ref, True, xe, halo)
    up_t = transposed(up_ref[layer])
    dn_t = halved(dn_ref[layer])
    gain = spread(g_ref[layer : layer + 1], lanes)
    scale = spread(s_ref[layer : layer + 1], lanes)
    keep = edge_lanes((chans, lanes)).astype(F32).astype(BF)
    packed = [None] * blocks
    if layer == 1:
        blank = jnp.zeros((HALO,) + flux.shape[1:], BF)
        flux[0:HALO] = blank
        flux[rows + HALO : rows + 2 * HALO] = blank
    norm_rows(a_ref, 0, count, halo, gain, even)
    for step in range(rows // count):
        row0 = step * count
        now, later = (even, odd) if step % 2 == 0 else (odd, even)
        if row0 + count < rows:
            norm_rows(a_ref, row0 + count, count, halo, gain, later)
        branch = branch_of(now[...], up_t, dn_t)
        made = []
        for r in range(count):
            y = x_ref[row0 + r].astype(F32) + scale * branch[:, r * lanes : (r + 1) * lanes]
            made.append(y.astype(BF))
            y_ref[row0 + r] = made[r]
        if layer == 0:
            for r in range(count):
                q, slot = (row0 + r) % blocks, (row0 + r) // blocks
                moved = made[r] * keep
                if slot:
                    moved = pltpu.roll(moved, SLOT * slot, 1)
                packed[q] = moved if packed[q] is None else packed[q] + moved
            if row0 % (4 * count) == 3 * count or row0 + count == rows:
                for q in range(blocks):
                    if row0 < 4 * count:
                        p_ref[q] = packed[q]
                    else:
                        p_ref[q] = p_ref[q] + packed[q]
                packed = [None] * blocks
        else:
            z = jnp.dot(fw_ref[...], jnp.concatenate(made, axis=1), preferred_element_type=F32)
            f = (0.5 * twice_gelu(z)).astype(BF)
            for r in range(count):
                flux[row0 + HALO + r] = f[:, r * lanes : (r + 1) * lanes]
    if layer == 1:
        rank = lax.axis_index("member")
        share = rows // members
        for k in range(members):
            chunk = flux[pl.ds((rank ^ k) * share, share + 2 * HALO)]
            if k % 2:
                give_ref[k // 2] = chunk
            else:
                keep_ref[k // 2] = chunk


def atmos_block(layer, members, x, a, edges, band, weights, count):
    rows, chans, lanes = x.shape
    blocks = rows // SLOTS
    args = [x, a, *edges, band, *weights]
    outs = [jax.ShapeDtypeStruct(x.shape, BF)]
    scratch = []
    if layer == 0:
        outs.append(jax.ShapeDtypeStruct((blocks, chans, lanes), BF))
    else:
        flux = weights[-1].shape[0]
        share = rows // members
        outs += [jax.ShapeDtypeStruct((members // 2, share + 2 * HALO, flux, lanes), BF)] * 2
        scratch.append(pltpu.VMEM((rows + 2 * HALO, flux, lanes), BF))
    return pl.pallas_call(
        functools.partial(atmos_kernel, layer, members, count),
        out_shape=outs,
        in_specs=[VMEM] * len(args),
        out_specs=[VMEM] * len(outs),
        scratch_shapes=scratch
        + [
            pltpu.VMEM((TAPS - 1, SPAN, chans, lanes), BF),
            pltpu.VMEM((blocks, chans, lanes), F32),
            pltpu.VMEM((chans, count * lanes), BF),
            pltpu.VMEM((chans, count * lanes), BF),
        ],
        compiler_params=params(BIG),
        cost_estimate=cost(8),
        name="atmos_block",
    )(*args)


def add_kernel(keep_ref, got_ref, *out_refs):
    for n, ref in enumerate(out_refs):
        k = n + keep_ref.shape[0] - len(out_refs)
        ref[...] = (keep_ref[k].astype(F32) + got_ref[k].astype(F32)).astype(BF)


def add_pairs(keep, got, skip):
    count = keep.shape[0] - skip
    return pl.pallas_call(
        add_kernel,
        out_shape=[jax.ShapeDtypeStruct(keep.shape[1:], BF)] * count,
        in_specs=[VMEM] * 2,
        out_specs=[VMEM] * count,
        compiler_params=params(24),
        name="add_pairs",
    )(keep, got)


def send_xor(value, bits):
    members = lax.axis_size("member")
    return lax.ppermute(value, "member", [(i, i ^ bits) for i in range(members)])


def force_kernel(members, *refs):
    near_refs, flux_refs = refs[:2], refs[2 : members // 2 + 1]
    ocean_ref, land_ref, ice_ref, lift_ref, mid_ref, p_ref, win, sem = refs[members // 2 + 1 :]
    span, flux, lanes = flux_refs[0].shape
    rows = land_ref.shape[0]
    chans = mid_ref.shape[1]
    share = rows // members
    blocks = p_ref.shape[0]
    first = lax.axis_index("member") * share - HALO
    start = jnp.clip(first, 0, rows - span)
    copy = pltpu.make_async_copy(ocean_ref.at[pl.ds(start, span)], win, sem)
    copy.start()
    total = near_refs[0][0].astype(F32) + near_refs[1][0].astype(F32)
    for ref in flux_refs:
        total = total + ref[...].astype(F32)
    low = (total / members).astype(BF)
    lift = jnp.concatenate([transposed(lift_ref[0]), transposed(lift_ref[1])], axis=0)
    terms = jnp.dot(
        lift, jnp.concatenate([low[r] for r in range(span)], axis=1), preferred_element_type=F32
    )
    keep = edge_lanes((chans, lanes)).astype(F32).astype(BF)
    packed = [None] * blocks
    copy.wait()
    for r in range(span):
        row = first + r
        safe = jnp.clip(row, 0, rows - 1)
        sea = (1 - land_ref[pl.ds(safe, 1), :]).astype(F32)
        ice = ice_ref[pl.ds(safe, 1), :].astype(F32)
        at = slice(r * lanes, (r + 1) * lanes)
        forcing = sea * ((1.0 - ice) * terms[:chans, at] + ice * terms[chans:, at])
        mid = win[jnp.clip(row - start, 0, span - 1)].astype(F32) + forcing
        inside = (row >= 0) & (row < rows)
        mid = jnp.where(inside, mid, 0.0).astype(BF)
        mid_ref[r] = mid
        q, slot = r % blocks, r // blocks
        moved = mid * keep
        if slot:
            moved = pltpu.roll(moved, SLOT * slot, 1)
        packed[q] = moved if packed[q] is None else packed[q] + moved
    for q in range(blocks):
        p_ref[q] = packed[q]


def force(members, chunks, ocean, land, ice, lift):
    span, _, lanes = chunks[-1].shape
    rows, chans, _ = ocean.shape
    return pl.pallas_call(
        functools.partial(force_kernel, members),
        out_shape=[
            jax.ShapeDtypeStruct((span, chans, lanes), BF),
            jax.ShapeDtypeStruct((OCEAN_BLOCKS, chans, lanes), BF),
        ],
        in_specs=[VMEM] * len(chunks) + [HBM, VMEM, VMEM, VMEM],
        out_specs=[VMEM] * 2,
        scratch_shapes=[pltpu.VMEM((span, chans, lanes), BF), pltpu.SemaphoreType.DMA(())],
        compiler_params=params(24),
        name="ocean_forcing",
    )(*chunks, ocean, land, ice, lift)


def ocean_kernel(mid_ref, a_ref, left_ref, right_ref, band_ref, land_ref, g_ref, up_ref, dn_ref, s_ref, sw_ref, new_ref, surf_ref, xe, halo, normed):
    share, chans, lanes = new_ref.shape
    halo_conv(left_ref, right_ref, band_ref, False, xe, halo)
    gain = spread(g_ref[...], lanes)
    scale = spread(s_ref[...], lanes)
    norm_rows(a_ref, 0, share, halo, gain, normed)
    branch = branch_of(normed[...], transposed(up_ref[...]), halved(dn_ref[...]))
    first = lax.axis_index("member") * share
    made = []
    for r in range(share):
        sea = (1 - land_ref[pl.ds(first + r, 1), :]).astype(F32)
        y = mid_ref[HALO + r].astype(F32) + scale * branch[:, r * lanes : (r + 1) * lanes]
        made.append((y * sea).astype(BF))
        new_ref[r] = made[r]
    surf = jnp.dot(
        sw_ref[...], jnp.concatenate(made, axis=1), preferred_element_type=F32
    )
    for r in range(share):
        surf_ref[r] = surf[:, r * lanes : (r + 1) * lanes].astype(BF)


def ocean_block(mid, a, left, right, band, land, gain, up, down, scale, surf_weight):
    share, chans, lanes = a.shape
    blocks = left.shape[0]
    return pl.pallas_call(
        ocean_kernel,
        out_shape=[
            jax.ShapeDtypeStruct((share, chans, lanes), BF),
            jax.ShapeDtypeStruct((share, surf_weight.shape[0], lanes), BF),
        ],
        in_specs=[VMEM] * 11,
        out_specs=[VMEM] * 2,
        scratch_shapes=[
            pltpu.VMEM((TAPS - 1, SPAN, chans, lanes), BF),
            pltpu.VMEM((blocks, chans, lanes), F32),
            pltpu.VMEM((chans, share * lanes), BF),
        ],
        compiler_params=params(24),
        name="ocean_block",
    )(mid, a, left, right, band, land, gain[None], up, down, scale[None], surf_weight)


def pair_kernel(own_ref, got_ref, out_ref):
    out_ref[0] = own_ref[...]
    out_ref[1] = got_ref[...]


def make_pair(own, got):
    return pl.pallas_call(
        pair_kernel,
        out_shape=jax.ShapeDtypeStruct((2,) + own.shape, BF),
        in_specs=[VMEM] * 2,
        out_specs=VMEM,
        compiler_params=params(24),
        name="surface_pair",
    )(own, got)


def couple_kernel(y_ref, land_ref, bw_ref, *refs):
    pair_refs, o_ref = refs[:-1], refs[-1]
    chans, lanes = y_ref.shape[1:]
    share = pair_refs[0].shape[1]
    rank = lax.axis_index("member")
    pair = pl.program_id(0)
    parity = rank % 2
    mine = pair ^ (rank // 2)
    surf = [None] * (2 * share)
    for side in range(2):
        for r in range(share):
            value = pair_refs[0][side ^ parity, r]
            for k, ref in enumerate(pair_refs[1:]):
                value = jnp.where(mine == k + 1, ref[side ^ parity, r], value)
            surf[side * share + r] = value
    back = jnp.dot(bw_ref[...], jnp.concatenate(surf, axis=1), preferred_element_type=F32)
    first = pair * 2 * share
    for r in range(2 * share):
        sea = (1 - land_ref[pl.ds(first + r, 1), :]).astype(F32)
        out = y_ref[first + r].astype(F32) + sea * back[:, r * lanes : (r + 1) * lanes]
        o_ref[r] = out.astype(BF)


def couple(y, land, back_weight, pairs):
    rows, chans, lanes = y.shape
    count = 2 * pairs[0].shape[1]
    return pl.pallas_call(
        couple_kernel,
        grid=(rows // count,),
        out_shape=jax.ShapeDtypeStruct(y.shape, BF),
        in_specs=[VMEM] * (3 + len(pairs)),
        out_specs=pl.BlockSpec((count, chans, lanes), lambda i: (i, 0, 0)),
        compiler_params=params(24),
        name="couple",
    )(y, land, back_weight, *pairs)


def local(
    atmos,
    ocean,
    land_mask,
    ice_mask,
    atm_kernel,
    atm_gain,
    atm_up,
    atm_down,
    atm_scale,
    flux_weight,
    flux_lift,
    ocn_kernel,
    ocn_gain,
    ocn_up,
    ocn_down,
    ocn_scale,
    surf_weight,
    back_weight,
):
    members = lax.axis_size("member")
    half = members // 2
    state = atmos[0]
    rows = state.shape[0]
    blocks = rows // SLOTS
    big, small = 4 * blocks, 2 * blocks
    atm = (atm_gain, atm_up, atm_down.transpose(0, 2, 1), atm_scale)
    taps = atm_kernel.transpose(1, 2, 0, 3)

    edges = neighbours(pack(state, big))
    a, band = convolve(0, state, taps, blocks)
    state, packed = atmos_block(0, members, state, a, edges, band, atm, small)

    edges = neighbours(packed)
    a, band = convolve(1, state, taps, blocks)
    state, keep, give = atmos_block(
        1, members, state, a, edges, band, (*atm, flux_weight.T), small
    )
    got = send_xor(give, 1)
    sums = add_pairs(keep, got, 1)
    sent = [send_xor(sums[k - 1], 2 * k) for k in range(half - 1, 0, -1)]
    band = ocean_band(ocn_kernel, sums[0])
    sent = [keep, got] + sent

    mid, packed = force(members, sent, ocean, land_mask, ice_mask, flux_lift)
    left, right = neighbours(packed)
    a = ocean_conv(mid, band)
    ocean_rows, surface = ocean_block(
        mid, a, left, right, band, land_mask, ocn_gain, ocn_up, ocn_down.T, ocn_scale, surf_weight.T
    )
    own = make_pair(surface, send_xor(surface, 1))
    pairs = [own] + [send_xor(own, 2 * k) for k in range(1, half)]
    out = couple(state, land_mask, back_weight.T, pairs)
    return (out[None], ocean_rows)


def solution(mesh):
    in_specs = (
        P("member", None, None, "lon"),
        P(None, None, "lon"),
        P(None, "lon"),
        P(None, "lon"),
    ) + (P(),) * 14
    out_specs = (P("member", None, None, "lon"), P("member", None, "lon"))
    return jax.shard_map(local, mesh=mesh, in_specs=in_specs, out_specs=out_specs, check_vma=False)
```

```python
import functools

import jax
import jax.numpy as jnp
from jax import lax
from jax.experimental import pallas as pl
from jax.experimental.pallas import tpu as pltpu
from jax.sharding import PartitionSpec as P

BF = jnp.bfloat16
F32 = jnp.float32
TANH_A = 0.7978845608028654
TANH_B = TANH_A * 0.044715
TAPS = 7
HALO = 3
GROUP = 16
SPAN = 16
OUT = SPAN - TAPS + 1
DEPTH = GROUP * SPAN
SLOT = 8
SLOTS = 16
OCEAN_BLOCKS = 2
BIG = 32
VMEM = pl.BlockSpec(memory_space=pltpu.VMEM)
ANY = pl.BlockSpec(memory_space=pl.ANY)
HBM = pl.BlockSpec(memory_space=pltpu.HBM)


def params(mib):
    return pltpu.CompilerParams(vmem_limit_bytes=mib * 2**20)


def cost(gflop):
    return pl.CostEstimate(flops=int(gflop * 1e9), bytes_accessed=0, transcendentals=0)


def twice_gelu(z):
    return z + z * jnp.tanh(z * (TANH_A + TANH_B * (z * z)))


def transposed(value):
    return value.astype(F32).T.astype(BF)


def halved(value):
    return (0.5 * value.astype(F32)).astype(BF)


def spread(row, lanes):
    return jnp.broadcast_to(row.T, (row.shape[1], lanes))


def edge_lanes(shape):
    lane = lax.broadcasted_iota(jnp.int32, shape, len(shape) - 1)
    return (lane < HALO) | (lane >= shape[-1] - HALO)


def pack_kernel(step, src_ref, p_ref, x_ref, sems):
    rows, chans, lanes = x_ref.shape
    blocks = p_ref.shape[0]
    copies = []
    for n in range(rows // step):
        at = slice(n * step, (n + 1) * step)
        copies.append(pltpu.make_async_copy(src_ref.at[at], x_ref.at[at], sems.at[n]))
        copies[n].start()
    keep = edge_lanes((chans, lanes)).astype(F32).astype(BF)
    for n in range(rows // step):
        copies[n].wait()
        for q in range(blocks):
            total = None if n == 0 else p_ref[q]
            for slot in range(n * step // blocks, (n + 1) * step // blocks):
                moved = x_ref[slot * blocks + q] * keep
                if slot:
                    moved = pltpu.roll(moved, SLOT * slot, 1)
                total = moved if total is None else total + moved
            p_ref[q] = total


def pack(x, step):
    rows, chans, lanes = x.shape
    return pl.pallas_call(
        functools.partial(pack_kernel, step),
        out_shape=jax.ShapeDtypeStruct((rows // SLOTS, chans, lanes), BF),
        in_specs=[HBM],
        out_specs=VMEM,
        scratch_shapes=[pltpu.VMEM(x.shape, BF), pltpu.SemaphoreType.DMA((rows // step,))],
        compiler_params=params(60),
        name="pack_edges",
    )(x)


def neighbours(packed):
    count = lax.axis_size("lon")
    left = lax.ppermute(packed, "lon", [(i, (i + 1) % count) for i in range(count)])
    right = lax.ppermute(packed, "lon", [((i + 1) % count, i) for i in range(count)])
    return left, right


def fill_base(taps, base):
    groups, _, wide = base.shape
    chans = groups * GROUP
    tall = TAPS * SLOT
    t = lax.broadcasted_iota(jnp.int32, (tall, wide), 0)
    n = lax.broadcasted_iota(jnp.int32, (tall, wide), 1)
    hit = (t % SLOT == n // DEPTH) & (t // SLOT == (n % DEPTH) // GROUP)
    columns = []
    for i in range(TAPS):
        columns.append(taps(i).T)
        columns.append(jnp.zeros((chans, SLOT - TAPS), F32))
    columns = jnp.concatenate(columns, axis=1).astype(BF)
    total = jnp.dot(columns, hit.astype(F32).astype(BF), preferred_element_type=F32)
    r = lax.broadcasted_iota(jnp.int32, (GROUP, wide), 0)
    c = lax.broadcasted_iota(jnp.int32, (GROUP, wide), 1)
    same = r == c % GROUP
    for g in range(groups):
        base[g] = jnp.where(same, total[GROUP * g : GROUP * (g + 1)], 0.0)


def fill_band(base, g, band):
    for j in range(TAPS):
        one = base[g, :, j * DEPTH : (j + 1) * DEPTH]
        for r in range(OUT):
            moved = pltpu.roll(one, GROUP * r, 1) if r else one
            band[GROUP * r : GROUP * (r + 1), j * DEPTH : (j + 1) * DEPTH] = moved.astype(BF)


def fill_shifts(x, pad, xj):
    count, _, lanes = x.shape
    lane = lax.broadcasted_iota(jnp.int32, (GROUP, lanes), 1)
    for j in range(TAPS):
        d = j - HALO
        if d:
            keep = ((lane < lanes - d) if d > 0 else (lane >= -d)).astype(F32).astype(BF)
            xj[j, pad : pad + count] = pltpu.roll(x, (-d) % lanes, 2) * keep[None]
        else:
            xj[j, pad : pad + count] = x


def clear_pads(pad, count, xj):
    tall, _, lanes = xj.shape[1:]
    for j in range(TAPS):
        if pad:
            xj[j, :pad] = jnp.zeros((pad, GROUP, lanes), BF)
        if tall > pad + count:
            xj[j, pad + count :] = jnp.zeros((tall - pad - count, GROUP, lanes), BF)


def apply_band(band, xj, a_ref):
    rows, _, lanes = a_ref.shape
    starts = [min(OUT * i, max(rows - OUT, 0)) for i in range(-(-rows // OUT))]
    field = jnp.concatenate(
        [
            jnp.concatenate([xj[j, s : s + SPAN].reshape(DEPTH, lanes) for j in range(TAPS)], axis=0)
            for s in starts
        ],
        axis=1,
    )
    out = jnp.dot(band, field, preferred_element_type=F32)
    take = min(OUT, rows)
    for n, s in enumerate(starts):
        part = out[: take * GROUP, n * lanes : (n + 1) * lanes]
        a_ref[s : s + take] = part.reshape(take, GROUP, lanes)


def conv_kernel(layer, x_ref, k_ref, a_ref, band_ref, base, even_xj, odd_xj, even_band, odd_band):
    rows, chans, lanes = x_ref.shape
    groups = chans // GROUP
    fill_base(lambda i: k_ref[i, :, layer, :], base)
    clear_pads(HALO, rows, even_xj)
    clear_pads(HALO, rows, odd_xj)

    def at(g):
        return pl.ds(pl.multiple_of(GROUP * g, GROUP), GROUP)

    def prepare(g, xj, band):
        fill_band(base, g, band)
        band_ref[g] = band[: band_ref.shape[1]]
        fill_shifts(x_ref[:, at(g), :], HALO, xj)

    prepare(0, even_xj, even_band)

    def pair(i, carry):
        prepare(2 * i + 1, odd_xj, odd_band)
        apply_band(even_band[...], even_xj, a_ref.at[:, at(2 * i), :])
        prepare(jnp.minimum(2 * i + 2, groups - 1), even_xj, even_band)
        apply_band(odd_band[...], odd_xj, a_ref.at[:, at(2 * i + 1), :])
        return carry

    lax.fori_loop(0, groups // 2, pair, 0)


def convolve(layer, x, taps, blocks):
    rows, chans, lanes = x.shape
    groups = chans // GROUP
    wide = TAPS * DEPTH
    return pl.pallas_call(
        functools.partial(conv_kernel, layer),
        out_shape=[
            jax.ShapeDtypeStruct((rows, chans, lanes), F32),
            jax.ShapeDtypeStruct((groups, blocks * GROUP, wide), BF),
        ],
        in_specs=[VMEM, VMEM],
        out_specs=[VMEM, VMEM],
        scratch_shapes=[
            pltpu.VMEM((groups, GROUP, wide), F32),
        ]
        + [pltpu.VMEM((TAPS, rows + 2 * HALO, GROUP, lanes), BF)] * 2
        + [pltpu.VMEM((GROUP * OUT, wide), BF)] * 2,
        compiler_params=params(BIG),
        cost_estimate=cost(8),
        name="conv",
    )(x, taps)


def prepare_kernel(k_ref, g_ref, up_ref, s_ref, _, band_ref, mat_ref, upt_ref, gain_ref, scale_ref, base):
    lanes = gain_ref.shape[1]
    mat_ref[...] = halo_matrix(lanes)
    upt_ref[...] = transposed(up_ref[...])
    gain_ref[...] = spread(g_ref[...], lanes)
    scale_ref[...] = spread(s_ref[...], lanes)
    fill_base(lambda i: k_ref[i], base)
    for g in range(base.shape[0]):
        fill_band(base, g, band_ref.at[g])


def prepare_ocean(taps, gain, up, scale, after):
    chans, hid = up.shape
    lanes = after.shape[-1]
    groups = chans // GROUP
    wide = TAPS * DEPTH
    return pl.pallas_call(
        prepare_kernel,
        out_shape=[
            jax.ShapeDtypeStruct((groups, GROUP * OUT, wide), BF),
            jax.ShapeDtypeStruct((2 * lanes, (TAPS - 1) * lanes), BF),
            jax.ShapeDtypeStruct((hid, chans), BF),
            jax.ShapeDtypeStruct((chans, lanes), F32),
            jax.ShapeDtypeStruct((chans, lanes), F32),
        ],
        in_specs=[VMEM] * 4 + [ANY],
        out_specs=[VMEM] * 5,
        scratch_shapes=[pltpu.VMEM((groups, GROUP, wide), F32)],
        compiler_params=params(24),
        cost_estimate=cost(3),
        name="prepare_ocean",
    )(taps, gain[None], up, scale[None], after)


def ocean_conv_kernel(x_ref, band_ref, a_ref, xj):
    count, chans, lanes = x_ref.shape
    for g in range(chans // GROUP):
        at = slice(GROUP * g, GROUP * (g + 1))
        clear_pads(0, count, xj.at[g])
        fill_shifts(x_ref[:, at, :], 0, xj.at[g])
        apply_band(band_ref[g], xj.at[g], a_ref.at[:, at, :])


def ocean_conv(x, band):
    count, chans, lanes = x.shape
    return pl.pallas_call(
        ocean_conv_kernel,
        out_shape=jax.ShapeDtypeStruct((count - 2 * HALO, chans, lanes), F32),
        in_specs=[VMEM, VMEM],
        out_specs=VMEM,
        scratch_shapes=[pltpu.VMEM((chans // GROUP, TAPS, max(count, SPAN), GROUP, lanes), BF)],
        compiler_params=params(24),
        cost_estimate=cost(2),
        name="ocean_conv",
    )(x, band)


def halo_matrix(lanes):
    shape = (lanes, lanes)
    src = lax.broadcasted_iota(jnp.int32, shape, 0)
    dst = lax.broadcasted_iota(jnp.int32, shape, 1)
    ahead = (src - dst + lanes) % lanes
    right = (src % SLOT < HALO) & (dst % SLOT >= SLOT - HALO)
    left = (src % SLOT >= SLOT - HALO) & (dst % SLOT < HALO)
    right = jnp.where(right, ahead, -1)
    left = jnp.where(left, ahead, -1)
    none = jnp.zeros(shape, BF)
    upper, lower = [], []
    for j in range(TAPS):
        d = j - HALO
        if d > 0:
            upper.append((right == d).astype(F32).astype(BF))
            lower.append(none)
        elif d < 0:
            upper.append(none)
            lower.append((left == lanes + d).astype(F32).astype(BF))
    return jnp.concatenate(
        [jnp.concatenate(upper, axis=1), jnp.concatenate(lower, axis=1)], axis=0
    )


def halo_conv(left, right, band, wrapped, matrix, xe, halo):
    blocks, chans, lanes = halo.shape
    wide = TAPS * DEPTH
    both = [jnp.concatenate([right[q], left[q]], axis=1) for q in range(blocks)]
    lane = lax.broadcasted_iota(jnp.int32, (chans, lanes), 1)
    slot = (lane + HALO) // SLOT % SLOTS

    def turned(value, shift, drop):
        parts = [pltpu.roll(value[:, n * lanes : (n + 1) * lanes], shift, 1) for n in range(2)]
        if drop >= 0:
            keep = (slot != drop).astype(F32).astype(BF)
            parts = [part * keep for part in parts]
        return jnp.concatenate(parts, axis=1)

    if wrapped:
        tall = (
            [turned(both[q], SLOT, 0) for q in range(blocks - HALO, blocks)]
            + both
            + [turned(both[q], lanes - SLOT, SLOTS - 1) for q in range(HALO)]
        )
    else:
        tall = both + [
            turned(both[e % blocks], lanes - SLOT * (e // blocks), -1)
            for e in range(blocks, blocks + 2 * HALO)
        ]
    field = jnp.concatenate(tall, axis=0)
    moved = jnp.dot(field, matrix, preferred_element_type=F32)
    count = len(tall)
    for a in range(TAPS - 1):
        part = moved[:, a * lanes : (a + 1) * lanes].astype(BF)
        xe[a, :count] = part.reshape(count, chans, lanes)
        xe[a, count:] = jnp.zeros((SPAN - count, chans, lanes), BF)
    low = HALO * DEPTH
    for g in range(chans // GROUP):
        at = slice(GROUP * g, GROUP * (g + 1))
        rhs = jnp.concatenate([xe[a, :, at, :].reshape(DEPTH, lanes) for a in range(TAPS - 1)], axis=0)
        tops = slice(0, blocks * GROUP)
        lhs = jnp.concatenate([band[g, tops, :low], band[g, tops, low + DEPTH : wide]], axis=1)
        out = jnp.dot(lhs, rhs, preferred_element_type=F32)
        halo[:, at, :] = out.reshape(blocks, GROUP, lanes)


def norm_rows(a_ref, row0, count, halo, gain, out):
    _, chans, lanes = a_ref.shape
    blocks = halo.shape[0]
    edge = edge_lanes((chans, lanes))
    for r in range(count):
        q, slot = (row0 + r) % blocks, (row0 + r) // blocks
        extra = pltpu.roll(halo[q], lanes - SLOT * slot, 1) if slot else halo[q]
        a = a_ref[row0 + r] + jnp.where(edge, extra, 0.0)
        center = a - jnp.mean(a, axis=0, keepdims=True)
        var = jnp.mean(center * center, axis=0, keepdims=True)
        normed = (center * lax.rsqrt(var + 1e-06) * gain).astype(BF)
        out[:, r * lanes : (r + 1) * lanes] = normed


def branch_of(normed, up_t, down_t):
    z = jnp.dot(up_t, normed, preferred_element_type=F32)
    h = twice_gelu(z.astype(BF))
    return jnp.dot(down_t, h, preferred_element_type=F32)


def atmos_kernel(layer, members, count, *refs):
    x_ref, a_ref, left_ref, right_ref, band_ref, g_ref, up_ref, dn_ref, s_ref = refs[:9]
    if layer == 0:
        y_ref, p_ref = refs[9:11]
    else:
        fw_ref, y_ref, keep_ref, give_ref, flux = refs[9:14]
    xe, halo, even, odd = refs[-4:]
    rows, chans, lanes = x_ref.shape
    blocks = halo.shape[0]
    halo_conv(left_ref, right_ref, band_ref, True, halo_matrix(lanes), xe, halo)
    up_t = transposed(up_ref[layer])
    dn_t = halved(dn_ref[layer])
    gain = spread(g_ref[layer : layer + 1], lanes)
    scale = spread(s_ref[layer : layer + 1], lanes)
    keep = edge_lanes((chans, lanes)).astype(F32).astype(BF)
    packed = [None] * blocks
    if layer == 1:
        blank = jnp.zeros((HALO,) + flux.shape[1:], BF)
        flux[0:HALO] = blank
        flux[rows + HALO : rows + 2 * HALO] = blank
    norm_rows(a_ref, 0, count, halo, gain, even)
    for step in range(rows // count):
        row0 = step * count
        now, later = (even, odd) if step % 2 == 0 else (odd, even)
        if row0 + count < rows:
            norm_rows(a_ref, row0 + count, count, halo, gain, later)
        branch = branch_of(now[...], up_t, dn_t)
        made = []
        for r in range(count):
            y = x_ref[row0 + r].astype(F32) + scale * branch[:, r * lanes : (r + 1) * lanes]
            made.append(y.astype(BF))
            y_ref[row0 + r] = made[r]
        if layer == 0:
            for r in range(count):
                q, slot = (row0 + r) % blocks, (row0 + r) // blocks
                moved = made[r] * keep
                if slot:
                    moved = pltpu.roll(moved, SLOT * slot, 1)
                packed[q] = moved if packed[q] is None else packed[q] + moved
            if row0 % (4 * count) == 3 * count or row0 + count == rows:
                for q in range(blocks):
                    if row0 < 4 * count:
                        p_ref[q] = packed[q]
                    else:
                        p_ref[q] = p_ref[q] + packed[q]
                packed = [None] * blocks
        else:
            z = jnp.dot(fw_ref[...], jnp.concatenate(made, axis=1), preferred_element_type=F32)
            f = (0.5 * twice_gelu(z)).astype(BF)
            for r in range(count):
                flux[row0 + HALO + r] = f[:, r * lanes : (r + 1) * lanes]
    if layer == 1:
        rank = lax.axis_index("member")
        share = rows // members
        for k in range(members):
            chunk = flux[pl.ds((rank ^ k) * share, share + 2 * HALO)]
            if k % 2:
                give_ref[k // 2] = chunk
            else:
                keep_ref[k // 2] = chunk


def atmos_block(layer, members, x, a, edges, band, weights, count):
    rows, chans, lanes = x.shape
    blocks = rows // SLOTS
    args = [x, a, *edges, band, *weights]
    outs = [jax.ShapeDtypeStruct(x.shape, BF)]
    scratch = []
    if layer == 0:
        outs.append(jax.ShapeDtypeStruct((blocks, chans, lanes), BF))
    else:
        flux = weights[-1].shape[0]
        share = rows // members
        outs += [jax.ShapeDtypeStruct((members // 2, share + 2 * HALO, flux, lanes), BF)] * 2
        scratch.append(pltpu.VMEM((rows + 2 * HALO, flux, lanes), BF))
    return pl.pallas_call(
        functools.partial(atmos_kernel, layer, members, count),
        out_shape=outs,
        in_specs=[VMEM] * len(args),
        out_specs=[VMEM] * len(outs),
        scratch_shapes=scratch
        + [
            pltpu.VMEM((TAPS - 1, SPAN, chans, lanes), BF),
            pltpu.VMEM((blocks, chans, lanes), F32),
            pltpu.VMEM((chans, count * lanes), BF),
            pltpu.VMEM((chans, count * lanes), BF),
        ],
        compiler_params=params(BIG),
        cost_estimate=cost(8),
        name="atmos_block",
    )(*args)


def add_kernel(keep_ref, got_ref, *out_refs):
    for n, ref in enumerate(out_refs):
        k = n + keep_ref.shape[0] - len(out_refs)
        ref[...] = (keep_ref[k].astype(F32) + got_ref[k].astype(F32)).astype(BF)


def add_pairs(keep, got, skip):
    count = keep.shape[0] - skip
    return pl.pallas_call(
        add_kernel,
        out_shape=[jax.ShapeDtypeStruct(keep.shape[1:], BF)] * count,
        in_specs=[VMEM] * 2,
        out_specs=[VMEM] * count,
        compiler_params=params(24),
        name="add_pairs",
    )(keep, got)


def send_xor(value, bits):
    members = lax.axis_size("member")
    return lax.ppermute(value, "member", [(i, i ^ bits) for i in range(members)])


def force_kernel(members, *refs):
    near_refs, flux_refs = refs[:2], refs[2 : members // 2 + 1]
    ocean_ref, land_ref, ice_ref, lift_ref, mid_ref, p_ref, win, sem = refs[members // 2 + 1 :]
    span, flux, lanes = flux_refs[0].shape
    rows = land_ref.shape[0]
    chans = mid_ref.shape[1]
    share = rows // members
    blocks = p_ref.shape[0]
    first = lax.axis_index("member") * share - HALO
    start = jnp.clip(first, 0, rows - span)
    copy = pltpu.make_async_copy(ocean_ref.at[pl.ds(start, span)], win, sem)
    copy.start()
    total = near_refs[0][0].astype(F32) + near_refs[1][0].astype(F32)
    for ref in flux_refs:
        total = total + ref[...].astype(F32)
    low = (total / members).astype(BF)
    lift = jnp.concatenate([transposed(lift_ref[0]), transposed(lift_ref[1])], axis=0)
    terms = jnp.dot(
        lift, jnp.concatenate([low[r] for r in range(span)], axis=1), preferred_element_type=F32
    )
    keep = edge_lanes((chans, lanes)).astype(F32).astype(BF)
    packed = [None] * blocks
    copy.wait()
    for r in range(span):
        row = first + r
        safe = jnp.clip(row, 0, rows - 1)
        sea = (1 - land_ref[pl.ds(safe, 1), :]).astype(F32)
        ice = ice_ref[pl.ds(safe, 1), :].astype(F32)
        at = slice(r * lanes, (r + 1) * lanes)
        forcing = sea * ((1.0 - ice) * terms[:chans, at] + ice * terms[chans:, at])
        mid = win[jnp.clip(row - start, 0, span - 1)].astype(F32) + forcing
        inside = (row >= 0) & (row < rows)
        mid = jnp.where(inside, mid, 0.0).astype(BF)
        mid_ref[r] = mid
        q, slot = r % blocks, r // blocks
        moved = mid * keep
        if slot:
            moved = pltpu.roll(moved, SLOT * slot, 1)
        packed[q] = moved if packed[q] is None else packed[q] + moved
    for q in range(blocks):
        p_ref[q] = packed[q]


def force(members, chunks, ocean, land, ice, lift):
    span, _, lanes = chunks[-1].shape
    rows, chans, _ = ocean.shape
    return pl.pallas_call(
        functools.partial(force_kernel, members),
        out_shape=[
            jax.ShapeDtypeStruct((span, chans, lanes), BF),
            jax.ShapeDtypeStruct((OCEAN_BLOCKS, chans, lanes), BF),
        ],
        in_specs=[VMEM] * len(chunks) + [HBM, VMEM, VMEM, VMEM],
        out_specs=[VMEM] * 2,
        scratch_shapes=[pltpu.VMEM((span, chans, lanes), BF), pltpu.SemaphoreType.DMA(())],
        compiler_params=params(24),
        name="ocean_forcing",
    )(*chunks, ocean, land, ice, lift)


def ocean_kernel(mid_ref, a_ref, left_ref, right_ref, band_ref, land_ref, mat_ref, upt_ref, gain_ref, scale_ref, dn_ref, sw_ref, new_ref, surf_ref, xe, halo, normed):
    share, chans, lanes = new_ref.shape
    halo_conv(left_ref, right_ref, band_ref, False, mat_ref[...], xe, halo)
    scale = scale_ref[...]
    norm_rows(a_ref, 0, share, halo, gain_ref[...], normed)
    branch = branch_of(normed[...], upt_ref[...], halved(dn_ref[...]))
    first = lax.axis_index("member") * share
    made = []
    for r in range(share):
        sea = (1 - land_ref[pl.ds(first + r, 1), :]).astype(F32)
        y = mid_ref[HALO + r].astype(F32) + scale * branch[:, r * lanes : (r + 1) * lanes]
        made.append((y * sea).astype(BF))
        new_ref[r] = made[r]
    surf = jnp.dot(
        sw_ref[...], jnp.concatenate(made, axis=1), preferred_element_type=F32
    )
    for r in range(share):
        surf_ref[r] = surf[:, r * lanes : (r + 1) * lanes].astype(BF)


def ocean_block(mid, a, left, right, band, land, ready, down, surf_weight):
    share, chans, lanes = a.shape
    blocks = left.shape[0]
    return pl.pallas_call(
        ocean_kernel,
        out_shape=[
            jax.ShapeDtypeStruct((share, chans, lanes), BF),
            jax.ShapeDtypeStruct((share, surf_weight.shape[0], lanes), BF),
        ],
        in_specs=[VMEM] * 12,
        out_specs=[VMEM] * 2,
        scratch_shapes=[
            pltpu.VMEM((TAPS - 1, SPAN, chans, lanes), BF),
            pltpu.VMEM((blocks, chans, lanes), F32),
            pltpu.VMEM((chans, share * lanes), BF),
        ],
        compiler_params=params(24),
        name="ocean_block",
    )(mid, a, left, right, band, land, *ready, down, surf_weight)


def pair_kernel(own_ref, got_ref, out_ref):
    out_ref[0] = own_ref[...]
    out_ref[1] = got_ref[...]


def make_pair(own, got):
    return pl.pallas_call(
        pair_kernel,
        out_shape=jax.ShapeDtypeStruct((2,) + own.shape, BF),
        in_specs=[VMEM] * 2,
        out_specs=VMEM,
        compiler_params=params(24),
        name="surface_pair",
    )(own, got)


def couple_kernel(y_ref, land_ref, bw_ref, *refs):
    pair_refs, o_ref = refs[:-1], refs[-1]
    chans, lanes = y_ref.shape[1:]
    share = pair_refs[0].shape[1]
    rank = lax.axis_index("member")
    pair = pl.program_id(0)
    parity = rank % 2
    mine = pair ^ (rank // 2)
    surf = [None] * (2 * share)
    for side in range(2):
        for r in range(share):
            value = pair_refs[0][side ^ parity, r]
            for k, ref in enumerate(pair_refs[1:]):
                value = jnp.where(mine == k + 1, ref[side ^ parity, r], value)
            surf[side * share + r] = value
    back = jnp.dot(bw_ref[...], jnp.concatenate(surf, axis=1), preferred_element_type=F32)
    first = pair * 2 * share
    for r in range(2 * share):
        sea = (1 - land_ref[pl.ds(first + r, 1), :]).astype(F32)
        out = y_ref[first + r].astype(F32) + sea * back[:, r * lanes : (r + 1) * lanes]
        o_ref[r] = out.astype(BF)


def couple(y, land, back_weight, pairs):
    rows, chans, lanes = y.shape
    count = 2 * pairs[0].shape[1]
    return pl.pallas_call(
        couple_kernel,
        grid=(rows // count,),
        out_shape=jax.ShapeDtypeStruct(y.shape, BF),
        in_specs=[VMEM] * (3 + len(pairs)),
        out_specs=pl.BlockSpec((count, chans, lanes), lambda i: (i, 0, 0)),
        compiler_params=params(24),
        name="couple",
    )(y, land, back_weight, *pairs)


def local(
    atmos,
    ocean,
    land_mask,
    ice_mask,
    atm_kernel,
    atm_gain,
    atm_up,
    atm_down,
    atm_scale,
    flux_weight,
    flux_lift,
    ocn_kernel,
    ocn_gain,
    ocn_up,
    ocn_down,
    ocn_scale,
    surf_weight,
    back_weight,
):
    members = lax.axis_size("member")
    half = members // 2
    state = atmos[0]
    rows = state.shape[0]
    blocks = rows // SLOTS
    big, small = 4 * blocks, 2 * blocks
    atm = (atm_gain, atm_up, atm_down.transpose(0, 2, 1), atm_scale)
    taps = atm_kernel.transpose(1, 2, 0, 3)

    edges = neighbours(pack(state, big))
    a, band = convolve(0, state, taps, blocks)
    state, packed = atmos_block(0, members, state, a, edges, band, atm, small)

    edges = neighbours(packed)
    a, band = convolve(1, state, taps, blocks)
    state, keep, give = atmos_block(
        1, members, state, a, edges, band, (*atm, flux_weight.T), small
    )
    got = send_xor(give, 1)
    sums = add_pairs(keep, got, 1)
    sent = [send_xor(sums[k - 1], 2 * k) for k in range(half - 1, 0, -1)]
    band, *ready = prepare_ocean(ocn_kernel, ocn_gain, ocn_up, ocn_scale, sums[0])
    sent = [keep, got] + sent

    mid, packed = force(members, sent, ocean, land_mask, ice_mask, flux_lift)
    left, right = neighbours(packed)
    a = ocean_conv(mid, band)
    ocean_rows, surface = ocean_block(
        mid, a, left, right, band, land_mask, ready, ocn_down.T, surf_weight.T
    )
    own = make_pair(surface, send_xor(surface, 1))
    pairs = [own] + [send_xor(own, 2 * k) for k in range(1, half)]
    out = couple(state, land_mask, back_weight.T, pairs)
    return (out[None], ocean_rows)


def solution(mesh):
    in_specs = (
        P("member", None, None, "lon"),
        P(None, None, "lon"),
        P(None, "lon"),
        P(None, "lon"),
    ) + (P(),) * 14
    out_specs = (P("member", None, None, "lon"), P("member", None, "lon"))
    return jax.shard_map(local, mesh=mesh, in_specs=in_specs, out_specs=out_specs, check_vma=False)
```

```python
import functools

import jax
import jax.numpy as jnp
from jax import lax
from jax.experimental import pallas as pl
from jax.experimental.pallas import tpu as pltpu
from jax.sharding import PartitionSpec as P

BF = jnp.bfloat16
F32 = jnp.float32
TANH_A = 0.7978845608028654
TANH_B = TANH_A * 0.044715
TAPS = 7
HALO = 3
GROUP = 16
SPAN = 16
OUT = SPAN - TAPS + 1
DEPTH = GROUP * SPAN
SLOT = 8
SLOTS = 16
OCEAN_BLOCKS = 2
BIG = 32
VMEM = pl.BlockSpec(memory_space=pltpu.VMEM)
ANY = pl.BlockSpec(memory_space=pl.ANY)
HBM = pl.BlockSpec(memory_space=pltpu.HBM)


def params(mib):
    return pltpu.CompilerParams(vmem_limit_bytes=mib * 2**20)


def cost(gflop):
    return pl.CostEstimate(flops=int(gflop * 1e9), bytes_accessed=0, transcendentals=0)


def twice_gelu(z):
    return z + z * jnp.tanh(z * (TANH_A + TANH_B * (z * z)))


def transposed(value):
    return value.astype(F32).T.astype(BF)


def halved(value):
    return (0.5 * value.astype(F32)).astype(BF)


def spread(row, lanes):
    return jnp.broadcast_to(row.T, (row.shape[1], lanes))


def edge_lanes(shape):
    lane = lax.broadcasted_iota(jnp.int32, shape, len(shape) - 1)
    return (lane < HALO) | (lane >= shape[-1] - HALO)


def pack_kernel(step, src_ref, p_ref, x_ref, sems):
    rows, chans, lanes = x_ref.shape
    blocks = p_ref.shape[0]
    copies = []
    for n in range(rows // step):
        at = slice(n * step, (n + 1) * step)
        copies.append(pltpu.make_async_copy(src_ref.at[at], x_ref.at[at], sems.at[n]))
        copies[n].start()
    keep = edge_lanes((chans, lanes)).astype(F32).astype(BF)
    for n in range(rows // step):
        copies[n].wait()
        for q in range(blocks):
            total = None if n == 0 else p_ref[q]
            for slot in range(n * step // blocks, (n + 1) * step // blocks):
                moved = x_ref[slot * blocks + q] * keep
                if slot:
                    moved = pltpu.roll(moved, SLOT * slot, 1)
                total = moved if total is None else total + moved
            p_ref[q] = total


def pack(x, step):
    rows, chans, lanes = x.shape
    return pl.pallas_call(
        functools.partial(pack_kernel, step),
        out_shape=jax.ShapeDtypeStruct((rows // SLOTS, chans, lanes), BF),
        in_specs=[HBM],
        out_specs=VMEM,
        scratch_shapes=[pltpu.VMEM(x.shape, BF), pltpu.SemaphoreType.DMA((rows // step,))],
        compiler_params=params(60),
        name="pack_edges",
    )(x)


def neighbours(packed):
    count = lax.axis_size("lon")
    first = lax.ppermute(packed, "lon", [(i, i ^ 1) for i in range(count)])
    second = lax.ppermute(
        packed, "lon", [(i, (i - 1) % count if i % 2 == 0 else (i + 1) % count) for i in range(count)]
    )
    return first, second


def by_side(first, second):
    even = lax.axis_index("lon") % 2 == 0
    return jnp.where(even, second, first), jnp.where(even, first, second)


def fill_base(taps, base):
    groups, _, wide = base.shape
    chans = groups * GROUP
    tall = TAPS * SLOT
    t = lax.broadcasted_iota(jnp.int32, (tall, wide), 0)
    n = lax.broadcasted_iota(jnp.int32, (tall, wide), 1)
    hit = (t % SLOT == n // DEPTH) & (t // SLOT == (n % DEPTH) // GROUP)
    columns = []
    for i in range(TAPS):
        columns.append(taps(i).T)
        columns.append(jnp.zeros((chans, SLOT - TAPS), F32))
    columns = jnp.concatenate(columns, axis=1).astype(BF)
    total = jnp.dot(columns, hit.astype(F32).astype(BF), preferred_element_type=F32)
    r = lax.broadcasted_iota(jnp.int32, (GROUP, wide), 0)
    c = lax.broadcasted_iota(jnp.int32, (GROUP, wide), 1)
    same = r == c % GROUP
    for g in range(groups):
        base[g] = jnp.where(same, total[GROUP * g : GROUP * (g + 1)], 0.0)


def fill_band(base, g, band):
    for j in range(TAPS):
        one = base[g, :, j * DEPTH : (j + 1) * DEPTH]
        for r in range(OUT):
            moved = pltpu.roll(one, GROUP * r, 1) if r else one
            band[GROUP * r : GROUP * (r + 1), j * DEPTH : (j + 1) * DEPTH] = moved.astype(BF)


def fill_shifts(x, pad, xj):
    count, _, lanes = x.shape
    lane = lax.broadcasted_iota(jnp.int32, (GROUP, lanes), 1)
    for j in range(TAPS):
        d = j - HALO
        if d:
            keep = ((lane < lanes - d) if d > 0 else (lane >= -d)).astype(F32).astype(BF)
            xj[j, pad : pad + count] = pltpu.roll(x, (-d) % lanes, 2) * keep[None]
        else:
            xj[j, pad : pad + count] = x


def clear_pads(pad, count, xj):
    tall, _, lanes = xj.shape[1:]
    for j in range(TAPS):
        if pad:
            xj[j, :pad] = jnp.zeros((pad, GROUP, lanes), BF)
        if tall > pad + count:
            xj[j, pad + count :] = jnp.zeros((tall - pad - count, GROUP, lanes), BF)


def apply_band(band, xj, a_ref):
    rows, _, lanes = a_ref.shape
    starts = [min(OUT * i, max(rows - OUT, 0)) for i in range(-(-rows // OUT))]
    field = jnp.concatenate(
        [
            jnp.concatenate([xj[j, s : s + SPAN].reshape(DEPTH, lanes) for j in range(TAPS)], axis=0)
            for s in starts
        ],
        axis=1,
    )
    out = jnp.dot(band, field, preferred_element_type=F32)
    take = min(OUT, rows)
    for n, s in enumerate(starts):
        part = out[: take * GROUP, n * lanes : (n + 1) * lanes]
        a_ref[s : s + take] = part.reshape(take, GROUP, lanes)


def conv_kernel(layer, x_ref, k_ref, a_ref, band_ref, base, even_xj, odd_xj, even_band, odd_band):
    rows, chans, lanes = x_ref.shape
    groups = chans // GROUP
    fill_base(lambda i: k_ref[i, :, layer, :], base)
    clear_pads(HALO, rows, even_xj)
    clear_pads(HALO, rows, odd_xj)

    def at(g):
        return pl.ds(pl.multiple_of(GROUP * g, GROUP), GROUP)

    def prepare(g, xj, band):
        fill_band(base, g, band)
        band_ref[g] = band[: band_ref.shape[1]]
        fill_shifts(x_ref[:, at(g), :], HALO, xj)

    prepare(0, even_xj, even_band)

    def pair(i, carry):
        prepare(2 * i + 1, odd_xj, odd_band)
        apply_band(even_band[...], even_xj, a_ref.at[:, at(2 * i), :])
        prepare(jnp.minimum(2 * i + 2, groups - 1), even_xj, even_band)
        apply_band(odd_band[...], odd_xj, a_ref.at[:, at(2 * i + 1), :])
        return carry

    lax.fori_loop(0, groups // 2, pair, 0)


def convolve(layer, x, taps, blocks):
    rows, chans, lanes = x.shape
    groups = chans // GROUP
    wide = TAPS * DEPTH
    return pl.pallas_call(
        functools.partial(conv_kernel, layer),
        out_shape=[
            jax.ShapeDtypeStruct((rows, chans, lanes), F32),
            jax.ShapeDtypeStruct((groups, blocks * GROUP, wide), BF),
        ],
        in_specs=[VMEM, VMEM],
        out_specs=[VMEM, VMEM],
        scratch_shapes=[
            pltpu.VMEM((groups, GROUP, wide), F32),
        ]
        + [pltpu.VMEM((TAPS, rows + 2 * HALO, GROUP, lanes), BF)] * 2
        + [pltpu.VMEM((GROUP * OUT, wide), BF)] * 2,
        compiler_params=params(BIG),
        cost_estimate=cost(8),
        name="conv",
    )(x, taps)


def prepare_kernel(k_ref, g_ref, up_ref, s_ref, _, band_ref, mat_ref, upt_ref, gain_ref, scale_ref, base):
    lanes = gain_ref.shape[1]
    mat_ref[...] = halo_matrix(lanes)
    upt_ref[...] = transposed(up_ref[...])
    gain_ref[...] = spread(g_ref[...], lanes)
    scale_ref[...] = spread(s_ref[...], lanes)
    fill_base(lambda i: k_ref[i], base)
    for g in range(base.shape[0]):
        fill_band(base, g, band_ref.at[g])


def prepare_ocean(taps, gain, up, scale, after):
    chans, hid = up.shape
    lanes = after.shape[-1]
    groups = chans // GROUP
    wide = TAPS * DEPTH
    return pl.pallas_call(
        prepare_kernel,
        out_shape=[
            jax.ShapeDtypeStruct((groups, GROUP * OUT, wide), BF),
            jax.ShapeDtypeStruct((2 * lanes, (TAPS - 1) * lanes), BF),
            jax.ShapeDtypeStruct((hid, chans), BF),
            jax.ShapeDtypeStruct((chans, lanes), F32),
            jax.ShapeDtypeStruct((chans, lanes), F32),
        ],
        in_specs=[VMEM] * 4 + [ANY],
        out_specs=[VMEM] * 5,
        scratch_shapes=[pltpu.VMEM((groups, GROUP, wide), F32)],
        compiler_params=params(24),
        cost_estimate=cost(3),
        name="prepare_ocean",
    )(taps, gain[None], up, scale[None], after)


def ocean_conv_kernel(x_ref, band_ref, a_ref, xj):
    count, chans, lanes = x_ref.shape
    for g in range(chans // GROUP):
        at = slice(GROUP * g, GROUP * (g + 1))
        clear_pads(0, count, xj.at[g])
        fill_shifts(x_ref[:, at, :], 0, xj.at[g])
        apply_band(band_ref[g], xj.at[g], a_ref.at[:, at, :])


def ocean_conv(x, band):
    count, chans, lanes = x.shape
    return pl.pallas_call(
        ocean_conv_kernel,
        out_shape=jax.ShapeDtypeStruct((count - 2 * HALO, chans, lanes), F32),
        in_specs=[VMEM, VMEM],
        out_specs=VMEM,
        scratch_shapes=[pltpu.VMEM((chans // GROUP, TAPS, max(count, SPAN), GROUP, lanes), BF)],
        compiler_params=params(24),
        cost_estimate=cost(2),
        name="ocean_conv",
    )(x, band)


def halo_matrix(lanes):
    shape = (lanes, lanes)
    src = lax.broadcasted_iota(jnp.int32, shape, 0)
    dst = lax.broadcasted_iota(jnp.int32, shape, 1)
    ahead = (src - dst + lanes) % lanes
    right = (src % SLOT < HALO) & (dst % SLOT >= SLOT - HALO)
    left = (src % SLOT >= SLOT - HALO) & (dst % SLOT < HALO)
    right = jnp.where(right, ahead, -1)
    left = jnp.where(left, ahead, -1)
    none = jnp.zeros(shape, BF)
    upper, lower = [], []
    for j in range(TAPS):
        d = j - HALO
        if d > 0:
            upper.append((right == d).astype(F32).astype(BF))
            lower.append(none)
        elif d < 0:
            upper.append(none)
            lower.append((left == lanes + d).astype(F32).astype(BF))
    return jnp.concatenate(
        [jnp.concatenate(upper, axis=1), jnp.concatenate(lower, axis=1)], axis=0
    )


def halo_conv(first, second, band, wrapped, matrix, xe, halo):
    blocks, chans, lanes = halo.shape
    wide = TAPS * DEPTH
    both = []
    for q in range(blocks):
        left, right = by_side(first[q], second[q])
        both.append(jnp.concatenate([right, left], axis=1))
    lane = lax.broadcasted_iota(jnp.int32, (chans, lanes), 1)
    slot = (lane + HALO) // SLOT % SLOTS

    def turned(value, shift, drop):
        parts = [pltpu.roll(value[:, n * lanes : (n + 1) * lanes], shift, 1) for n in range(2)]
        if drop >= 0:
            keep = (slot != drop).astype(F32).astype(BF)
            parts = [part * keep for part in parts]
        return jnp.concatenate(parts, axis=1)

    if wrapped:
        tall = (
            [turned(both[q], SLOT, 0) for q in range(blocks - HALO, blocks)]
            + both
            + [turned(both[q], lanes - SLOT, SLOTS - 1) for q in range(HALO)]
        )
    else:
        tall = both + [
            turned(both[e % blocks], lanes - SLOT * (e // blocks), -1)
            for e in range(blocks, blocks + 2 * HALO)
        ]
    field = jnp.concatenate(tall, axis=0)
    moved = jnp.dot(field, matrix, preferred_element_type=F32)
    count = len(tall)
    for a in range(TAPS - 1):
        part = moved[:, a * lanes : (a + 1) * lanes].astype(BF)
        xe[a, :count] = part.reshape(count, chans, lanes)
        xe[a, count:] = jnp.zeros((SPAN - count, chans, lanes), BF)
    low = HALO * DEPTH
    for g in range(chans // GROUP):
        at = slice(GROUP * g, GROUP * (g + 1))
        rhs = jnp.concatenate([xe[a, :, at, :].reshape(DEPTH, lanes) for a in range(TAPS - 1)], axis=0)
        tops = slice(0, blocks * GROUP)
        lhs = jnp.concatenate([band[g, tops, :low], band[g, tops, low + DEPTH : wide]], axis=1)
        out = jnp.dot(lhs, rhs, preferred_element_type=F32)
        halo[:, at, :] = out.reshape(blocks, GROUP, lanes)


def norm_rows(a_ref, row0, count, halo, gain, out):
    _, chans, lanes = a_ref.shape
    blocks = halo.shape[0]
    edge = edge_lanes((chans, lanes))
    for r in range(count):
        q, slot = (row0 + r) % blocks, (row0 + r) // blocks
        extra = pltpu.roll(halo[q], lanes - SLOT * slot, 1) if slot else halo[q]
        a = a_ref[row0 + r] + jnp.where(edge, extra, 0.0)
        center = a - jnp.mean(a, axis=0, keepdims=True)
        var = jnp.mean(center * center, axis=0, keepdims=True)
        normed = (center * lax.rsqrt(var + 1e-06) * gain).astype(BF)
        out[:, r * lanes : (r + 1) * lanes] = normed


def branch_of(normed, up_t, down_t):
    z = jnp.dot(up_t, normed, preferred_element_type=F32)
    h = twice_gelu(z.astype(BF))
    return jnp.dot(down_t, h, preferred_element_type=F32)


def atmos_kernel(layer, members, count, *refs):
    x_ref, a_ref, left_ref, right_ref, band_ref, g_ref, up_ref, dn_ref, s_ref = refs[:9]
    if layer == 0:
        y_ref, p_ref = refs[9:11]
    else:
        fw_ref, y_ref, keep_ref, give_ref, flux = refs[9:14]
    xe, halo, even, odd = refs[-4:]
    rows, chans, lanes = x_ref.shape
    blocks = halo.shape[0]
    halo_conv(left_ref, right_ref, band_ref, True, halo_matrix(lanes), xe, halo)
    up_t = transposed(up_ref[layer])
    dn_t = halved(dn_ref[layer])
    gain = spread(g_ref[layer : layer + 1], lanes)
    scale = spread(s_ref[layer : layer + 1], lanes)
    keep = edge_lanes((chans, lanes)).astype(F32).astype(BF)
    packed = [None] * blocks
    if layer == 1:
        blank = jnp.zeros((HALO,) + flux.shape[1:], BF)
        flux[0:HALO] = blank
        flux[rows + HALO : rows + 2 * HALO] = blank
    norm_rows(a_ref, 0, count, halo, gain, even)
    for step in range(rows // count):
        row0 = step * count
        now, later = (even, odd) if step % 2 == 0 else (odd, even)
        if row0 + count < rows:
            norm_rows(a_ref, row0 + count, count, halo, gain, later)
        branch = branch_of(now[...], up_t, dn_t)
        made = []
        for r in range(count):
            y = x_ref[row0 + r].astype(F32) + scale * branch[:, r * lanes : (r + 1) * lanes]
            made.append(y.astype(BF))
            y_ref[row0 + r] = made[r]
        if layer == 0:
            for r in range(count):
                q, slot = (row0 + r) % blocks, (row0 + r) // blocks
                moved = made[r] * keep
                if slot:
                    moved = pltpu.roll(moved, SLOT * slot, 1)
                packed[q] = moved if packed[q] is None else packed[q] + moved
            if row0 % (4 * count) == 3 * count or row0 + count == rows:
                for q in range(blocks):
                    if row0 < 4 * count:
                        p_ref[q] = packed[q]
                    else:
                        p_ref[q] = p_ref[q] + packed[q]
                packed = [None] * blocks
        else:
            z = jnp.dot(fw_ref[...], jnp.concatenate(made, axis=1), preferred_element_type=F32)
            f = (0.5 * twice_gelu(z)).astype(BF)
            for r in range(count):
                flux[row0 + HALO + r] = f[:, r * lanes : (r + 1) * lanes]
    if layer == 1:
        rank = lax.axis_index("member")
        share = rows // members
        for k in range(members):
            chunk = flux[pl.ds((rank ^ k) * share, share + 2 * HALO)]
            if k % 2:
                give_ref[k // 2] = chunk
            else:
                keep_ref[k // 2] = chunk


def atmos_block(layer, members, x, a, edges, band, weights, count):
    rows, chans, lanes = x.shape
    blocks = rows // SLOTS
    args = [x, a, *edges, band, *weights]
    outs = [jax.ShapeDtypeStruct(x.shape, BF)]
    scratch = []
    if layer == 0:
        outs.append(jax.ShapeDtypeStruct((blocks, chans, lanes), BF))
    else:
        flux = weights[-1].shape[0]
        share = rows // members
        outs += [jax.ShapeDtypeStruct((members // 2, share + 2 * HALO, flux, lanes), BF)] * 2
        scratch.append(pltpu.VMEM((rows + 2 * HALO, flux, lanes), BF))
    return pl.pallas_call(
        functools.partial(atmos_kernel, layer, members, count),
        out_shape=outs,
        in_specs=[VMEM] * len(args),
        out_specs=[VMEM] * len(outs),
        scratch_shapes=scratch
        + [
            pltpu.VMEM((TAPS - 1, SPAN, chans, lanes), BF),
            pltpu.VMEM((blocks, chans, lanes), F32),
            pltpu.VMEM((chans, count * lanes), BF),
            pltpu.VMEM((chans, count * lanes), BF),
        ],
        compiler_params=params(BIG),
        cost_estimate=cost(8),
        name="atmos_block",
    )(*args)


def add_kernel(keep_ref, got_ref, *out_refs):
    for n, ref in enumerate(out_refs):
        k = n + keep_ref.shape[0] - len(out_refs)
        ref[...] = (keep_ref[k].astype(F32) + got_ref[k].astype(F32)).astype(BF)


def add_pairs(keep, got, skip):
    count = keep.shape[0] - skip
    return pl.pallas_call(
        add_kernel,
        out_shape=[jax.ShapeDtypeStruct(keep.shape[1:], BF)] * count,
        in_specs=[VMEM] * 2,
        out_specs=[VMEM] * count,
        compiler_params=params(24),
        name="add_pairs",
    )(keep, got)


def send_xor(value, bits):
    members = lax.axis_size("member")
    return lax.ppermute(value, "member", [(i, i ^ bits) for i in range(members)])


def force_kernel(members, *refs):
    near_refs, flux_refs = refs[:2], refs[2 : members // 2 + 1]
    ocean_ref, land_ref, ice_ref, lift_ref, mid_ref, p_ref, win, sem = refs[members // 2 + 1 :]
    span, flux, lanes = flux_refs[0].shape
    rows = land_ref.shape[0]
    chans = mid_ref.shape[1]
    share = rows // members
    blocks = p_ref.shape[0]
    first = lax.axis_index("member") * share - HALO
    start = jnp.clip(first, 0, rows - span)
    copy = pltpu.make_async_copy(ocean_ref.at[pl.ds(start, span)], win, sem)
    copy.start()
    total = near_refs[0][0].astype(F32) + near_refs[1][0].astype(F32)
    for ref in flux_refs:
        total = total + ref[...].astype(F32)
    low = (total / members).astype(BF)
    lift = jnp.concatenate([transposed(lift_ref[0]), transposed(lift_ref[1])], axis=0)
    terms = jnp.dot(
        lift, jnp.concatenate([low[r] for r in range(span)], axis=1), preferred_element_type=F32
    )
    keep = edge_lanes((chans, lanes)).astype(F32).astype(BF)
    packed = [None] * blocks
    copy.wait()
    for r in range(span):
        row = first + r
        safe = jnp.clip(row, 0, rows - 1)
        sea = (1 - land_ref[pl.ds(safe, 1), :]).astype(F32)
        ice = ice_ref[pl.ds(safe, 1), :].astype(F32)
        at = slice(r * lanes, (r + 1) * lanes)
        forcing = sea * ((1.0 - ice) * terms[:chans, at] + ice * terms[chans:, at])
        mid = win[jnp.clip(row - start, 0, span - 1)].astype(F32) + forcing
        inside = (row >= 0) & (row < rows)
        mid = jnp.where(inside, mid, 0.0).astype(BF)
        mid_ref[r] = mid
        q, slot = r % blocks, r // blocks
        moved = mid * keep
        if slot:
            moved = pltpu.roll(moved, SLOT * slot, 1)
        packed[q] = moved if packed[q] is None else packed[q] + moved
    for q in range(blocks):
        p_ref[q] = packed[q]


def force(members, chunks, ocean, land, ice, lift):
    span, _, lanes = chunks[-1].shape
    rows, chans, _ = ocean.shape
    return pl.pallas_call(
        functools.partial(force_kernel, members),
        out_shape=[
            jax.ShapeDtypeStruct((span, chans, lanes), BF),
            jax.ShapeDtypeStruct((OCEAN_BLOCKS, chans, lanes), BF),
        ],
        in_specs=[VMEM] * len(chunks) + [HBM, VMEM, VMEM, VMEM],
        out_specs=[VMEM] * 2,
        scratch_shapes=[pltpu.VMEM((span, chans, lanes), BF), pltpu.SemaphoreType.DMA(())],
        compiler_params=params(24),
        name="ocean_forcing",
    )(*chunks, ocean, land, ice, lift)


def ocean_kernel(mid_ref, a_ref, left_ref, right_ref, band_ref, land_ref, mat_ref, upt_ref, gain_ref, scale_ref, dn_ref, sw_ref, new_ref, surf_ref, xe, halo, normed):
    share, chans, lanes = new_ref.shape
    halo_conv(left_ref, right_ref, band_ref, False, mat_ref[...], xe, halo)
    scale = scale_ref[...]
    norm_rows(a_ref, 0, share, halo, gain_ref[...], normed)
    branch = branch_of(normed[...], upt_ref[...], halved(dn_ref[...]))
    first = lax.axis_index("member") * share
    made = []
    for r in range(share):
        sea = (1 - land_ref[pl.ds(first + r, 1), :]).astype(F32)
        y = mid_ref[HALO + r].astype(F32) + scale * branch[:, r * lanes : (r + 1) * lanes]
        made.append((y * sea).astype(BF))
        new_ref[r] = made[r]
    surf = jnp.dot(
        sw_ref[...], jnp.concatenate(made, axis=1), preferred_element_type=F32
    )
    for r in range(share):
        surf_ref[r] = surf[:, r * lanes : (r + 1) * lanes].astype(BF)


def ocean_block(mid, a, left, right, band, land, ready, down, surf_weight):
    share, chans, lanes = a.shape
    blocks = left.shape[0]
    return pl.pallas_call(
        ocean_kernel,
        out_shape=[
            jax.ShapeDtypeStruct((share, chans, lanes), BF),
            jax.ShapeDtypeStruct((share, surf_weight.shape[0], lanes), BF),
        ],
        in_specs=[VMEM] * 12,
        out_specs=[VMEM] * 2,
        scratch_shapes=[
            pltpu.VMEM((TAPS - 1, SPAN, chans, lanes), BF),
            pltpu.VMEM((blocks, chans, lanes), F32),
            pltpu.VMEM((chans, share * lanes), BF),
        ],
        compiler_params=params(24),
        name="ocean_block",
    )(mid, a, left, right, band, land, *ready, down, surf_weight)


def pair_kernel(own_ref, got_ref, out_ref):
    out_ref[0] = own_ref[...]
    out_ref[1] = got_ref[...]


def make_pair(own, got):
    return pl.pallas_call(
        pair_kernel,
        out_shape=jax.ShapeDtypeStruct((2,) + own.shape, BF),
        in_specs=[VMEM] * 2,
        out_specs=VMEM,
        compiler_params=params(24),
        name="surface_pair",
    )(own, got)


def couple_kernel(k, y_ref, land_ref, bw_ref, pair_ref, *refs):
    o_ref, buf, sems = refs[-3:]
    chans, lanes = y_ref.shape[1:]
    share = pair_ref.shape[1]
    rank = lax.axis_index("member")
    parity = rank % 2
    first = ((rank // 2) ^ k) * 2 * share
    surf = [pair_ref[side ^ parity, r] for side in range(2) for r in range(share)]
    back = jnp.dot(bw_ref[...], jnp.concatenate(surf, axis=1), preferred_element_type=F32)
    copies = []
    for side in range(2):
        for r in range(side * share, (side + 1) * share):
            sea = (1 - land_ref[pl.ds(first + r, 1), :]).astype(F32)
            out = y_ref[first + r].astype(F32) + sea * back[:, r * lanes : (r + 1) * lanes]
            buf[r] = out.astype(BF)
        copies.append(
            pltpu.make_async_copy(
                buf.at[pl.ds(side * share, share)],
                o_ref.at[pl.ds(first + side * share, share)],
                sems.at[side],
            )
        )
        copies[side].start()
    for copy in copies:
        copy.wait()


def couple(k, y, land, back_weight, pair, earlier):
    _, chans, lanes = y.shape
    return pl.pallas_call(
        functools.partial(couple_kernel, k),
        out_shape=jax.ShapeDtypeStruct(y.shape, BF),
        in_specs=[VMEM] * 4 + [HBM] * len(earlier),
        out_specs=HBM,
        scratch_shapes=[
            pltpu.VMEM((2 * pair.shape[1], chans, lanes), BF),
            pltpu.SemaphoreType.DMA((2,)),
        ],
        input_output_aliases={4: 0} if earlier else {},
        compiler_params=params(24),
        name="couple",
    )(y, land, back_weight, pair, *earlier)


def local(
    atmos,
    ocean,
    land_mask,
    ice_mask,
    atm_kernel,
    atm_gain,
    atm_up,
    atm_down,
    atm_scale,
    flux_weight,
    flux_lift,
    ocn_kernel,
    ocn_gain,
    ocn_up,
    ocn_down,
    ocn_scale,
    surf_weight,
    back_weight,
):
    members = lax.axis_size("member")
    half = members // 2
    state = atmos[0]
    rows = state.shape[0]
    blocks = rows // SLOTS
    big, small = 4 * blocks, 2 * blocks
    atm = (atm_gain, atm_up, atm_down.transpose(0, 2, 1), atm_scale)
    taps = atm_kernel.transpose(1, 2, 0, 3)

    edges = neighbours(pack(state, big))
    a, band = convolve(0, state, taps, blocks)
    state, packed = atmos_block(0, members, state, a, edges, band, atm, small)

    edges = neighbours(packed)
    a, band = convolve(1, state, taps, blocks)
    state, keep, give = atmos_block(
        1, members, state, a, edges, band, (*atm, flux_weight.T), small
    )
    got = send_xor(give, 1)
    sums = add_pairs(keep, got, 1)
    sent = [send_xor(sums[k - 1], 2 * k) for k in range(half - 1, 0, -1)]
    band, *ready = prepare_ocean(ocn_kernel, ocn_gain, ocn_up, ocn_scale, sums[0])
    sent = [keep, got] + sent

    mid, packed = force(members, sent, ocean, land_mask, ice_mask, flux_lift)
    left, right = neighbours(packed)
    a = ocean_conv(mid, band)
    ocean_rows, surface = ocean_block(
        mid, a, left, right, band, land_mask, ready, ocn_down.T, surf_weight.T
    )
    own = make_pair(surface, send_xor(surface, 1))
    pairs = [own] + [send_xor(own, 2 * k) for k in range(1, half)]
    out = []
    for k, pair in enumerate(pairs):
        out = [couple(k, state, land_mask, back_weight.T, pair, out)]
    out = out[0]
    return (out[None], ocean_rows)


def solution(mesh):
    in_specs = (
        P("member", None, None, "lon"),
        P(None, None, "lon"),
        P(None, "lon"),
        P(None, "lon"),
    ) + (P(),) * 14
    out_specs = (P("member", None, None, "lon"), P("member", None, "lon"))
    return jax.shard_map(local, mesh=mesh, in_specs=in_specs, out_specs=out_specs, check_vma=False)
```

```python
import functools

import jax
import jax.numpy as jnp
from jax import lax
from jax.experimental import pallas as pl
from jax.experimental.pallas import tpu as pltpu
from jax.sharding import PartitionSpec as P

BF = jnp.bfloat16
F32 = jnp.float32
TANH_A = 0.7978845608028654
TANH_B = TANH_A * 0.044715
TAPS = 7
HALO = 3
GROUP = 16
SPAN = 16
OUT = SPAN - TAPS + 1
DEPTH = GROUP * SPAN
SLOT = 8
SLOTS = 16
OCEAN_BLOCKS = 2
BIG = 32
VMEM = pl.BlockSpec(memory_space=pltpu.VMEM)
ANY = pl.BlockSpec(memory_space=pl.ANY)
HBM = pl.BlockSpec(memory_space=pltpu.HBM)


def params(mib):
    return pltpu.CompilerParams(vmem_limit_bytes=mib * 2**20)


def cost(gflop):
    return pl.CostEstimate(flops=int(gflop * 1e9), bytes_accessed=0, transcendentals=0)


def twice_gelu(z):
    return z + z * jnp.tanh(z * (TANH_A + TANH_B * (z * z)))


def transposed(value):
    return value.astype(F32).T.astype(BF)


def halved(value):
    return (0.5 * value.astype(F32)).astype(BF)


def spread(row, lanes):
    return jnp.broadcast_to(row.T, (row.shape[1], lanes))


def edge_lanes(shape):
    lane = lax.broadcasted_iota(jnp.int32, shape, len(shape) - 1)
    return (lane < HALO) | (lane >= shape[-1] - HALO)


def pack_kernel(step, src_ref, p_ref, x_ref, sems):
    rows, chans, lanes = x_ref.shape
    blocks = p_ref.shape[0]
    copies = []
    for n in range(rows // step):
        at = slice(n * step, (n + 1) * step)
        copies.append(pltpu.make_async_copy(src_ref.at[at], x_ref.at[at], sems.at[n]))
        copies[n].start()
    keep = edge_lanes((chans, lanes)).astype(F32).astype(BF)
    for n in range(rows // step):
        copies[n].wait()
        for q in range(blocks):
            total = None if n == 0 else p_ref[q]
            for slot in range(n * step // blocks, (n + 1) * step // blocks):
                moved = x_ref[slot * blocks + q] * keep
                if slot:
                    moved = pltpu.roll(moved, SLOT * slot, 1)
                total = moved if total is None else total + moved
            p_ref[q] = total


def pack(x, step):
    rows, chans, lanes = x.shape
    return pl.pallas_call(
        functools.partial(pack_kernel, step),
        out_shape=jax.ShapeDtypeStruct((rows // SLOTS, chans, lanes), BF),
        in_specs=[HBM],
        out_specs=VMEM,
        scratch_shapes=[pltpu.VMEM(x.shape, BF), pltpu.SemaphoreType.DMA((rows // step,))],
        compiler_params=params(60),
        name="pack_edges",
    )(x)


def neighbours(packed):
    count = lax.axis_size("lon")
    first = lax.ppermute(packed, "lon", [(i, i ^ 1) for i in range(count)])
    second = lax.ppermute(
        packed, "lon", [(i, (i - 1) % count if i % 2 == 0 else (i + 1) % count) for i in range(count)]
    )
    return first, second


def by_side(first, second):
    even = lax.axis_index("lon") % 2 == 0
    return jnp.where(even, second, first), jnp.where(even, first, second)


def fill_base(taps, base):
    groups, _, wide = base.shape
    chans = groups * GROUP
    tall = TAPS * SLOT
    t = lax.broadcasted_iota(jnp.int32, (tall, wide), 0)
    n = lax.broadcasted_iota(jnp.int32, (tall, wide), 1)
    hit = (t % SLOT == n // DEPTH) & (t // SLOT == (n % DEPTH) // GROUP)
    columns = []
    for i in range(TAPS):
        columns.append(taps(i).T)
        columns.append(jnp.zeros((chans, SLOT - TAPS), F32))
    columns = jnp.concatenate(columns, axis=1).astype(BF)
    total = jnp.dot(columns, hit.astype(F32).astype(BF), preferred_element_type=F32)
    r = lax.broadcasted_iota(jnp.int32, (GROUP, wide), 0)
    c = lax.broadcasted_iota(jnp.int32, (GROUP, wide), 1)
    same = r == c % GROUP
    for g in range(groups):
        base[g] = jnp.where(same, total[GROUP * g : GROUP * (g + 1)], 0.0)


def fill_band(base, g, band):
    for j in range(TAPS):
        one = base[g, :, j * DEPTH : (j + 1) * DEPTH]
        for r in range(OUT):
            moved = pltpu.roll(one, GROUP * r, 1) if r else one
            band[GROUP * r : GROUP * (r + 1), j * DEPTH : (j + 1) * DEPTH] = moved.astype(BF)


def fill_shifts(x, pad, xj):
    count, _, lanes = x.shape
    lane = lax.broadcasted_iota(jnp.int32, (GROUP, lanes), 1)
    for j in range(TAPS):
        d = j - HALO
        if d:
            keep = ((lane < lanes - d) if d > 0 else (lane >= -d)).astype(F32).astype(BF)
            xj[j, pad : pad + count] = pltpu.roll(x, (-d) % lanes, 2) * keep[None]
        else:
            xj[j, pad : pad + count] = x


def clear_pads(pad, count, xj):
    tall, _, lanes = xj.shape[1:]
    for j in range(TAPS):
        if pad:
            xj[j, :pad] = jnp.zeros((pad, GROUP, lanes), BF)
        if tall > pad + count:
            xj[j, pad + count :] = jnp.zeros((tall - pad - count, GROUP, lanes), BF)


def apply_band(band, xj, a_ref):
    rows, _, lanes = a_ref.shape
    starts = [min(OUT * i, max(rows - OUT, 0)) for i in range(-(-rows // OUT))]
    field = jnp.concatenate(
        [
            jnp.concatenate([xj[j, s : s + SPAN].reshape(DEPTH, lanes) for j in range(TAPS)], axis=0)
            for s in starts
        ],
        axis=1,
    )
    out = jnp.dot(band, field, preferred_element_type=F32)
    take = min(OUT, rows)
    for n, s in enumerate(starts):
        part = out[: take * GROUP, n * lanes : (n + 1) * lanes]
        a_ref[s : s + take] = part.reshape(take, GROUP, lanes)


def conv_kernel(layer, x_ref, k_ref, a_ref, band_ref, base, even_xj, odd_xj, even_band, odd_band):
    rows, chans, lanes = x_ref.shape
    groups = chans // GROUP
    fill_base(lambda i: k_ref[i, :, layer, :], base)
    clear_pads(HALO, rows, even_xj)
    clear_pads(HALO, rows, odd_xj)

    def at(g):
        return pl.ds(pl.multiple_of(GROUP * g, GROUP), GROUP)

    def prepare(g, xj, band):
        fill_band(base, g, band)
        band_ref[g] = band[: band_ref.shape[1]]
        fill_shifts(x_ref[:, at(g), :], HALO, xj)

    prepare(0, even_xj, even_band)

    def pair(i, carry):
        prepare(2 * i + 1, odd_xj, odd_band)
        apply_band(even_band[...], even_xj, a_ref.at[:, at(2 * i), :])
        prepare(jnp.minimum(2 * i + 2, groups - 1), even_xj, even_band)
        apply_band(odd_band[...], odd_xj, a_ref.at[:, at(2 * i + 1), :])
        return carry

    lax.fori_loop(0, groups // 2, pair, 0)


def convolve(layer, x, taps, blocks):
    rows, chans, lanes = x.shape
    groups = chans // GROUP
    wide = TAPS * DEPTH
    return pl.pallas_call(
        functools.partial(conv_kernel, layer),
        out_shape=[
            jax.ShapeDtypeStruct((rows, chans, lanes), F32),
            jax.ShapeDtypeStruct((groups, blocks * GROUP, wide), BF),
        ],
        in_specs=[VMEM, VMEM],
        out_specs=[VMEM, VMEM],
        scratch_shapes=[
            pltpu.VMEM((groups, GROUP, wide), F32),
        ]
        + [pltpu.VMEM((TAPS, rows + 2 * HALO, GROUP, lanes), BF)] * 2
        + [pltpu.VMEM((GROUP * OUT, wide), BF)] * 2,
        compiler_params=params(BIG),
        cost_estimate=cost(8),
        name="conv",
    )(x, taps)


def prepare_kernel(k_ref, g_ref, up_ref, s_ref, _, band_ref, mat_ref, upt_ref, gain_ref, scale_ref, base):
    lanes = gain_ref.shape[1]
    mat_ref[...] = halo_matrix(lanes)
    upt_ref[...] = transposed(up_ref[...])
    gain_ref[...] = spread(g_ref[...], lanes)
    scale_ref[...] = spread(s_ref[...], lanes)
    fill_base(lambda i: k_ref[i], base)
    for g in range(base.shape[0]):
        fill_band(base, g, band_ref.at[g])


def prepare_ocean(taps, gain, up, scale, after):
    chans, hid = up.shape
    lanes = after.shape[-1]
    groups = chans // GROUP
    wide = TAPS * DEPTH
    return pl.pallas_call(
        prepare_kernel,
        out_shape=[
            jax.ShapeDtypeStruct((groups, GROUP * OUT, wide), BF),
            jax.ShapeDtypeStruct((2 * lanes, (TAPS - 1) * lanes), BF),
            jax.ShapeDtypeStruct((hid, chans), BF),
            jax.ShapeDtypeStruct((chans, lanes), F32),
            jax.ShapeDtypeStruct((chans, lanes), F32),
        ],
        in_specs=[VMEM] * 4 + [ANY],
        out_specs=[VMEM] * 5,
        scratch_shapes=[pltpu.VMEM((groups, GROUP, wide), F32)],
        compiler_params=params(24),
        cost_estimate=cost(3),
        name="prepare_ocean",
    )(taps, gain[None], up, scale[None], after)


def ocean_conv_kernel(x_ref, band_ref, a_ref, xj):
    count, chans, lanes = x_ref.shape
    for g in range(chans // GROUP):
        at = slice(GROUP * g, GROUP * (g + 1))
        clear_pads(0, count, xj.at[g])
        fill_shifts(x_ref[:, at, :], 0, xj.at[g])
        apply_band(band_ref[g], xj.at[g], a_ref.at[:, at, :])


def ocean_conv(x, band):
    count, chans, lanes = x.shape
    return pl.pallas_call(
        ocean_conv_kernel,
        out_shape=jax.ShapeDtypeStruct((count - 2 * HALO, chans, lanes), F32),
        in_specs=[VMEM, VMEM],
        out_specs=VMEM,
        scratch_shapes=[pltpu.VMEM((chans // GROUP, TAPS, max(count, SPAN), GROUP, lanes), BF)],
        compiler_params=params(24),
        cost_estimate=cost(2),
        name="ocean_conv",
    )(x, band)


def halo_matrix(lanes):
    shape = (lanes, lanes)
    src = lax.broadcasted_iota(jnp.int32, shape, 0)
    dst = lax.broadcasted_iota(jnp.int32, shape, 1)
    ahead = (src - dst + lanes) % lanes
    right = (src % SLOT < HALO) & (dst % SLOT >= SLOT - HALO)
    left = (src % SLOT >= SLOT - HALO) & (dst % SLOT < HALO)
    right = jnp.where(right, ahead, -1)
    left = jnp.where(left, ahead, -1)
    none = jnp.zeros(shape, BF)
    upper, lower = [], []
    for j in range(TAPS):
        d = j - HALO
        if d > 0:
            upper.append((right == d).astype(F32).astype(BF))
            lower.append(none)
        elif d < 0:
            upper.append(none)
            lower.append((left == lanes + d).astype(F32).astype(BF))
    return jnp.concatenate(
        [jnp.concatenate(upper, axis=1), jnp.concatenate(lower, axis=1)], axis=0
    )


def halo_conv(first, second, band, wrapped, matrix, xe, halo):
    blocks, chans, lanes = halo.shape
    wide = TAPS * DEPTH
    both = []
    for q in range(blocks):
        left, right = by_side(first[q], second[q])
        both.append(jnp.concatenate([right, left], axis=1))
    lane = lax.broadcasted_iota(jnp.int32, (chans, lanes), 1)
    slot = (lane + HALO) // SLOT % SLOTS

    def turned(value, shift, drop):
        parts = [pltpu.roll(value[:, n * lanes : (n + 1) * lanes], shift, 1) for n in range(2)]
        if drop >= 0:
            keep = (slot != drop).astype(F32).astype(BF)
            parts = [part * keep for part in parts]
        return jnp.concatenate(parts, axis=1)

    if wrapped:
        tall = (
            [turned(both[q], SLOT, 0) for q in range(blocks - HALO, blocks)]
            + both
            + [turned(both[q], lanes - SLOT, SLOTS - 1) for q in range(HALO)]
        )
    else:
        tall = both + [
            turned(both[e % blocks], lanes - SLOT * (e // blocks), -1)
            for e in range(blocks, blocks + 2 * HALO)
        ]
    field = jnp.concatenate(tall, axis=0)
    moved = jnp.dot(field, matrix, preferred_element_type=F32)
    count = len(tall)
    for a in range(TAPS - 1):
        part = moved[:, a * lanes : (a + 1) * lanes].astype(BF)
        xe[a, :count] = part.reshape(count, chans, lanes)
        xe[a, count:] = jnp.zeros((SPAN - count, chans, lanes), BF)
    low = HALO * DEPTH
    for g in range(chans // GROUP):
        at = slice(GROUP * g, GROUP * (g + 1))
        rhs = jnp.concatenate([xe[a, :, at, :].reshape(DEPTH, lanes) for a in range(TAPS - 1)], axis=0)
        tops = slice(0, blocks * GROUP)
        lhs = jnp.concatenate([band[g, tops, :low], band[g, tops, low + DEPTH : wide]], axis=1)
        out = jnp.dot(lhs, rhs, preferred_element_type=F32)
        halo[:, at, :] = out.reshape(blocks, GROUP, lanes)


def turned_by(value, slots):
    lanes = value.shape[-1]
    if isinstance(slots, int):
        shift = SLOT * slots % lanes
        return pltpu.roll(value, shift, 1) if shift else value
    return pltpu.roll(value, lax.rem(SLOT * slots + lanes, lanes), 1)


def norm_rows(a_ref, base, off, count, halo, gain, out):
    _, chans, lanes = a_ref.shape
    blocks = halo.shape[0]
    edge = edge_lanes((chans, lanes))
    for r in range(count):
        extra = turned_by(halo[(off + r) % blocks], -(base // blocks + (off + r) // blocks))
        a = a_ref[base + off + r] + jnp.where(edge, extra, 0.0)
        center = a - jnp.mean(a, axis=0, keepdims=True)
        var = jnp.mean(center * center, axis=0, keepdims=True)
        normed = (center * lax.rsqrt(var + 1e-06) * gain).astype(BF)
        out[:, r * lanes : (r + 1) * lanes] = normed


def branch_of(normed, up_t, down_t):
    z = jnp.dot(up_t, normed, preferred_element_type=F32)
    h = twice_gelu(z.astype(BF))
    return jnp.dot(down_t, h, preferred_element_type=F32)


def atmos_kernel(layer, near, members, count, steps, *refs):
    x_ref, a_ref, g_ref, up_ref, dn_ref, s_ref = refs[:6]
    refs = refs[6:]
    even, odd = refs[-2:]
    rows, chans, lanes = x_ref.shape
    base = 0
    if layer == 0:
        first_ref, second_ref, band_ref, y_ref, p_ref, xe, halo = refs[:-2]
        blocks = halo.shape[0]
        packed = [None] * blocks
        keep = edge_lanes((chans, lanes)).astype(F32).astype(BF)
    else:
        rank = lax.axis_index("member")
        half = members // 2
        upper = (rank >= half) if near else (rank < half)
        base = jnp.where(upper, rows - steps * count, 0)
        if near:
            fw_ref, _, old_ref, halo, y_ref, keep_ref, give_ref, flux = refs[:-2]
        else:
            fw_ref, first_ref, second_ref, band_ref = refs[:4]
            y_ref, keep_ref, give_ref, flux, halo, xe = refs[4:-2]
    if near:
        flux[...] = old_ref[...]
    else:
        halo_conv(first_ref, second_ref, band_ref, True, halo_matrix(lanes), xe, halo)
        if layer == 1:
            blank = jnp.zeros((HALO,) + flux.shape[1:], BF)
            flux[0:HALO] = blank
            flux[rows + HALO : rows + 2 * HALO] = blank
    up_t = transposed(up_ref[layer])
    dn_t = halved(dn_ref[layer])
    gain = spread(g_ref[layer : layer + 1], lanes)
    scale = spread(s_ref[layer : layer + 1], lanes)
    norm_rows(a_ref, base, 0, count, halo, gain, even)
    for step in range(steps):
        off = step * count
        now, later = (even, odd) if step % 2 == 0 else (odd, even)
        if step + 1 < steps:
            norm_rows(a_ref, base, off + count, count, halo, gain, later)
        branch = branch_of(now[...], up_t, dn_t)
        made = []
        for r in range(count):
            y = x_ref[base + off + r].astype(F32) + scale * branch[:, r * lanes : (r + 1) * lanes]
            made.append(y.astype(BF))
            y_ref[base + off + r] = made[r]
        if layer == 0:
            for r in range(count):
                q, slot = (off + r) % blocks, (off + r) // blocks
                moved = turned_by(made[r] * keep, slot)
                packed[q] = moved if packed[q] is None else packed[q] + moved
            if step % 4 == 3 or step + 1 == steps:
                for q in range(blocks):
                    p_ref[q] = packed[q] if step < 4 else p_ref[q] + packed[q]
                packed = [None] * blocks
        else:
            z = jnp.dot(fw_ref[...], jnp.concatenate(made, axis=1), preferred_element_type=F32)
            f = (0.5 * twice_gelu(z)).astype(BF)
            for r in range(count):
                flux[base + off + HALO + r] = f[:, r * lanes : (r + 1) * lanes]
    if layer == 1:
        share = rows // members
        for k in range(half):
            dst = rank ^ (k if near else half + k)
            chunk = flux[pl.ds(dst * share, share + 2 * HALO)]
            if k % 2:
                give_ref[k // 2] = chunk
            else:
                keep_ref[k // 2] = chunk


def atmos_block(layer, near, members, x, a, weights, others, count, steps):
    rows, chans, lanes = x.shape
    blocks = rows // SLOTS
    args = [x, a, *weights, *others]
    outs = [jax.ShapeDtypeStruct(x.shape, BF)]
    halo = jax.ShapeDtypeStruct((blocks, chans, lanes), F32)
    shifts = pltpu.VMEM((TAPS - 1, SPAN, chans, lanes), BF)
    if layer == 0:
        outs.append(jax.ShapeDtypeStruct((blocks, chans, lanes), BF))
        scratch = [shifts, pltpu.VMEM(halo.shape, F32)]
    else:
        flux = weights[-1].shape[0]
        share = rows // members
        field = (rows + 2 * HALO, flux, lanes)
        outs += [jax.ShapeDtypeStruct((members // 4, share + 2 * HALO, flux, lanes), BF)] * 2
        if near:
            scratch = [pltpu.VMEM(field, BF)]
        else:
            outs += [jax.ShapeDtypeStruct(field, BF), halo]
            scratch = [shifts]
    return pl.pallas_call(
        functools.partial(atmos_kernel, layer, near, members, count, steps),
        out_shape=outs,
        in_specs=[VMEM] * len(args),
        out_specs=[VMEM] * len(outs),
        scratch_shapes=scratch + [pltpu.VMEM((chans, count * lanes), BF)] * 2,
        input_output_aliases={7: 0} if near else {},
        compiler_params=params(BIG),
        cost_estimate=cost(8 * steps * count / rows),
        name="atmos_block",
    )(*args)


def add_kernel(keep_ref, got_ref, *out_refs):
    for n, ref in enumerate(out_refs):
        k = n + keep_ref.shape[0] - len(out_refs)
        ref[...] = (keep_ref[k].astype(F32) + got_ref[k].astype(F32)).astype(BF)


def add_pairs(keep, got, skip):
    count = keep.shape[0] - skip
    return pl.pallas_call(
        add_kernel,
        out_shape=[jax.ShapeDtypeStruct(keep.shape[1:], BF)] * count,
        in_specs=[VMEM] * 2,
        out_specs=[VMEM] * count,
        compiler_params=params(24),
        name="add_pairs",
    )(keep, got)


def send_xor(value, bits):
    members = lax.axis_size("member")
    return lax.ppermute(value, "member", [(i, i ^ bits) for i in range(members)])


def force_kernel(members, *refs):
    near_refs, flux_refs = refs[:2], refs[2 : members // 2 + 1]
    ocean_ref, land_ref, ice_ref, lift_ref, mid_ref, p_ref, win, sem = refs[members // 2 + 1 :]
    span, flux, lanes = flux_refs[0].shape
    rows = land_ref.shape[0]
    chans = mid_ref.shape[1]
    share = rows // members
    blocks = p_ref.shape[0]
    first = lax.axis_index("member") * share - HALO
    start = jnp.clip(first, 0, rows - span)
    copy = pltpu.make_async_copy(ocean_ref.at[pl.ds(start, span)], win, sem)
    copy.start()
    total = near_refs[0][0].astype(F32) + near_refs[1][0].astype(F32)
    for ref in flux_refs:
        total = total + ref[...].astype(F32)
    low = (total / members).astype(BF)
    lift = jnp.concatenate([transposed(lift_ref[0]), transposed(lift_ref[1])], axis=0)
    terms = jnp.dot(
        lift, jnp.concatenate([low[r] for r in range(span)], axis=1), preferred_element_type=F32
    )
    keep = edge_lanes((chans, lanes)).astype(F32).astype(BF)
    packed = [None] * blocks
    copy.wait()
    for r in range(span):
        row = first + r
        safe = jnp.clip(row, 0, rows - 1)
        sea = (1 - land_ref[pl.ds(safe, 1), :]).astype(F32)
        ice = ice_ref[pl.ds(safe, 1), :].astype(F32)
        at = slice(r * lanes, (r + 1) * lanes)
        forcing = sea * ((1.0 - ice) * terms[:chans, at] + ice * terms[chans:, at])
        mid = win[jnp.clip(row - start, 0, span - 1)].astype(F32) + forcing
        inside = (row >= 0) & (row < rows)
        mid = jnp.where(inside, mid, 0.0).astype(BF)
        mid_ref[r] = mid
        q, slot = r % blocks, r // blocks
        moved = mid * keep
        if slot:
            moved = pltpu.roll(moved, SLOT * slot, 1)
        packed[q] = moved if packed[q] is None else packed[q] + moved
    for q in range(blocks):
        p_ref[q] = packed[q]


def force(members, chunks, ocean, land, ice, lift):
    span, _, lanes = chunks[-1].shape
    rows, chans, _ = ocean.shape
    return pl.pallas_call(
        functools.partial(force_kernel, members),
        out_shape=[
            jax.ShapeDtypeStruct((span, chans, lanes), BF),
            jax.ShapeDtypeStruct((OCEAN_BLOCKS, chans, lanes), BF),
        ],
        in_specs=[VMEM] * len(chunks) + [HBM, VMEM, VMEM, VMEM],
        out_specs=[VMEM] * 2,
        scratch_shapes=[pltpu.VMEM((span, chans, lanes), BF), pltpu.SemaphoreType.DMA(())],
        compiler_params=params(24),
        name="ocean_forcing",
    )(*chunks, ocean, land, ice, lift)


def ocean_kernel(mid_ref, a_ref, left_ref, right_ref, band_ref, land_ref, mat_ref, upt_ref, gain_ref, scale_ref, dn_ref, sw_ref, new_ref, surf_ref, xe, halo, normed):
    share, chans, lanes = new_ref.shape
    halo_conv(left_ref, right_ref, band_ref, False, mat_ref[...], xe, halo)
    scale = scale_ref[...]
    norm_rows(a_ref, 0, 0, share, halo, gain_ref[...], normed)
    branch = branch_of(normed[...], upt_ref[...], halved(dn_ref[...]))
    first = lax.axis_index("member") * share
    made = []
    for r in range(share):
        sea = (1 - land_ref[pl.ds(first + r, 1), :]).astype(F32)
        y = mid_ref[HALO + r].astype(F32) + scale * branch[:, r * lanes : (r + 1) * lanes]
        made.append((y * sea).astype(BF))
        new_ref[r] = made[r]
    surf = jnp.dot(
        sw_ref[...], jnp.concatenate(made, axis=1), preferred_element_type=F32
    )
    for r in range(share):
        surf_ref[r] = surf[:, r * lanes : (r + 1) * lanes].astype(BF)


def ocean_block(mid, a, left, right, band, land, ready, down, surf_weight):
    share, chans, lanes = a.shape
    blocks = left.shape[0]
    return pl.pallas_call(
        ocean_kernel,
        out_shape=[
            jax.ShapeDtypeStruct((share, chans, lanes), BF),
            jax.ShapeDtypeStruct((share, surf_weight.shape[0], lanes), BF),
        ],
        in_specs=[VMEM] * 12,
        out_specs=[VMEM] * 2,
        scratch_shapes=[
            pltpu.VMEM((TAPS - 1, SPAN, chans, lanes), BF),
            pltpu.VMEM((blocks, chans, lanes), F32),
            pltpu.VMEM((chans, share * lanes), BF),
        ],
        compiler_params=params(24),
        name="ocean_block",
    )(mid, a, left, right, band, land, *ready, down, surf_weight)


def pair_kernel(own_ref, got_ref, out_ref):
    out_ref[0] = own_ref[...]
    out_ref[1] = got_ref[...]


def make_pair(own, got):
    return pl.pallas_call(
        pair_kernel,
        out_shape=jax.ShapeDtypeStruct((2,) + own.shape, BF),
        in_specs=[VMEM] * 2,
        out_specs=VMEM,
        compiler_params=params(24),
        name="surface_pair",
    )(own, got)


def couple_kernel(k, y_ref, land_ref, bw_ref, pair_ref, *refs):
    o_ref, buf, sems = refs[-3:]
    chans, lanes = y_ref.shape[1:]
    share = pair_ref.shape[1]
    rank = lax.axis_index("member")
    parity = rank % 2
    first = ((rank // 2) ^ k) * 2 * share
    surf = [pair_ref[side ^ parity, r] for side in range(2) for r in range(share)]
    back = jnp.dot(bw_ref[...], jnp.concatenate(surf, axis=1), preferred_element_type=F32)
    copies = []
    piece = share // 2
    for n in range(4):
        for r in range(n * piece, (n + 1) * piece):
            sea = (1 - land_ref[pl.ds(first + r, 1), :]).astype(F32)
            out = y_ref[first + r].astype(F32) + sea * back[:, r * lanes : (r + 1) * lanes]
            buf[r] = out.astype(BF)
        copies.append(
            pltpu.make_async_copy(
                buf.at[pl.ds(n * piece, piece)],
                o_ref.at[pl.ds(first + n * piece, piece)],
                sems.at[n],
            )
        )
        copies[n].start()
    for copy in copies:
        copy.wait()


def couple(k, y, land, back_weight, pair, earlier):
    _, chans, lanes = y.shape
    return pl.pallas_call(
        functools.partial(couple_kernel, k),
        out_shape=jax.ShapeDtypeStruct(y.shape, BF),
        in_specs=[VMEM] * 4 + [HBM] * len(earlier),
        out_specs=HBM,
        scratch_shapes=[
            pltpu.VMEM((2 * pair.shape[1], chans, lanes), BF),
            pltpu.SemaphoreType.DMA((4,)),
        ],
        input_output_aliases={4: 0} if earlier else {},
        compiler_params=params(24),
        name="couple",
    )(y, land, back_weight, pair, *earlier)


def local(
    atmos,
    ocean,
    land_mask,
    ice_mask,
    atm_kernel,
    atm_gain,
    atm_up,
    atm_down,
    atm_scale,
    flux_weight,
    flux_lift,
    ocn_kernel,
    ocn_gain,
    ocn_up,
    ocn_down,
    ocn_scale,
    surf_weight,
    back_weight,
):
    members = lax.axis_size("member")
    half = members // 2
    state = atmos[0]
    rows = state.shape[0]
    blocks = rows // SLOTS
    big, small = 4 * blocks, 2 * blocks
    atm = (atm_gain, atm_up, atm_down.transpose(0, 2, 1), atm_scale)
    taps = atm_kernel.transpose(1, 2, 0, 3)

    edges = neighbours(pack(state, big))
    a, band = convolve(0, state, taps, blocks)
    steps = rows // small
    near_steps = (rows // 2) // small - 1
    state, packed = atmos_block(0, False, members, state, a, atm, [*edges, band], small, steps)

    edges = neighbours(packed)
    a, band = convolve(1, state, taps, blocks)
    weights = (*atm, flux_weight.T)
    partly, far_keep, give, flux, halo = atmos_block(
        1, False, members, state, a, weights, [*edges, band], small, steps - near_steps
    )
    far_got = send_xor(give, 1)
    state, keep, give = atmos_block(
        1, True, members, state, a, weights, [partly, flux, halo], small, near_steps
    )
    far_got, give = lax.optimization_barrier((far_got, give))
    far_sums = add_pairs(far_keep, far_got, 0)
    give, *far_sums = lax.optimization_barrier((give, *far_sums))
    sent = [send_xor(far_sums[k], half + 2 * k) for k in reversed(range(len(far_sums)))]
    got = send_xor(give, 1)
    sums = add_pairs(keep, got, 1)
    sent += [send_xor(part, 2 * k + 2) for k, part in enumerate(sums)]
    band, *ready = prepare_ocean(ocn_kernel, ocn_gain, ocn_up, ocn_scale, sums[0])
    sent = [keep, got] + sent
    mid, packed = force(members, sent, ocean, land_mask, ice_mask, flux_lift)
    left, right = neighbours(packed)
    a = ocean_conv(mid, band)
    ocean_rows, surface = ocean_block(
        mid, a, left, right, band, land_mask, ready, ocn_down.T, surf_weight.T
    )
    own = make_pair(surface, send_xor(surface, 1))
    pairs = [own] + [send_xor(own, 2 * k) for k in range(1, half)]
    out = []
    for k, pair in enumerate(pairs):
        out = [couple(k, state, land_mask, back_weight.T, pair, out)]
    out = out[0]
    return (out[None], ocean_rows)


def solution(mesh):
    in_specs = (
        P("member", None, None, "lon"),
        P(None, None, "lon"),
        P(None, "lon"),
        P(None, "lon"),
    ) + (P(),) * 14
    out_specs = (P("member", None, None, "lon"), P("member", None, "lon"))
    return jax.shard_map(local, mesh=mesh, in_specs=in_specs, out_specs=out_specs, check_vma=False)
```

```python
import functools

import jax
import jax.numpy as jnp
from jax import lax
from jax.experimental import pallas as pl
from jax.experimental.pallas import tpu as pltpu
from jax.sharding import PartitionSpec as P

BF = jnp.bfloat16
F32 = jnp.float32
TANH_A = 0.7978845608028654
TANH_B = TANH_A * 0.044715
TAPS = 7
HALO = 3
GROUP = 16
SPAN = 16
OUT = SPAN - TAPS + 1
DEPTH = GROUP * SPAN
SLOT = 8
SLOTS = 16
OCEAN_BLOCKS = 2
BIG = 32
VMEM = pl.BlockSpec(memory_space=pltpu.VMEM)
ANY = pl.BlockSpec(memory_space=pl.ANY)
HBM = pl.BlockSpec(memory_space=pltpu.HBM)


def params(mib):
    return pltpu.CompilerParams(vmem_limit_bytes=mib * 2**20)


def cost(gflop):
    return pl.CostEstimate(flops=int(gflop * 1e9), bytes_accessed=0, transcendentals=0)


def twice_gelu(z):
    return z + z * jnp.tanh(z * (TANH_A + TANH_B * (z * z)))


def transposed(value):
    return value.astype(F32).T.astype(BF)


def halved(value):
    return (0.5 * value.astype(F32)).astype(BF)


def spread(row, lanes):
    return jnp.broadcast_to(row.T, (row.shape[1], lanes))


def edge_lanes(shape):
    lane = lax.broadcasted_iota(jnp.int32, shape, len(shape) - 1)
    return (lane < HALO) | (lane >= shape[-1] - HALO)


def pack_kernel(step, src_ref, p_ref, x_ref, sems):
    rows, chans, lanes = x_ref.shape
    blocks = p_ref.shape[0]
    copies = []
    for n in range(rows // step):
        at = slice(n * step, (n + 1) * step)
        copies.append(pltpu.make_async_copy(src_ref.at[at], x_ref.at[at], sems.at[n]))
        copies[n].start()
    keep = edge_lanes((chans, lanes)).astype(F32).astype(BF)
    for n in range(rows // step):
        copies[n].wait()
        for q in range(blocks):
            total = None if n == 0 else p_ref[q]
            for slot in range(n * step // blocks, (n + 1) * step // blocks):
                moved = x_ref[slot * blocks + q] * keep
                if slot:
                    moved = pltpu.roll(moved, SLOT * slot, 1)
                total = moved if total is None else total + moved
            p_ref[q] = total


def pack(x, step):
    rows, chans, lanes = x.shape
    return pl.pallas_call(
        functools.partial(pack_kernel, step),
        out_shape=jax.ShapeDtypeStruct((rows // SLOTS, chans, lanes), BF),
        in_specs=[HBM],
        out_specs=VMEM,
        scratch_shapes=[pltpu.VMEM(x.shape, BF), pltpu.SemaphoreType.DMA((rows // step,))],
        compiler_params=params(60),
        name="pack_edges",
    )(x)


def neighbours(packed):
    count = lax.axis_size("lon")
    first = lax.ppermute(packed, "lon", [(i, i ^ 1) for i in range(count)])
    second = lax.ppermute(
        packed, "lon", [(i, (i - 1) % count if i % 2 == 0 else (i + 1) % count) for i in range(count)]
    )
    return first, second


def by_side(first, second):
    even = lax.axis_index("lon") % 2 == 0
    return jnp.where(even, second, first), jnp.where(even, first, second)


def fill_base(taps, base):
    groups, _, wide = base.shape
    chans = groups * GROUP
    tall = TAPS * SLOT
    t = lax.broadcasted_iota(jnp.int32, (tall, wide), 0)
    n = lax.broadcasted_iota(jnp.int32, (tall, wide), 1)
    hit = (t % SLOT == n // DEPTH) & (t // SLOT == (n % DEPTH) // GROUP)
    columns = []
    for i in range(TAPS):
        columns.append(taps(i).T)
        columns.append(jnp.zeros((chans, SLOT - TAPS), F32))
    columns = jnp.concatenate(columns, axis=1).astype(BF)
    total = jnp.dot(columns, hit.astype(F32).astype(BF), preferred_element_type=F32)
    r = lax.broadcasted_iota(jnp.int32, (GROUP, wide), 0)
    c = lax.broadcasted_iota(jnp.int32, (GROUP, wide), 1)
    same = r == c % GROUP
    for g in range(groups):
        base[g] = jnp.where(same, total[GROUP * g : GROUP * (g + 1)], 0.0)


def fill_band(base, g, band):
    for j in range(TAPS):
        one = base[g, :, j * DEPTH : (j + 1) * DEPTH]
        for r in range(OUT):
            moved = pltpu.roll(one, GROUP * r, 1) if r else one
            band[GROUP * r : GROUP * (r + 1), j * DEPTH : (j + 1) * DEPTH] = moved.astype(BF)


def fill_shifts(x, pad, xj):
    count, _, lanes = x.shape
    lane = lax.broadcasted_iota(jnp.int32, (GROUP, lanes), 1)
    for j in range(TAPS):
        d = j - HALO
        if d:
            keep = ((lane < lanes - d) if d > 0 else (lane >= -d)).astype(F32).astype(BF)
            xj[j, pad : pad + count] = pltpu.roll(x, (-d) % lanes, 2) * keep[None]
        else:
            xj[j, pad : pad + count] = x


def clear_pads(pad, count, xj):
    tall, _, lanes = xj.shape[1:]
    for j in range(TAPS):
        if pad:
            xj[j, :pad] = jnp.zeros((pad, GROUP, lanes), BF)
        if tall > pad + count:
            xj[j, pad + count :] = jnp.zeros((tall - pad - count, GROUP, lanes), BF)


def apply_band(band, xj, a_ref):
    rows, _, lanes = a_ref.shape
    starts = [min(OUT * i, max(rows - OUT, 0)) for i in range(-(-rows // OUT))]
    field = jnp.concatenate(
        [
            jnp.concatenate([xj[j, s : s + SPAN].reshape(DEPTH, lanes) for j in range(TAPS)], axis=0)
            for s in starts
        ],
        axis=1,
    )
    out = jnp.dot(band, field, preferred_element_type=F32)
    take = min(OUT, rows)
    for n, s in enumerate(starts):
        part = out[: take * GROUP, n * lanes : (n + 1) * lanes]
        a_ref[s : s + take] = part.reshape(take, GROUP, lanes)


def conv_kernel(layer, x_ref, k_ref, a_ref, band_ref, base, even_xj, odd_xj, even_band, odd_band):
    rows, chans, lanes = x_ref.shape
    groups = chans // GROUP
    fill_base(lambda i: k_ref[i, :, layer, :], base)
    clear_pads(HALO, rows, even_xj)
    clear_pads(HALO, rows, odd_xj)

    def at(g):
        return pl.ds(pl.multiple_of(GROUP * g, GROUP), GROUP)

    def prepare(g, xj, band):
        fill_band(base, g, band)
        band_ref[g] = band[: band_ref.shape[1]]
        fill_shifts(x_ref[:, at(g), :], HALO, xj)

    prepare(0, even_xj, even_band)

    def pair(i, carry):
        prepare(2 * i + 1, odd_xj, odd_band)
        apply_band(even_band[...], even_xj, a_ref.at[:, at(2 * i), :])
        prepare(jnp.minimum(2 * i + 2, groups - 1), even_xj, even_band)
        apply_band(odd_band[...], odd_xj, a_ref.at[:, at(2 * i + 1), :])
        return carry

    lax.fori_loop(0, groups // 2, pair, 0)


def convolve(layer, x, taps, blocks):
    rows, chans, lanes = x.shape
    groups = chans // GROUP
    wide = TAPS * DEPTH
    return pl.pallas_call(
        functools.partial(conv_kernel, layer),
        out_shape=[
            jax.ShapeDtypeStruct((rows, chans, lanes), F32),
            jax.ShapeDtypeStruct((groups, blocks * GROUP, wide), BF),
        ],
        in_specs=[VMEM, VMEM],
        out_specs=[VMEM, VMEM],
        scratch_shapes=[
            pltpu.VMEM((groups, GROUP, wide), F32),
        ]
        + [pltpu.VMEM((TAPS, rows + 2 * HALO, GROUP, lanes), BF)] * 2
        + [pltpu.VMEM((GROUP * OUT, wide), BF)] * 2,
        compiler_params=params(BIG),
        cost_estimate=cost(8),
        name="conv",
    )(x, taps)


def window(members, rows):
    share = rows // members
    span = share + 2 * HALO
    first = lax.axis_index("member") * share - HALO
    return span, first, jnp.clip(first, 0, rows - span)


def prepare_kernel(members, k_ref, g_ref, up_ref, s_ref, lift_ref, ocean_ref, _, *refs):
    band_ref, mat_ref, upt_ref, gain_ref, scale_ref, lift_out, win_ref, base, sem = refs
    lanes = gain_ref.shape[1]
    span, _, start = window(members, ocean_ref.shape[0])
    copy = pltpu.make_async_copy(ocean_ref.at[pl.ds(start, span)], win_ref, sem)
    copy.start()
    mat_ref[...] = halo_matrix(lanes)
    upt_ref[...] = transposed(up_ref[...])
    gain_ref[...] = spread(g_ref[...], lanes)
    scale_ref[...] = spread(s_ref[...], lanes)
    lift_out[...] = jnp.concatenate([transposed(lift_ref[0]), transposed(lift_ref[1])], axis=0)
    fill_base(lambda i: k_ref[i], base)
    for g in range(base.shape[0]):
        fill_band(base, g, band_ref.at[g])
    copy.wait()


def prepare_ocean(members, taps, gain, up, scale, lift, ocean, after):
    chans, hid = up.shape
    rows, _, lanes = ocean.shape
    flux = lift.shape[1]
    groups = chans // GROUP
    wide = TAPS * DEPTH
    span = rows // members + 2 * HALO
    return pl.pallas_call(
        functools.partial(prepare_kernel, members),
        out_shape=[
            jax.ShapeDtypeStruct((groups, GROUP * OUT, wide), BF),
            jax.ShapeDtypeStruct((2 * lanes, (TAPS - 1) * lanes), BF),
            jax.ShapeDtypeStruct((hid, chans), BF),
            jax.ShapeDtypeStruct((chans, lanes), F32),
            jax.ShapeDtypeStruct((chans, lanes), F32),
            jax.ShapeDtypeStruct((2 * chans, flux), BF),
            jax.ShapeDtypeStruct((span, chans, lanes), BF),
        ],
        in_specs=[VMEM] * 5 + [HBM, ANY],
        out_specs=[VMEM] * 7,
        scratch_shapes=[pltpu.VMEM((groups, GROUP, wide), F32), pltpu.SemaphoreType.DMA(())],
        compiler_params=params(24),
        cost_estimate=cost(3),
        name="prepare_ocean",
    )(taps, gain[None], up, scale[None], lift, ocean, after)


def ocean_conv_kernel(x_ref, band_ref, a_ref, xj):
    count, chans, lanes = x_ref.shape
    for g in range(chans // GROUP):
        at = slice(GROUP * g, GROUP * (g + 1))
        clear_pads(0, count, xj.at[g])
        fill_shifts(x_ref[:, at, :], 0, xj.at[g])
        apply_band(band_ref[g], xj.at[g], a_ref.at[:, at, :])


def ocean_conv(x, band):
    count, chans, lanes = x.shape
    return pl.pallas_call(
        ocean_conv_kernel,
        out_shape=jax.ShapeDtypeStruct((count - 2 * HALO, chans, lanes), F32),
        in_specs=[VMEM, VMEM],
        out_specs=VMEM,
        scratch_shapes=[pltpu.VMEM((chans // GROUP, TAPS, max(count, SPAN), GROUP, lanes), BF)],
        compiler_params=params(24),
        cost_estimate=cost(2),
        name="ocean_conv",
    )(x, band)


def halo_matrix(lanes):
    shape = (lanes, lanes)
    src = lax.broadcasted_iota(jnp.int32, shape, 0)
    dst = lax.broadcasted_iota(jnp.int32, shape, 1)
    ahead = (src - dst + lanes) % lanes
    right = (src % SLOT < HALO) & (dst % SLOT >= SLOT - HALO)
    left = (src % SLOT >= SLOT - HALO) & (dst % SLOT < HALO)
    right = jnp.where(right, ahead, -1)
    left = jnp.where(left, ahead, -1)
    none = jnp.zeros(shape, BF)
    upper, lower = [], []
    for j in range(TAPS):
        d = j - HALO
        if d > 0:
            upper.append((right == d).astype(F32).astype(BF))
            lower.append(none)
        elif d < 0:
            upper.append(none)
            lower.append((left == lanes + d).astype(F32).astype(BF))
    return jnp.concatenate(
        [jnp.concatenate(upper, axis=1), jnp.concatenate(lower, axis=1)], axis=0
    )


def halo_conv(first, second, band, wrapped, matrix, xe, halo):
    blocks, chans, lanes = halo.shape
    both = []
    for q in range(blocks):
        left, right = by_side(first[q], second[q])
        both.append(jnp.concatenate([right, left], axis=1))
    lane = lax.broadcasted_iota(jnp.int32, (chans, lanes), 1)
    slot = (lane + HALO) // SLOT % SLOTS

    def turned(value, shift, drop):
        parts = [pltpu.roll(value[:, n * lanes : (n + 1) * lanes], shift, 1) for n in range(2)]
        if drop >= 0:
            keep = (slot != drop).astype(F32).astype(BF)
            parts = [part * keep for part in parts]
        return jnp.concatenate(parts, axis=1)

    if wrapped:
        tall = (
            [turned(both[q], SLOT, 0) for q in range(blocks - HALO, blocks)]
            + both
            + [turned(both[q], lanes - SLOT, SLOTS - 1) for q in range(HALO)]
        )
    else:
        tall = both + [
            turned(both[e % blocks], lanes - SLOT * (e // blocks), -1)
            for e in range(blocks, blocks + 2 * HALO)
        ]
    field = jnp.concatenate(tall, axis=0)
    moved = jnp.dot(field, matrix, preferred_element_type=F32)
    count = len(tall)
    span = xe.shape[1]
    for a in range(TAPS - 1):
        part = moved[:, a * lanes : (a + 1) * lanes].astype(BF)
        xe[a, :count] = part.reshape(count, chans, lanes)
        if count < span:
            xe[a, count:] = jnp.zeros((span - count, chans, lanes), BF)
    tops = slice(0, blocks * GROUP)
    side = [j for j in range(TAPS) if j != HALO]
    for g in range(chans // GROUP):
        at = slice(GROUP * g, GROUP * (g + 1))
        rhs = jnp.concatenate(
            [xe[a, :, at, :].reshape(span * GROUP, lanes) for a in range(TAPS - 1)], axis=0
        )
        lhs = jnp.concatenate(
            [band[g, tops, j * DEPTH : j * DEPTH + span * GROUP] for j in side], axis=1
        )
        out = jnp.dot(lhs, rhs, preferred_element_type=F32)
        halo[:, at, :] = out.reshape(blocks, GROUP, lanes)


def turned_by(value, slots):
    lanes = value.shape[-1]
    if isinstance(slots, int):
        shift = SLOT * slots % lanes
        return pltpu.roll(value, shift, 1) if shift else value
    return pltpu.roll(value, lax.rem(SLOT * slots + lanes, lanes), 1)


def norm_rows(a_ref, base, off, count, halo, gain, out):
    _, chans, lanes = a_ref.shape
    blocks = halo.shape[0]
    edge = edge_lanes((chans, lanes))
    for r in range(count):
        extra = turned_by(halo[(off + r) % blocks], -(base // blocks + (off + r) // blocks))
        a = a_ref[base + off + r] + jnp.where(edge, extra, 0.0)
        center = a - jnp.mean(a, axis=0, keepdims=True)
        var = jnp.mean(center * center, axis=0, keepdims=True)
        normed = (center * lax.rsqrt(var + 1e-06) * gain).astype(BF)
        out[:, r * lanes : (r + 1) * lanes] = normed


def branch_of(normed, up_t, down_t):
    z = jnp.dot(up_t, normed, preferred_element_type=F32)
    h = twice_gelu(z.astype(BF))
    return jnp.dot(down_t, h, preferred_element_type=F32)


def atmos_kernel(layer, near, members, count, steps, *refs):
    x_ref, a_ref, g_ref, up_ref, dn_ref, s_ref = refs[:6]
    refs = refs[6:]
    even, odd = refs[-2:]
    rows, chans, lanes = x_ref.shape
    base = 0
    if layer == 0:
        first_ref, second_ref, band_ref, y_ref, p_ref, xe, halo = refs[:-2]
        blocks = halo.shape[0]
        packed = [None] * blocks
        keep = edge_lanes((chans, lanes)).astype(F32).astype(BF)
    else:
        rank = lax.axis_index("member")
        half = members // 2
        upper = (rank >= half) if near else (rank < half)
        base = jnp.where(upper, rows - steps * count, 0)
        if near:
            fw_ref, _, old_ref, halo, y_ref, keep_ref, give_ref, flux = refs[:-2]
        else:
            fw_ref, first_ref, second_ref, band_ref = refs[:4]
            y_ref, keep_ref, give_ref, flux, halo, xe = refs[4:-2]
    if near:
        flux[...] = old_ref[...]
    else:
        halo_conv(first_ref, second_ref, band_ref, True, halo_matrix(lanes), xe, halo)
        if layer == 1:
            blank = jnp.zeros((HALO,) + flux.shape[1:], BF)
            flux[0:HALO] = blank
            flux[rows + HALO : rows + 2 * HALO] = blank
    up_t = transposed(up_ref[layer])
    dn_t = halved(dn_ref[layer])
    gain = spread(g_ref[layer : layer + 1], lanes)
    scale = spread(s_ref[layer : layer + 1], lanes)
    norm_rows(a_ref, base, 0, count, halo, gain, even)
    for step in range(steps):
        off = step * count
        now, later = (even, odd) if step % 2 == 0 else (odd, even)
        if step + 1 < steps:
            norm_rows(a_ref, base, off + count, count, halo, gain, later)
        branch = branch_of(now[...], up_t, dn_t)
        made = []
        for r in range(count):
            y = x_ref[base + off + r].astype(F32) + scale * branch[:, r * lanes : (r + 1) * lanes]
            made.append(y.astype(BF))
            y_ref[base + off + r] = made[r]
        if layer == 0:
            for r in range(count):
                q, slot = (off + r) % blocks, (off + r) // blocks
                moved = turned_by(made[r] * keep, slot)
                packed[q] = moved if packed[q] is None else packed[q] + moved
            if step % 4 == 3 or step + 1 == steps:
                for q in range(blocks):
                    p_ref[q] = packed[q] if step < 4 else p_ref[q] + packed[q]
                packed = [None] * blocks
        else:
            z = jnp.dot(fw_ref[...], jnp.concatenate(made, axis=1), preferred_element_type=F32)
            f = (0.5 * twice_gelu(z)).astype(BF)
            for r in range(count):
                flux[base + off + HALO + r] = f[:, r * lanes : (r + 1) * lanes]
    if layer == 1:
        share = rows // members
        for k in range(half):
            dst = rank ^ (k if near else half + k)
            chunk = flux[pl.ds(dst * share, share + 2 * HALO)]
            if k % 2:
                give_ref[k // 2] = chunk
            else:
                keep_ref[k // 2] = chunk


def atmos_block(layer, near, members, x, a, weights, others, count, steps):
    rows, chans, lanes = x.shape
    blocks = rows // SLOTS
    args = [x, a, *weights, *others]
    outs = [jax.ShapeDtypeStruct(x.shape, BF)]
    halo = jax.ShapeDtypeStruct((blocks, chans, lanes), F32)
    shifts = pltpu.VMEM((TAPS - 1, SPAN, chans, lanes), BF)
    if layer == 0:
        outs.append(jax.ShapeDtypeStruct((blocks, chans, lanes), BF))
        scratch = [shifts, pltpu.VMEM(halo.shape, F32)]
    else:
        flux = weights[-1].shape[0]
        share = rows // members
        field = (rows + 2 * HALO, flux, lanes)
        outs += [jax.ShapeDtypeStruct((members // 4, share + 2 * HALO, flux, lanes), BF)] * 2
        if near:
            scratch = [pltpu.VMEM(field, BF)]
        else:
            outs += [jax.ShapeDtypeStruct(field, BF), halo]
            scratch = [shifts]
    return pl.pallas_call(
        functools.partial(atmos_kernel, layer, near, members, count, steps),
        out_shape=outs,
        in_specs=[VMEM] * len(args),
        out_specs=[VMEM] * len(outs),
        scratch_shapes=scratch + [pltpu.VMEM((chans, count * lanes), BF)] * 2,
        input_output_aliases={7: 0} if near else {},
        compiler_params=params(BIG),
        cost_estimate=cost(8 * steps * count / rows),
        name="atmos_block",
    )(*args)


def add_kernel(keep_ref, got_ref, *out_refs):
    for n, ref in enumerate(out_refs):
        k = n + keep_ref.shape[0] - len(out_refs)
        ref[...] = (keep_ref[k].astype(F32) + got_ref[k].astype(F32)).astype(BF)


def add_pairs(keep, got, skip):
    count = keep.shape[0] - skip
    return pl.pallas_call(
        add_kernel,
        out_shape=[jax.ShapeDtypeStruct(keep.shape[1:], BF)] * count,
        in_specs=[VMEM] * 2,
        out_specs=[VMEM] * count,
        compiler_params=params(24),
        name="add_pairs",
    )(keep, got)


def send_xor(value, bits):
    members = lax.axis_size("member")
    return lax.ppermute(value, "member", [(i, i ^ bits) for i in range(members)])


def force_kernel(members, *refs):
    near_refs, flux_refs = refs[:2], refs[2 : members // 2 + 1]
    win_ref, land_ref, ice_ref, lift_ref, mid_ref, p_ref = refs[members // 2 + 1 :]
    lanes = land_ref.shape[1]
    rows = land_ref.shape[0]
    chans = mid_ref.shape[1]
    blocks = p_ref.shape[0]
    span, first, start = window(members, rows)
    total = near_refs[0][0].astype(F32) + near_refs[1][0].astype(F32)
    for ref in flux_refs:
        total = total + ref[...].astype(F32)
    low = (total / members).astype(BF)
    columns = jnp.concatenate([low[r] for r in range(span)], axis=1)
    terms = jnp.dot(lift_ref[...], columns, preferred_element_type=F32)
    keep = edge_lanes((chans, lanes)).astype(F32).astype(BF)
    packed = [None] * blocks
    for r in range(span):
        row = first + r
        safe = jnp.clip(row, 0, rows - 1)
        sea = (1 - land_ref[pl.ds(safe, 1), :]).astype(F32)
        ice = ice_ref[pl.ds(safe, 1), :].astype(F32)
        at = slice(r * lanes, (r + 1) * lanes)
        forcing = sea * ((1.0 - ice) * terms[:chans, at] + ice * terms[chans:, at])
        mid = win_ref[jnp.clip(row - start, 0, span - 1)].astype(F32) + forcing
        inside = (row >= 0) & (row < rows)
        mid = jnp.where(inside, mid, 0.0).astype(BF)
        mid_ref[r] = mid
        q, slot = r % blocks, r // blocks
        moved = mid * keep
        if slot:
            moved = pltpu.roll(moved, SLOT * slot, 1)
        packed[q] = moved if packed[q] is None else packed[q] + moved
    for q in range(blocks):
        p_ref[q] = packed[q]


def force(members, chunks, win, land, ice, lift):
    span, chans, lanes = win.shape
    return pl.pallas_call(
        functools.partial(force_kernel, members),
        out_shape=[
            jax.ShapeDtypeStruct((span, chans, lanes), BF),
            jax.ShapeDtypeStruct((OCEAN_BLOCKS, chans, lanes), BF),
        ],
        in_specs=[VMEM] * (len(chunks) + 4),
        out_specs=[VMEM] * 2,
        compiler_params=params(24),
        name="ocean_forcing",
    )(*chunks, win, land, ice, lift)


def ocean_kernel(mid_ref, a_ref, left_ref, right_ref, band_ref, land_ref, mat_ref, upt_ref, gain_ref, scale_ref, dn_ref, sw_ref, new_ref, surf_ref, xe, halo, normed):
    share, chans, lanes = new_ref.shape
    halo_conv(left_ref, right_ref, band_ref, False, mat_ref[...], xe, halo)
    scale = scale_ref[...]
    norm_rows(a_ref, 0, 0, share, halo, gain_ref[...], normed)
    branch = branch_of(normed[...], upt_ref[...], halved(dn_ref[...]))
    first = lax.axis_index("member") * share
    made = []
    for r in range(share):
        sea = (1 - land_ref[pl.ds(first + r, 1), :]).astype(F32)
        y = mid_ref[HALO + r].astype(F32) + scale * branch[:, r * lanes : (r + 1) * lanes]
        made.append((y * sea).astype(BF))
        new_ref[r] = made[r]
    surf = jnp.dot(
        sw_ref[...], jnp.concatenate(made, axis=1), preferred_element_type=F32
    )
    for r in range(share):
        surf_ref[r] = surf[:, r * lanes : (r + 1) * lanes].astype(BF)


def ocean_block(mid, a, left, right, band, land, ready, down, surf_weight):
    share, chans, lanes = a.shape
    blocks = left.shape[0]
    return pl.pallas_call(
        ocean_kernel,
        out_shape=[
            jax.ShapeDtypeStruct((share, chans, lanes), BF),
            jax.ShapeDtypeStruct((share, surf_weight.shape[0], lanes), BF),
        ],
        in_specs=[VMEM] * 12,
        out_specs=[VMEM] * 2,
        scratch_shapes=[
            pltpu.VMEM((TAPS - 1, OCEAN_BLOCKS + 2 * HALO, chans, lanes), BF),
            pltpu.VMEM((blocks, chans, lanes), F32),
            pltpu.VMEM((chans, share * lanes), BF),
        ],
        compiler_params=params(24),
        name="ocean_block",
    )(mid, a, left, right, band, land, *ready, down, surf_weight)


def pair_kernel(own_ref, got_ref, out_ref):
    out_ref[0] = own_ref[...]
    out_ref[1] = got_ref[...]


def make_pair(own, got):
    return pl.pallas_call(
        pair_kernel,
        out_shape=jax.ShapeDtypeStruct((2,) + own.shape, BF),
        in_specs=[VMEM] * 2,
        out_specs=VMEM,
        compiler_params=params(24),
        name="surface_pair",
    )(own, got)


def couple_kernel(ks, y_ref, land_ref, bw_ref, *refs):
    pair_refs = refs[: len(ks)]
    o_ref, buf, sems = refs[-3:]
    chans, lanes = y_ref.shape[1:]
    share = pair_refs[0].shape[1]
    rank = lax.axis_index("member")
    parity = rank % 2
    copies = []
    for n, (k, pair_ref) in enumerate(zip(ks, pair_refs)):
        first = ((rank // 2) ^ k) * 2 * share
        surf = [pair_ref[side ^ parity, r] for side in range(2) for r in range(share)]
        back = jnp.dot(bw_ref[...], jnp.concatenate(surf, axis=1), preferred_element_type=F32)
        for r in range(2 * share):
            sea = (1 - land_ref[pl.ds(first + r, 1), :]).astype(F32)
            out = y_ref[first + r].astype(F32) + sea * back[:, r * lanes : (r + 1) * lanes]
            buf[n, r] = out.astype(BF)
        copies.append(
            pltpu.make_async_copy(buf.at[n], o_ref.at[pl.ds(first, 2 * share)], sems.at[n])
        )
        copies[n].start()
    for copy in copies:
        copy.wait()


def couple(ks, y, land, back_weight, pairs, earlier):
    _, chans, lanes = y.shape
    count = len(ks)
    return pl.pallas_call(
        functools.partial(couple_kernel, ks),
        out_shape=jax.ShapeDtypeStruct(y.shape, BF),
        in_specs=[VMEM] * (3 + count) + [HBM] * len(earlier),
        out_specs=HBM,
        scratch_shapes=[
            pltpu.VMEM((count, 2 * pairs[0].shape[1], chans, lanes), BF),
            pltpu.SemaphoreType.DMA((count,)),
        ],
        input_output_aliases={3 + count: 0} if earlier else {},
        compiler_params=params(24),
        name="couple",
    )(y, land, back_weight, *pairs, *earlier)


def local(
    atmos,
    ocean,
    land_mask,
    ice_mask,
    atm_kernel,
    atm_gain,
    atm_up,
    atm_down,
    atm_scale,
    flux_weight,
    flux_lift,
    ocn_kernel,
    ocn_gain,
    ocn_up,
    ocn_down,
    ocn_scale,
    surf_weight,
    back_weight,
):
    members = lax.axis_size("member")
    half = members // 2
    state = atmos[0]
    rows = state.shape[0]
    blocks = rows // SLOTS
    small = 2 * blocks
    atm = (atm_gain, atm_up, atm_down.transpose(0, 2, 1), atm_scale)
    taps = atm_kernel.transpose(1, 2, 0, 3)

    edges = neighbours(pack(state, small))
    a, band = convolve(0, state, taps, blocks)
    steps = rows // small
    near_steps = (rows // 2) // small - 1
    state, packed = atmos_block(0, False, members, state, a, atm, [*edges, band], small, steps)

    edges = neighbours(packed)
    a, band = convolve(1, state, taps, blocks)
    weights = (*atm, flux_weight.T)
    partly, far_keep, give, flux, halo = atmos_block(
        1, False, members, state, a, weights, [*edges, band], small, steps - near_steps
    )
    far_got = send_xor(give, 1)
    state, keep, give = atmos_block(
        1, True, members, state, a, weights, [partly, flux, halo], small, near_steps
    )
    far_got, give = lax.optimization_barrier((far_got, give))
    far_sums = add_pairs(far_keep, far_got, 0)
    give, *far_sums = lax.optimization_barrier((give, *far_sums))
    sent = [send_xor(far_sums[k], half + 2 * k) for k in reversed(range(len(far_sums)))]
    got = send_xor(give, 1)
    sums = add_pairs(keep, got, 1)
    sent += [send_xor(part, 2 * k + 2) for k, part in enumerate(sums)]
    band, *ready, lift, win = prepare_ocean(
        members, ocn_kernel, ocn_gain, ocn_up, ocn_scale, flux_lift, ocean, sums[0]
    )
    sent = [keep, got] + sent
    mid, packed = force(members, sent, win, land_mask, ice_mask, lift)
    left, right = neighbours(packed)
    a = ocean_conv(mid, band)
    ocean_rows, surface = ocean_block(
        mid, a, left, right, band, land_mask, ready, ocn_down.T, surf_weight.T
    )
    own = make_pair(surface, send_xor(surface, 1))
    pairs = [own] + [send_xor(own, 2 * k) for k in range(1, half)]
    out = couple((0,), state, land_mask, back_weight.T, pairs[:1], [])
    rest = tuple(range(1, half))
    out = couple(rest, state, land_mask, back_weight.T, pairs[1:], [out])
    return (out[None], ocean_rows)


def solution(mesh):
    in_specs = (
        P("member", None, None, "lon"),
        P(None, None, "lon"),
        P(None, "lon"),
        P(None, "lon"),
    ) + (P(),) * 14
    out_specs = (P("member", None, None, "lon"), P("member", None, "lon"))
    return jax.shard_map(local, mesh=mesh, in_specs=in_specs, out_specs=out_specs, check_vma=False)
```

```python
import functools

import jax
import jax.numpy as jnp
from jax import lax
from jax.experimental import pallas as pl
from jax.experimental.pallas import tpu as pltpu
from jax.sharding import PartitionSpec as P

BF = jnp.bfloat16
F32 = jnp.float32
TANH_A = 0.7978845608028654
TANH_B = TANH_A * 0.044715
TAPS = 7
HALO = 3
GROUP = 16
SPAN = 16
OUT = SPAN - TAPS + 1
DEPTH = GROUP * SPAN
SLOT = 8
SLOTS = 16
OCEAN_BLOCKS = 2
BIG = 32
VMEM = pl.BlockSpec(memory_space=pltpu.VMEM)
ANY = pl.BlockSpec(memory_space=pl.ANY)
HBM = pl.BlockSpec(memory_space=pltpu.HBM)


def params(mib):
    return pltpu.CompilerParams(vmem_limit_bytes=mib * 2**20)


def cost(gflop):
    return pl.CostEstimate(flops=int(gflop * 1e9), bytes_accessed=0, transcendentals=0)


def twice_gelu(z):
    return z + z * jnp.tanh(z * (TANH_A + TANH_B * (z * z)))


def transposed(value):
    return value.astype(F32).T.astype(BF)


def halved(value):
    return (0.5 * value.astype(F32)).astype(BF)


def spread(row, lanes):
    return jnp.broadcast_to(row.T, (row.shape[1], lanes))


def edge_lanes(shape):
    lane = lax.broadcasted_iota(jnp.int32, shape, len(shape) - 1)
    return (lane < HALO) | (lane >= shape[-1] - HALO)


def pack_kernel(step, src_ref, p_ref, x_ref, sems):
    rows, chans, lanes = x_ref.shape
    blocks = p_ref.shape[0]
    copies = []
    for n in range(rows // step):
        at = slice(n * step, (n + 1) * step)
        copies.append(pltpu.make_async_copy(src_ref.at[at], x_ref.at[at], sems.at[n]))
        copies[n].start()
    keep = edge_lanes((chans, lanes)).astype(F32).astype(BF)
    for n in range(rows // step):
        copies[n].wait()
        for q in range(blocks):
            total = None if n == 0 else p_ref[q]
            for slot in range(n * step // blocks, (n + 1) * step // blocks):
                moved = x_ref[slot * blocks + q] * keep
                if slot:
                    moved = pltpu.roll(moved, SLOT * slot, 1)
                total = moved if total is None else total + moved
            p_ref[q] = total


def pack(x, step):
    rows, chans, lanes = x.shape
    return pl.pallas_call(
        functools.partial(pack_kernel, step),
        out_shape=jax.ShapeDtypeStruct((rows // SLOTS, chans, lanes), BF),
        in_specs=[HBM],
        out_specs=VMEM,
        scratch_shapes=[pltpu.VMEM(x.shape, BF), pltpu.SemaphoreType.DMA((rows // step,))],
        compiler_params=params(60),
        name="pack_edges",
    )(x)


def neighbours(packed):
    count = lax.axis_size("lon")
    first = lax.ppermute(
        packed, "lon", [(i, (i - 1) % count if i % 2 == 0 else (i + 1) % count) for i in range(count)]
    )
    second = lax.ppermute(packed, "lon", [(i, i ^ 1) for i in range(count)])
    return first, second


def by_side(first, second):
    even = lax.axis_index("lon") % 2 == 0
    return jnp.where(even, first, second), jnp.where(even, second, first)


def fill_base(taps, base):
    groups, _, wide = base.shape
    chans = groups * GROUP
    tall = TAPS * SLOT
    t = lax.broadcasted_iota(jnp.int32, (tall, wide), 0)
    n = lax.broadcasted_iota(jnp.int32, (tall, wide), 1)
    hit = (t % SLOT == n // DEPTH) & (t // SLOT == (n % DEPTH) // GROUP)
    columns = []
    for i in range(TAPS):
        columns.append(taps(i).T)
        columns.append(jnp.zeros((chans, SLOT - TAPS), F32))
    columns = jnp.concatenate(columns, axis=1).astype(BF)
    total = jnp.dot(columns, hit.astype(F32).astype(BF), preferred_element_type=F32)
    r = lax.broadcasted_iota(jnp.int32, (GROUP, wide), 0)
    c = lax.broadcasted_iota(jnp.int32, (GROUP, wide), 1)
    same = r == c % GROUP
    for g in range(groups):
        base[g] = jnp.where(same, total[GROUP * g : GROUP * (g + 1)], 0.0)


def fill_band(base, g, band):
    for j in range(TAPS):
        one = base[g, :, j * DEPTH : (j + 1) * DEPTH]
        for r in range(OUT):
            moved = pltpu.roll(one, GROUP * r, 1) if r else one
            band[GROUP * r : GROUP * (r + 1), j * DEPTH : (j + 1) * DEPTH] = moved.astype(BF)


def fill_shifts(x, pad, xj):
    count, _, lanes = x.shape
    lane = lax.broadcasted_iota(jnp.int32, (GROUP, lanes), 1)
    for j in range(TAPS):
        d = j - HALO
        if d:
            keep = ((lane < lanes - d) if d > 0 else (lane >= -d)).astype(F32).astype(BF)
            xj[j, pad : pad + count] = pltpu.roll(x, (-d) % lanes, 2) * keep[None]
        else:
            xj[j, pad : pad + count] = x


def clear_pads(pad, count, xj):
    tall, _, lanes = xj.shape[1:]
    for j in range(TAPS):
        if pad:
            xj[j, :pad] = jnp.zeros((pad, GROUP, lanes), BF)
        if tall > pad + count:
            xj[j, pad + count :] = jnp.zeros((tall - pad - count, GROUP, lanes), BF)


def apply_band(band, xj, a_ref):
    rows, _, lanes = a_ref.shape
    starts = [min(OUT * i, max(rows - OUT, 0)) for i in range(-(-rows // OUT))]
    field = jnp.concatenate(
        [
            jnp.concatenate([xj[j, s : s + SPAN].reshape(DEPTH, lanes) for j in range(TAPS)], axis=0)
            for s in starts
        ],
        axis=1,
    )
    out = jnp.dot(band, field, preferred_element_type=F32)
    take = min(OUT, rows)
    for n, s in enumerate(starts):
        part = out[: take * GROUP, n * lanes : (n + 1) * lanes]
        a_ref[s : s + take] = part.reshape(take, GROUP, lanes)


def conv_kernel(layer, x_ref, k_ref, a_ref, band_ref, base, even_xj, odd_xj, even_band, odd_band):
    rows, chans, lanes = x_ref.shape
    groups = chans // GROUP
    fill_base(lambda i: k_ref[i, :, layer, :], base)
    clear_pads(HALO, rows, even_xj)
    clear_pads(HALO, rows, odd_xj)

    def at(g):
        return pl.ds(pl.multiple_of(GROUP * g, GROUP), GROUP)

    def prepare(g, xj, band):
        fill_band(base, g, band)
        band_ref[g] = band[: band_ref.shape[1]]
        fill_shifts(x_ref[:, at(g), :], HALO, xj)

    prepare(0, even_xj, even_band)

    def pair(i, carry):
        prepare(2 * i + 1, odd_xj, odd_band)
        apply_band(even_band[...], even_xj, a_ref.at[:, at(2 * i), :])
        prepare(jnp.minimum(2 * i + 2, groups - 1), even_xj, even_band)
        apply_band(odd_band[...], odd_xj, a_ref.at[:, at(2 * i + 1), :])
        return carry

    lax.fori_loop(0, groups // 2, pair, 0)


def convolve(layer, x, taps, blocks):
    rows, chans, lanes = x.shape
    groups = chans // GROUP
    wide = TAPS * DEPTH
    return pl.pallas_call(
        functools.partial(conv_kernel, layer),
        out_shape=[
            jax.ShapeDtypeStruct((rows, chans, lanes), F32),
            jax.ShapeDtypeStruct((groups, blocks * GROUP, wide), BF),
        ],
        in_specs=[VMEM, VMEM],
        out_specs=[VMEM, VMEM],
        scratch_shapes=[
            pltpu.VMEM((groups, GROUP, wide), F32),
        ]
        + [pltpu.VMEM((TAPS, rows + 2 * HALO, GROUP, lanes), BF)] * 2
        + [pltpu.VMEM((GROUP * OUT, wide), BF)] * 2,
        compiler_params=params(BIG),
        cost_estimate=cost(8),
        name="conv",
    )(x, taps)


def window(members, rows):
    share = rows // members
    span = share + 2 * HALO
    first = lax.axis_index("member") * share - HALO
    return span, first, jnp.clip(first, 0, rows - span)


def prepare_kernel(members, k_ref, g_ref, up_ref, s_ref, lift_ref, ocean_ref, _, *refs):
    band_ref, mat_ref, upt_ref, gain_ref, scale_ref, lift_out, win_ref, base, sem = refs
    lanes = gain_ref.shape[1]
    span, _, start = window(members, ocean_ref.shape[0])
    copy = pltpu.make_async_copy(ocean_ref.at[pl.ds(start, span)], win_ref, sem)
    copy.start()
    mat_ref[...] = halo_matrix(lanes)
    upt_ref[...] = transposed(up_ref[...])
    gain_ref[...] = spread(g_ref[...], lanes)
    scale_ref[...] = spread(s_ref[...], lanes)
    lift_out[...] = jnp.concatenate([transposed(lift_ref[0]), transposed(lift_ref[1])], axis=0)
    fill_base(lambda i: k_ref[i], base)
    for g in range(base.shape[0]):
        fill_band(base, g, band_ref.at[g])
    copy.wait()


def prepare_ocean(members, taps, gain, up, scale, lift, ocean, after):
    chans, hid = up.shape
    rows, _, lanes = ocean.shape
    flux = lift.shape[1]
    groups = chans // GROUP
    wide = TAPS * DEPTH
    span = rows // members + 2 * HALO
    return pl.pallas_call(
        functools.partial(prepare_kernel, members),
        out_shape=[
            jax.ShapeDtypeStruct((groups, GROUP * OUT, wide), BF),
            jax.ShapeDtypeStruct((2 * lanes, (TAPS - 1) * lanes), BF),
            jax.ShapeDtypeStruct((hid, chans), BF),
            jax.ShapeDtypeStruct((chans, lanes), F32),
            jax.ShapeDtypeStruct((chans, lanes), F32),
            jax.ShapeDtypeStruct((2 * chans, flux), BF),
            jax.ShapeDtypeStruct((span, chans, lanes), BF),
        ],
        in_specs=[VMEM] * 5 + [HBM, ANY],
        out_specs=[VMEM] * 7,
        scratch_shapes=[pltpu.VMEM((groups, GROUP, wide), F32), pltpu.SemaphoreType.DMA(())],
        compiler_params=params(24),
        cost_estimate=cost(3),
        name="prepare_ocean",
    )(taps, gain[None], up, scale[None], lift, ocean, after)


def ocean_conv_kernel(x_ref, band_ref, a_ref, xj):
    count, chans, lanes = x_ref.shape
    for g in range(chans // GROUP):
        at = slice(GROUP * g, GROUP * (g + 1))
        clear_pads(0, count, xj.at[g])
        fill_shifts(x_ref[:, at, :], 0, xj.at[g])
        apply_band(band_ref[g], xj.at[g], a_ref.at[:, at, :])


def ocean_conv(x, band):
    count, chans, lanes = x.shape
    return pl.pallas_call(
        ocean_conv_kernel,
        out_shape=jax.ShapeDtypeStruct((count - 2 * HALO, chans, lanes), F32),
        in_specs=[VMEM, VMEM],
        out_specs=VMEM,
        scratch_shapes=[pltpu.VMEM((chans // GROUP, TAPS, max(count, SPAN), GROUP, lanes), BF)],
        compiler_params=params(24),
        cost_estimate=cost(2),
        name="ocean_conv",
    )(x, band)


def halo_matrix(lanes):
    shape = (lanes, lanes)
    src = lax.broadcasted_iota(jnp.int32, shape, 0)
    dst = lax.broadcasted_iota(jnp.int32, shape, 1)
    ahead = (src - dst + lanes) % lanes
    right = (src % SLOT < HALO) & (dst % SLOT >= SLOT - HALO)
    left = (src % SLOT >= SLOT - HALO) & (dst % SLOT < HALO)
    right = jnp.where(right, ahead, -1)
    left = jnp.where(left, ahead, -1)
    none = jnp.zeros(shape, BF)
    upper, lower = [], []
    for j in range(TAPS):
        d = j - HALO
        if d > 0:
            upper.append((right == d).astype(F32).astype(BF))
            lower.append(none)
        elif d < 0:
            upper.append(none)
            lower.append((left == lanes + d).astype(F32).astype(BF))
    return jnp.concatenate(
        [jnp.concatenate(upper, axis=1), jnp.concatenate(lower, axis=1)], axis=0
    )


def halo_conv(first, second, band, wrapped, matrix, xe, halo):
    blocks, chans, lanes = halo.shape
    both = []
    for q in range(blocks):
        left, right = by_side(first[q], second[q])
        both.append(jnp.concatenate([right, left], axis=1))
    lane = lax.broadcasted_iota(jnp.int32, (chans, lanes), 1)
    slot = (lane + HALO) // SLOT % SLOTS

    def turned(value, shift, drop):
        parts = [pltpu.roll(value[:, n * lanes : (n + 1) * lanes], shift, 1) for n in range(2)]
        if drop >= 0:
            keep = (slot != drop).astype(F32).astype(BF)
            parts = [part * keep for part in parts]
        return jnp.concatenate(parts, axis=1)

    if wrapped:
        tall = (
            [turned(both[q], SLOT, 0) for q in range(blocks - HALO, blocks)]
            + both
            + [turned(both[q], lanes - SLOT, SLOTS - 1) for q in range(HALO)]
        )
    else:
        tall = both + [
            turned(both[e % blocks], lanes - SLOT * (e // blocks), -1)
            for e in range(blocks, blocks + 2 * HALO)
        ]
    field = jnp.concatenate(tall, axis=0)
    moved = jnp.dot(field, matrix, preferred_element_type=F32)
    count = len(tall)
    span = xe.shape[1]
    for a in range(TAPS - 1):
        part = moved[:, a * lanes : (a + 1) * lanes].astype(BF)
        xe[a, :count] = part.reshape(count, chans, lanes)
        if count < span:
            xe[a, count:] = jnp.zeros((span - count, chans, lanes), BF)
    tops = slice(0, blocks * GROUP)
    side = [j for j in range(TAPS) if j != HALO]
    for g in range(chans // GROUP):
        at = slice(GROUP * g, GROUP * (g + 1))
        rhs = jnp.concatenate(
            [xe[a, :, at, :].reshape(span * GROUP, lanes) for a in range(TAPS - 1)], axis=0
        )
        lhs = jnp.concatenate(
            [band[g, tops, j * DEPTH : j * DEPTH + span * GROUP] for j in side], axis=1
        )
        out = jnp.dot(lhs, rhs, preferred_element_type=F32)
        halo[:, at, :] = out.reshape(blocks, GROUP, lanes)


def turned_by(value, slots):
    lanes = value.shape[-1]
    if isinstance(slots, int):
        shift = SLOT * slots % lanes
        return pltpu.roll(value, shift, 1) if shift else value
    return pltpu.roll(value, lax.rem(SLOT * slots + lanes, lanes), 1)


def norm_rows(a_ref, base, off, count, halo, gain, out):
    _, chans, lanes = a_ref.shape
    blocks = halo.shape[0]
    edge = edge_lanes((chans, lanes))
    for r in range(count):
        extra = turned_by(halo[(off + r) % blocks], -(base // blocks + (off + r) // blocks))
        a = a_ref[base + off + r] + jnp.where(edge, extra, 0.0)
        center = a - jnp.mean(a, axis=0, keepdims=True)
        var = jnp.mean(center * center, axis=0, keepdims=True)
        normed = (center * lax.rsqrt(var + 1e-06) * gain).astype(BF)
        out[:, r * lanes : (r + 1) * lanes] = normed


def branch_of(normed, up_t, down_t):
    z = jnp.dot(up_t, normed, preferred_element_type=F32)
    h = twice_gelu(z.astype(BF))
    return jnp.dot(down_t, h, preferred_element_type=F32)


def atmos_kernel(layer, near, members, count, steps, *refs):
    x_ref, a_ref, g_ref, up_ref, dn_ref, s_ref = refs[:6]
    refs = refs[6:]
    even, odd = refs[-2:]
    rows, chans, lanes = x_ref.shape
    base = 0
    if layer == 0:
        first_ref, second_ref, band_ref, y_ref, p_ref, xe, halo = refs[:-2]
        blocks = halo.shape[0]
        packed = [None] * blocks
        keep = edge_lanes((chans, lanes)).astype(F32).astype(BF)
    else:
        rank = lax.axis_index("member")
        half = members // 2
        upper = (rank >= half) if near else (rank < half)
        base = jnp.where(upper, rows - steps * count, 0)
        if near:
            fw_ref, _, old_ref, halo, y_ref, keep_ref, give_ref, flux = refs[:-2]
        else:
            fw_ref, first_ref, second_ref, band_ref = refs[:4]
            y_ref, keep_ref, give_ref, flux, halo, xe = refs[4:-2]
    if near:
        flux[...] = old_ref[...]
    else:
        halo_conv(first_ref, second_ref, band_ref, True, halo_matrix(lanes), xe, halo)
        if layer == 1:
            blank = jnp.zeros((HALO,) + flux.shape[1:], BF)
            flux[0:HALO] = blank
            flux[rows + HALO : rows + 2 * HALO] = blank
    up_t = transposed(up_ref[layer])
    dn_t = halved(dn_ref[layer])
    gain = spread(g_ref[layer : layer + 1], lanes)
    scale = spread(s_ref[layer : layer + 1], lanes)
    norm_rows(a_ref, base, 0, count, halo, gain, even)
    for step in range(steps):
        off = step * count
        now, later = (even, odd) if step % 2 == 0 else (odd, even)
        if step + 1 < steps:
            norm_rows(a_ref, base, off + count, count, halo, gain, later)
        branch = branch_of(now[...], up_t, dn_t)
        made = []
        for r in range(count):
            y = x_ref[base + off + r].astype(F32) + scale * branch[:, r * lanes : (r + 1) * lanes]
            made.append(y.astype(BF))
            y_ref[base + off + r] = made[r]
        if layer == 0:
            for r in range(count):
                q, slot = (off + r) % blocks, (off + r) // blocks
                moved = turned_by(made[r] * keep, slot)
                packed[q] = moved if packed[q] is None else packed[q] + moved
            if step % 4 == 3 or step + 1 == steps:
                for q in range(blocks):
                    p_ref[q] = packed[q] if step < 4 else p_ref[q] + packed[q]
                packed = [None] * blocks
        else:
            z = jnp.dot(fw_ref[...], jnp.concatenate(made, axis=1), preferred_element_type=F32)
            f = (0.5 * twice_gelu(z)).astype(BF)
            for r in range(count):
                flux[base + off + HALO + r] = f[:, r * lanes : (r + 1) * lanes]
    if layer == 1:
        share = rows // members
        for k in range(half):
            dst = rank ^ (k if near else half + k)
            chunk = flux[pl.ds(dst * share, share + 2 * HALO)]
            if k % 2:
                give_ref[k // 2] = chunk
            else:
                keep_ref[k // 2] = chunk


def atmos_block(layer, near, members, x, a, weights, others, count, steps):
    rows, chans, lanes = x.shape
    blocks = rows // SLOTS
    args = [x, a, *weights, *others]
    outs = [jax.ShapeDtypeStruct(x.shape, BF)]
    halo = jax.ShapeDtypeStruct((blocks, chans, lanes), F32)
    shifts = pltpu.VMEM((TAPS - 1, SPAN, chans, lanes), BF)
    if layer == 0:
        outs.append(jax.ShapeDtypeStruct((blocks, chans, lanes), BF))
        scratch = [shifts, pltpu.VMEM(halo.shape, F32)]
    else:
        flux = weights[-1].shape[0]
        share = rows // members
        field = (rows + 2 * HALO, flux, lanes)
        outs += [jax.ShapeDtypeStruct((members // 4, share + 2 * HALO, flux, lanes), BF)] * 2
        if near:
            scratch = [pltpu.VMEM(field, BF)]
        else:
            outs += [jax.ShapeDtypeStruct(field, BF), halo]
            scratch = [shifts]
    return pl.pallas_call(
        functools.partial(atmos_kernel, layer, near, members, count, steps),
        out_shape=outs,
        in_specs=[VMEM] * len(args),
        out_specs=[VMEM] * len(outs),
        scratch_shapes=scratch + [pltpu.VMEM((chans, count * lanes), BF)] * 2,
        input_output_aliases={7: 0} if near else {},
        compiler_params=params(BIG),
        cost_estimate=cost(8 * steps * count / rows),
        name="atmos_block",
    )(*args)


def add_kernel(keep_ref, got_ref, *out_refs):
    for n, ref in enumerate(out_refs):
        k = n + keep_ref.shape[0] - len(out_refs)
        ref[...] = (keep_ref[k].astype(F32) + got_ref[k].astype(F32)).astype(BF)


def add_pairs(keep, got, skip):
    count = keep.shape[0] - skip
    return pl.pallas_call(
        add_kernel,
        out_shape=[jax.ShapeDtypeStruct(keep.shape[1:], BF)] * count,
        in_specs=[VMEM] * 2,
        out_specs=[VMEM] * count,
        compiler_params=params(24),
        name="add_pairs",
    )(keep, got)


def send_xor(value, bits):
    members = lax.axis_size("member")
    return lax.ppermute(value, "member", [(i, i ^ bits) for i in range(members)])


def force_kernel(members, *refs):
    near_refs, flux_refs = refs[:2], refs[2 : members // 2 + 1]
    win_ref, land_ref, ice_ref, lift_ref, mid_ref, p_ref = refs[members // 2 + 1 :]
    lanes = land_ref.shape[1]
    rows = land_ref.shape[0]
    chans = mid_ref.shape[1]
    blocks = p_ref.shape[0]
    span, first, start = window(members, rows)
    total = near_refs[0][0].astype(F32) + near_refs[1][0].astype(F32)
    for ref in flux_refs:
        total = total + ref[...].astype(F32)
    low = (total / members).astype(BF)
    columns = jnp.concatenate([low[r] for r in range(span)], axis=1)
    terms = jnp.dot(lift_ref[...], columns, preferred_element_type=F32)
    keep = edge_lanes((chans, lanes)).astype(F32).astype(BF)
    packed = [None] * blocks
    for r in range(span):
        row = first + r
        safe = jnp.clip(row, 0, rows - 1)
        sea = (1 - land_ref[pl.ds(safe, 1), :]).astype(F32)
        ice = ice_ref[pl.ds(safe, 1), :].astype(F32)
        at = slice(r * lanes, (r + 1) * lanes)
        forcing = sea * ((1.0 - ice) * terms[:chans, at] + ice * terms[chans:, at])
        mid = win_ref[jnp.clip(row - start, 0, span - 1)].astype(F32) + forcing
        inside = (row >= 0) & (row < rows)
        mid = jnp.where(inside, mid, 0.0).astype(BF)
        mid_ref[r] = mid
        q, slot = r % blocks, r // blocks
        moved = mid * keep
        if slot:
            moved = pltpu.roll(moved, SLOT * slot, 1)
        packed[q] = moved if packed[q] is None else packed[q] + moved
    for q in range(blocks):
        p_ref[q] = packed[q]


def force(members, chunks, win, land, ice, lift):
    span, chans, lanes = win.shape
    return pl.pallas_call(
        functools.partial(force_kernel, members),
        out_shape=[
            jax.ShapeDtypeStruct((span, chans, lanes), BF),
            jax.ShapeDtypeStruct((OCEAN_BLOCKS, chans, lanes), BF),
        ],
        in_specs=[VMEM] * (len(chunks) + 4),
        out_specs=[VMEM] * 2,
        compiler_params=params(24),
        name="ocean_forcing",
    )(*chunks, win, land, ice, lift)


def ocean_kernel(mid_ref, a_ref, left_ref, right_ref, band_ref, land_ref, mat_ref, upt_ref, gain_ref, scale_ref, dn_ref, sw_ref, new_ref, surf_ref, xe, halo, normed):
    share, chans, lanes = new_ref.shape
    halo_conv(left_ref, right_ref, band_ref, False, mat_ref[...], xe, halo)
    scale = scale_ref[...]
    norm_rows(a_ref, 0, 0, share, halo, gain_ref[...], normed)
    branch = branch_of(normed[...], upt_ref[...], halved(dn_ref[...]))
    first = lax.axis_index("member") * share
    made = []
    for r in range(share):
        sea = (1 - land_ref[pl.ds(first + r, 1), :]).astype(F32)
        y = mid_ref[HALO + r].astype(F32) + scale * branch[:, r * lanes : (r + 1) * lanes]
        made.append((y * sea).astype(BF))
        new_ref[r] = made[r]
    surf = jnp.dot(
        sw_ref[...], jnp.concatenate(made, axis=1), preferred_element_type=F32
    )
    for r in range(share):
        surf_ref[r] = surf[:, r * lanes : (r + 1) * lanes].astype(BF)


def ocean_block(mid, a, left, right, band, land, ready, down, surf_weight):
    share, chans, lanes = a.shape
    blocks = left.shape[0]
    return pl.pallas_call(
        ocean_kernel,
        out_shape=[
            jax.ShapeDtypeStruct((share, chans, lanes), BF),
            jax.ShapeDtypeStruct((share, surf_weight.shape[0], lanes), BF),
        ],
        in_specs=[VMEM] * 12,
        out_specs=[VMEM] * 2,
        scratch_shapes=[
            pltpu.VMEM((TAPS - 1, OCEAN_BLOCKS + 2 * HALO, chans, lanes), BF),
            pltpu.VMEM((blocks, chans, lanes), F32),
            pltpu.VMEM((chans, share * lanes), BF),
        ],
        compiler_params=params(24),
        name="ocean_block",
    )(mid, a, left, right, band, land, *ready, down, surf_weight)


def pair_kernel(own_ref, got_ref, out_ref):
    out_ref[0] = own_ref[...]
    out_ref[1] = got_ref[...]


def make_pair(own, got):
    return pl.pallas_call(
        pair_kernel,
        out_shape=jax.ShapeDtypeStruct((2,) + own.shape, BF),
        in_specs=[VMEM] * 2,
        out_specs=VMEM,
        compiler_params=params(24),
        name="surface_pair",
    )(own, got)


def couple_kernel(ks, y_ref, land_ref, bw_ref, *refs):
    pair_refs = refs[: len(ks)]
    o_ref, buf, sems = refs[-3:]
    chans, lanes = y_ref.shape[1:]
    share = pair_refs[0].shape[1]
    rank = lax.axis_index("member")
    parity = rank % 2
    copies = []
    for n, (k, pair_ref) in enumerate(zip(ks, pair_refs)):
        first = ((rank // 2) ^ k) * 2 * share
        surf = [pair_ref[side ^ parity, r] for side in range(2) for r in range(share)]
        back = jnp.dot(bw_ref[...], jnp.concatenate(surf, axis=1), preferred_element_type=F32)
        for r in range(2 * share):
            sea = (1 - land_ref[pl.ds(first + r, 1), :]).astype(F32)
            out = y_ref[first + r].astype(F32) + sea * back[:, r * lanes : (r + 1) * lanes]
            buf[n, r] = out.astype(BF)
        copies.append(
            pltpu.make_async_copy(buf.at[n], o_ref.at[pl.ds(first, 2 * share)], sems.at[n])
        )
        copies[n].start()
    for copy in copies:
        copy.wait()


def couple(ks, y, land, back_weight, pairs, earlier):
    _, chans, lanes = y.shape
    count = len(ks)
    return pl.pallas_call(
        functools.partial(couple_kernel, ks),
        out_shape=jax.ShapeDtypeStruct(y.shape, BF),
        in_specs=[VMEM] * (3 + count) + [HBM] * len(earlier),
        out_specs=HBM,
        scratch_shapes=[
            pltpu.VMEM((count, 2 * pairs[0].shape[1], chans, lanes), BF),
            pltpu.SemaphoreType.DMA((count,)),
        ],
        input_output_aliases={3 + count: 0} if earlier else {},
        compiler_params=params(24),
        name="couple",
    )(y, land, back_weight, *pairs, *earlier)


def local(
    atmos,
    ocean,
    land_mask,
    ice_mask,
    atm_kernel,
    atm_gain,
    atm_up,
    atm_down,
    atm_scale,
    flux_weight,
    flux_lift,
    ocn_kernel,
    ocn_gain,
    ocn_up,
    ocn_down,
    ocn_scale,
    surf_weight,
    back_weight,
):
    members = lax.axis_size("member")
    half = members // 2
    state = atmos[0]
    rows = state.shape[0]
    blocks = rows // SLOTS
    small = 2 * blocks
    atm = (atm_gain, atm_up, atm_down.transpose(0, 2, 1), atm_scale)
    taps = atm_kernel.transpose(1, 2, 0, 3)

    edges = neighbours(pack(state, 2 * small))
    a, band = convolve(0, state, taps, blocks)
    steps = rows // small
    near_steps = (rows // 2) // small - 1
    state, packed = atmos_block(0, False, members, state, a, atm, [*edges, band], small, steps)

    edges = neighbours(packed)
    a, band = convolve(1, state, taps, blocks)
    weights = (*atm, flux_weight.T)
    partly, far_keep, give, flux, halo = atmos_block(
        1, False, members, state, a, weights, [*edges, band], small, steps - near_steps
    )
    far_got = send_xor(give, 1)
    state, keep, give = atmos_block(
        1, True, members, state, a, weights, [partly, flux, halo], small, near_steps
    )
    far_got, give = lax.optimization_barrier((far_got, give))
    far_sums = add_pairs(far_keep, far_got, 0)
    give, *far_sums = lax.optimization_barrier((give, *far_sums))
    sent = [send_xor(far_sums[k], half + 2 * k) for k in reversed(range(len(far_sums)))]
    got = send_xor(give, 1)
    sums = add_pairs(keep, got, 1)
    sent += [send_xor(part, 2 * k + 2) for k, part in enumerate(sums)]
    band, *ready, lift, win = prepare_ocean(
        members, ocn_kernel, ocn_gain, ocn_up, ocn_scale, flux_lift, ocean, sums[0]
    )
    sent = [keep, got] + sent
    mid, packed = force(members, sent, win, land_mask, ice_mask, lift)
    left, right = neighbours(packed)
    a = ocean_conv(mid, band)
    ocean_rows, surface = ocean_block(
        mid, a, left, right, band, land_mask, ready, ocn_down.T, surf_weight.T
    )
    own = make_pair(surface, send_xor(surface, 1))
    rest = tuple(range(half - 1, 0, -1))
    pairs = [send_xor(own, 2 * k) for k in rest]
    out = couple((0,), state, land_mask, back_weight.T, [own], [])
    out = couple(rest, state, land_mask, back_weight.T, pairs, [out])
    return (out[None], ocean_rows)


def solution(mesh):
    in_specs = (
        P("member", None, None, "lon"),
        P(None, None, "lon"),
        P(None, "lon"),
        P(None, "lon"),
    ) + (P(),) * 14
    out_specs = (P("member", None, None, "lon"), P("member", None, "lon"))
    return jax.shard_map(local, mesh=mesh, in_specs=in_specs, out_specs=out_specs, check_vma=False)
```

```python
import functools

import jax
import jax.numpy as jnp
from jax import lax
from jax.experimental import pallas as pl
from jax.experimental.pallas import tpu as pltpu
from jax.sharding import PartitionSpec as P

BF = jnp.bfloat16
F32 = jnp.float32
TANH_A = 0.7978845608028654
TANH_B = TANH_A * 0.044715
TAPS = 7
HALO = 3
GROUP = 16
SPAN = 16
OUT = SPAN - TAPS + 1
DEPTH = GROUP * SPAN
SLOT = 8
SLOTS = 16
OCEAN_BLOCKS = 2
BIG = 32
VMEM = pl.BlockSpec(memory_space=pltpu.VMEM)
ANY = pl.BlockSpec(memory_space=pl.ANY)
HBM = pl.BlockSpec(memory_space=pltpu.HBM)


def params(mib):
    return pltpu.CompilerParams(vmem_limit_bytes=mib * 2**20)


def cost(gflop):
    return pl.CostEstimate(flops=int(gflop * 1e9), bytes_accessed=0, transcendentals=0)


def twice_gelu(z):
    return z + z * jnp.tanh(z * (TANH_A + TANH_B * (z * z)))


def transposed(value):
    return value.astype(F32).T.astype(BF)


def halved(value):
    return (0.5 * value.astype(F32)).astype(BF)


def spread(row, lanes):
    return jnp.broadcast_to(row.T, (row.shape[1], lanes))


def edge_lanes(shape):
    lane = lax.broadcasted_iota(jnp.int32, shape, len(shape) - 1)
    return (lane < HALO) | (lane >= shape[-1] - HALO)


def pack_kernel(step, src_ref, p_ref, x_ref, sems):
    rows, chans, lanes = x_ref.shape
    blocks = p_ref.shape[0]
    copies = []
    for n in range(rows // step):
        at = slice(n * step, (n + 1) * step)
        copies.append(pltpu.make_async_copy(src_ref.at[at], x_ref.at[at], sems.at[n]))
        copies[n].start()
    keep = edge_lanes((chans, lanes)).astype(F32).astype(BF)
    for n in range(rows // step):
        copies[n].wait()
        for q in range(blocks):
            total = None if n == 0 else p_ref[q]
            for slot in range(n * step // blocks, (n + 1) * step // blocks):
                moved = x_ref[slot * blocks + q] * keep
                if slot:
                    moved = pltpu.roll(moved, SLOT * slot, 1)
                total = moved if total is None else total + moved
            p_ref[q] = total


def pack(x, step):
    rows, chans, lanes = x.shape
    return pl.pallas_call(
        functools.partial(pack_kernel, step),
        out_shape=jax.ShapeDtypeStruct((rows // SLOTS, chans, lanes), BF),
        in_specs=[HBM],
        out_specs=VMEM,
        scratch_shapes=[pltpu.VMEM(x.shape, BF), pltpu.SemaphoreType.DMA((rows // step,))],
        compiler_params=params(60),
        name="pack_edges",
    )(x)


def neighbours(packed, wrap_first):
    count = lax.axis_size("lon")
    inner = [(i, i ^ 1) for i in range(count)]
    outer = [(i, (i - 1) % count if i % 2 == 0 else (i + 1) % count) for i in range(count)]
    return [
        lax.ppermute(packed, "lon", pairs)
        for pairs in ((outer, inner) if wrap_first else (inner, outer))
    ]


def by_side(first, second, wrap_first):
    swap = (lax.axis_index("lon") % 2 == 0) != wrap_first
    return jnp.where(swap, second, first), jnp.where(swap, first, second)


def fill_base(taps, base):
    groups, _, wide = base.shape
    chans = groups * GROUP
    tall = TAPS * SLOT
    t = lax.broadcasted_iota(jnp.int32, (tall, wide), 0)
    n = lax.broadcasted_iota(jnp.int32, (tall, wide), 1)
    hit = (t % SLOT == n // DEPTH) & (t // SLOT == (n % DEPTH) // GROUP)
    columns = []
    for i in range(TAPS):
        columns.append(taps(i).T)
        columns.append(jnp.zeros((chans, SLOT - TAPS), F32))
    columns = jnp.concatenate(columns, axis=1).astype(BF)
    total = jnp.dot(columns, hit.astype(F32).astype(BF), preferred_element_type=F32)
    r = lax.broadcasted_iota(jnp.int32, (GROUP, wide), 0)
    c = lax.broadcasted_iota(jnp.int32, (GROUP, wide), 1)
    same = r == c % GROUP
    for g in range(groups):
        base[g] = jnp.where(same, total[GROUP * g : GROUP * (g + 1)], 0.0)


def fill_band(base, g, band):
    for j in range(TAPS):
        one = base[g, :, j * DEPTH : (j + 1) * DEPTH]
        for r in range(OUT):
            moved = pltpu.roll(one, GROUP * r, 1) if r else one
            band[GROUP * r : GROUP * (r + 1), j * DEPTH : (j + 1) * DEPTH] = moved.astype(BF)


def fill_shifts(x, pad, xj):
    count, _, lanes = x.shape
    lane = lax.broadcasted_iota(jnp.int32, (GROUP, lanes), 1)
    for j in range(TAPS):
        d = j - HALO
        if d:
            keep = ((lane < lanes - d) if d > 0 else (lane >= -d)).astype(F32).astype(BF)
            xj[j, pad : pad + count] = pltpu.roll(x, (-d) % lanes, 2) * keep[None]
        else:
            xj[j, pad : pad + count] = x


def clear_pads(pad, count, xj):
    tall, _, lanes = xj.shape[1:]
    for j in range(TAPS):
        if pad:
            xj[j, :pad] = jnp.zeros((pad, GROUP, lanes), BF)
        if tall > pad + count:
            xj[j, pad + count :] = jnp.zeros((tall - pad - count, GROUP, lanes), BF)


def apply_band(band, xj, a_ref):
    rows, _, lanes = a_ref.shape
    starts = [min(OUT * i, max(rows - OUT, 0)) for i in range(-(-rows // OUT))]
    field = jnp.concatenate(
        [
            jnp.concatenate([xj[j, s : s + SPAN].reshape(DEPTH, lanes) for j in range(TAPS)], axis=0)
            for s in starts
        ],
        axis=1,
    )
    out = jnp.dot(band, field, preferred_element_type=F32)
    take = min(OUT, rows)
    for n, s in enumerate(starts):
        part = out[: take * GROUP, n * lanes : (n + 1) * lanes]
        a_ref[s : s + take] = part.reshape(take, GROUP, lanes)


def conv_kernel(layer, x_ref, k_ref, a_ref, band_ref, base, even_xj, odd_xj, even_band, odd_band):
    rows, chans, lanes = x_ref.shape
    groups = chans // GROUP
    fill_base(lambda i: k_ref[i, :, layer, :], base)
    clear_pads(HALO, rows, even_xj)
    clear_pads(HALO, rows, odd_xj)

    def at(g):
        return pl.ds(pl.multiple_of(GROUP * g, GROUP), GROUP)

    def prepare(g, xj, band):
        fill_band(base, g, band)
        band_ref[g] = band[: band_ref.shape[1]]
        fill_shifts(x_ref[:, at(g), :], HALO, xj)

    prepare(0, even_xj, even_band)

    def pair(i, carry):
        prepare(2 * i + 1, odd_xj, odd_band)
        apply_band(even_band[...], even_xj, a_ref.at[:, at(2 * i), :])
        prepare(jnp.minimum(2 * i + 2, groups - 1), even_xj, even_band)
        apply_band(odd_band[...], odd_xj, a_ref.at[:, at(2 * i + 1), :])
        return carry

    lax.fori_loop(0, groups // 2, pair, 0)


def convolve(layer, x, taps, blocks):
    rows, chans, lanes = x.shape
    groups = chans // GROUP
    wide = TAPS * DEPTH
    return pl.pallas_call(
        functools.partial(conv_kernel, layer),
        out_shape=[
            jax.ShapeDtypeStruct((rows, chans, lanes), F32),
            jax.ShapeDtypeStruct((groups, blocks * GROUP, wide), BF),
        ],
        in_specs=[VMEM, VMEM],
        out_specs=[VMEM, VMEM],
        scratch_shapes=[
            pltpu.VMEM((groups, GROUP, wide), F32),
        ]
        + [pltpu.VMEM((TAPS, rows + 2 * HALO, GROUP, lanes), BF)] * 2
        + [pltpu.VMEM((GROUP * OUT, wide), BF)] * 2,
        compiler_params=params(BIG),
        cost_estimate=cost(8),
        name="conv",
    )(x, taps)


def window(members, rows):
    share = rows // members
    span = share + 2 * HALO
    first = lax.axis_index("member") * share - HALO
    return span, first, jnp.clip(first, 0, rows - span)


def prepare_kernel(members, k_ref, g_ref, up_ref, s_ref, lift_ref, ocean_ref, _, *refs):
    band_ref, mat_ref, upt_ref, gain_ref, scale_ref, lift_out, win_ref, base, sem = refs
    lanes = gain_ref.shape[1]
    span, _, start = window(members, ocean_ref.shape[0])
    copy = pltpu.make_async_copy(ocean_ref.at[pl.ds(start, span)], win_ref, sem)
    copy.start()
    mat_ref[...] = halo_matrix(lanes)
    upt_ref[...] = transposed(up_ref[...])
    gain_ref[...] = spread(g_ref[...], lanes)
    scale_ref[...] = spread(s_ref[...], lanes)
    lift_out[...] = jnp.concatenate([transposed(lift_ref[0]), transposed(lift_ref[1])], axis=0)
    fill_base(lambda i: k_ref[i], base)
    for g in range(base.shape[0]):
        fill_band(base, g, band_ref.at[g])
    copy.wait()


def prepare_ocean(members, taps, gain, up, scale, lift, ocean, after):
    chans, hid = up.shape
    rows, _, lanes = ocean.shape
    flux = lift.shape[1]
    groups = chans // GROUP
    wide = TAPS * DEPTH
    span = rows // members + 2 * HALO
    return pl.pallas_call(
        functools.partial(prepare_kernel, members),
        out_shape=[
            jax.ShapeDtypeStruct((groups, GROUP * OUT, wide), BF),
            jax.ShapeDtypeStruct((2 * lanes, (TAPS - 1) * lanes), BF),
            jax.ShapeDtypeStruct((hid, chans), BF),
            jax.ShapeDtypeStruct((chans, lanes), F32),
            jax.ShapeDtypeStruct((chans, lanes), F32),
            jax.ShapeDtypeStruct((2 * chans, flux), BF),
            jax.ShapeDtypeStruct((span, chans, lanes), BF),
        ],
        in_specs=[VMEM] * 5 + [HBM, ANY],
        out_specs=[VMEM] * 7,
        scratch_shapes=[pltpu.VMEM((groups, GROUP, wide), F32), pltpu.SemaphoreType.DMA(())],
        compiler_params=params(24),
        cost_estimate=cost(3),
        name="prepare_ocean",
    )(taps, gain[None], up, scale[None], lift, ocean, after)


def ocean_conv_kernel(x_ref, band_ref, a_ref, xj):
    count, chans, lanes = x_ref.shape
    for g in range(chans // GROUP):
        at = slice(GROUP * g, GROUP * (g + 1))
        clear_pads(0, count, xj.at[g])
        fill_shifts(x_ref[:, at, :], 0, xj.at[g])
        apply_band(band_ref[g], xj.at[g], a_ref.at[:, at, :])


def ocean_conv(x, band):
    count, chans, lanes = x.shape
    return pl.pallas_call(
        ocean_conv_kernel,
        out_shape=jax.ShapeDtypeStruct((count - 2 * HALO, chans, lanes), F32),
        in_specs=[VMEM, VMEM],
        out_specs=VMEM,
        scratch_shapes=[pltpu.VMEM((chans // GROUP, TAPS, max(count, SPAN), GROUP, lanes), BF)],
        compiler_params=params(24),
        cost_estimate=cost(2),
        name="ocean_conv",
    )(x, band)


def halo_matrix(lanes):
    shape = (lanes, lanes)
    src = lax.broadcasted_iota(jnp.int32, shape, 0)
    dst = lax.broadcasted_iota(jnp.int32, shape, 1)
    ahead = (src - dst + lanes) % lanes
    right = (src % SLOT < HALO) & (dst % SLOT >= SLOT - HALO)
    left = (src % SLOT >= SLOT - HALO) & (dst % SLOT < HALO)
    right = jnp.where(right, ahead, -1)
    left = jnp.where(left, ahead, -1)
    none = jnp.zeros(shape, BF)
    upper, lower = [], []
    for j in range(TAPS):
        d = j - HALO
        if d > 0:
            upper.append((right == d).astype(F32).astype(BF))
            lower.append(none)
        elif d < 0:
            upper.append(none)
            lower.append((left == lanes + d).astype(F32).astype(BF))
    return jnp.concatenate(
        [jnp.concatenate(upper, axis=1), jnp.concatenate(lower, axis=1)], axis=0
    )


def halo_conv(first, second, band, wrapped, matrix, xe, halo):
    blocks, chans, lanes = halo.shape
    both = []
    for q in range(blocks):
        left, right = by_side(first[q], second[q], wrapped)
        both.append(jnp.concatenate([right, left], axis=1))
    lane = lax.broadcasted_iota(jnp.int32, (chans, lanes), 1)
    slot = (lane + HALO) // SLOT % SLOTS

    def turned(value, shift, drop):
        parts = [pltpu.roll(value[:, n * lanes : (n + 1) * lanes], shift, 1) for n in range(2)]
        if drop >= 0:
            keep = (slot != drop).astype(F32).astype(BF)
            parts = [part * keep for part in parts]
        return jnp.concatenate(parts, axis=1)

    if wrapped:
        tall = (
            [turned(both[q], SLOT, 0) for q in range(blocks - HALO, blocks)]
            + both
            + [turned(both[q], lanes - SLOT, SLOTS - 1) for q in range(HALO)]
        )
    else:
        tall = both + [
            turned(both[e % blocks], lanes - SLOT * (e // blocks), -1)
            for e in range(blocks, blocks + 2 * HALO)
        ]
    field = jnp.concatenate(tall, axis=0)
    moved = jnp.dot(field, matrix, preferred_element_type=F32)
    count = len(tall)
    span = xe.shape[1]
    for a in range(TAPS - 1):
        part = moved[:, a * lanes : (a + 1) * lanes].astype(BF)
        xe[a, :count] = part.reshape(count, chans, lanes)
        if count < span:
            xe[a, count:] = jnp.zeros((span - count, chans, lanes), BF)
    tops = slice(0, blocks * GROUP)
    side = [j for j in range(TAPS) if j != HALO]
    for g in range(chans // GROUP):
        at = slice(GROUP * g, GROUP * (g + 1))
        rhs = jnp.concatenate(
            [xe[a, :, at, :].reshape(span * GROUP, lanes) for a in range(TAPS - 1)], axis=0
        )
        lhs = jnp.concatenate(
            [band[g, tops, j * DEPTH : j * DEPTH + span * GROUP] for j in side], axis=1
        )
        out = jnp.dot(lhs, rhs, preferred_element_type=F32)
        halo[:, at, :] = out.reshape(blocks, GROUP, lanes)


def turned_by(value, slots):
    lanes = value.shape[-1]
    if isinstance(slots, int):
        shift = SLOT * slots % lanes
        return pltpu.roll(value, shift, 1) if shift else value
    return pltpu.roll(value, lax.rem(SLOT * slots + lanes, lanes), 1)


def norm_rows(a_ref, base, off, count, halo, gain, out):
    _, chans, lanes = a_ref.shape
    blocks = halo.shape[0]
    edge = edge_lanes((chans, lanes))
    for r in range(count):
        extra = turned_by(halo[(off + r) % blocks], -(base // blocks + (off + r) // blocks))
        a = a_ref[base + off + r] + jnp.where(edge, extra, 0.0)
        center = a - jnp.mean(a, axis=0, keepdims=True)
        var = jnp.mean(center * center, axis=0, keepdims=True)
        normed = (center * lax.rsqrt(var + 1e-06) * gain).astype(BF)
        out[:, r * lanes : (r + 1) * lanes] = normed


def branch_of(normed, up_t, down_t):
    z = jnp.dot(up_t, normed, preferred_element_type=F32)
    h = twice_gelu(z.astype(BF))
    return jnp.dot(down_t, h, preferred_element_type=F32)


def atmos_kernel(layer, near, members, count, steps, *refs):
    x_ref, a_ref, g_ref, up_ref, dn_ref, s_ref = refs[:6]
    refs = refs[6:]
    even, odd = refs[-2:]
    rows, chans, lanes = x_ref.shape
    base = 0
    if layer == 0:
        first_ref, second_ref, band_ref, y_ref, p_ref, xe, halo = refs[:-2]
        blocks = halo.shape[0]
        packed = [None] * blocks
        keep = edge_lanes((chans, lanes)).astype(F32).astype(BF)
    else:
        rank = lax.axis_index("member")
        half = members // 2
        upper = (rank >= half) if near else (rank < half)
        base = jnp.where(upper, rows - steps * count, 0)
        if near:
            fw_ref, _, old_ref, halo, y_ref, keep_ref, give_ref, flux = refs[:-2]
        else:
            fw_ref, first_ref, second_ref, band_ref = refs[:4]
            y_ref, keep_ref, give_ref, flux, halo, xe = refs[4:-2]
    if near:
        flux[...] = old_ref[...]
    else:
        halo_conv(first_ref, second_ref, band_ref, True, halo_matrix(lanes), xe, halo)
        if layer == 1:
            blank = jnp.zeros((HALO,) + flux.shape[1:], BF)
            flux[0:HALO] = blank
            flux[rows + HALO : rows + 2 * HALO] = blank
    up_t = transposed(up_ref[layer])
    dn_t = halved(dn_ref[layer])
    gain = spread(g_ref[layer : layer + 1], lanes)
    scale = spread(s_ref[layer : layer + 1], lanes)
    norm_rows(a_ref, base, 0, count, halo, gain, even)
    for step in range(steps):
        off = step * count
        now, later = (even, odd) if step % 2 == 0 else (odd, even)
        if step + 1 < steps:
            norm_rows(a_ref, base, off + count, count, halo, gain, later)
        branch = branch_of(now[...], up_t, dn_t)
        made = []
        for r in range(count):
            y = x_ref[base + off + r].astype(F32) + scale * branch[:, r * lanes : (r + 1) * lanes]
            made.append(y.astype(BF))
            y_ref[base + off + r] = made[r]
        if layer == 0:
            for r in range(count):
                q, slot = (off + r) % blocks, (off + r) // blocks
                moved = turned_by(made[r] * keep, slot)
                packed[q] = moved if packed[q] is None else packed[q] + moved
            if step % 4 == 3 or step + 1 == steps:
                for q in range(blocks):
                    p_ref[q] = packed[q] if step < 4 else p_ref[q] + packed[q]
                packed = [None] * blocks
        else:
            z = jnp.dot(fw_ref[...], jnp.concatenate(made, axis=1), preferred_element_type=F32)
            f = (0.5 * twice_gelu(z)).astype(BF)
            for r in range(count):
                flux[base + off + HALO + r] = f[:, r * lanes : (r + 1) * lanes]
    if layer == 1:
        share = rows // members
        for k in range(half):
            dst = rank ^ (k if near else half + k)
            chunk = flux[pl.ds(dst * share, share + 2 * HALO)]
            if k % 2:
                give_ref[k // 2] = chunk
            else:
                keep_ref[k // 2] = chunk


def atmos_block(layer, near, members, x, a, weights, others, count, steps):
    rows, chans, lanes = x.shape
    blocks = rows // SLOTS
    args = [x, a, *weights, *others]
    outs = [jax.ShapeDtypeStruct(x.shape, BF)]
    halo = jax.ShapeDtypeStruct((blocks, chans, lanes), F32)
    shifts = pltpu.VMEM((TAPS - 1, SPAN, chans, lanes), BF)
    if layer == 0:
        outs.append(jax.ShapeDtypeStruct((blocks, chans, lanes), BF))
        scratch = [shifts, pltpu.VMEM(halo.shape, F32)]
    else:
        flux = weights[-1].shape[0]
        share = rows // members
        field = (rows + 2 * HALO, flux, lanes)
        outs += [jax.ShapeDtypeStruct((members // 4, share + 2 * HALO, flux, lanes), BF)] * 2
        if near:
            scratch = [pltpu.VMEM(field, BF)]
        else:
            outs += [jax.ShapeDtypeStruct(field, BF), halo]
            scratch = [shifts]
    return pl.pallas_call(
        functools.partial(atmos_kernel, layer, near, members, count, steps),
        out_shape=outs,
        in_specs=[VMEM] * len(args),
        out_specs=[VMEM] * len(outs),
        scratch_shapes=scratch + [pltpu.VMEM((chans, count * lanes), BF)] * 2,
        input_output_aliases={7: 0} if near else {},
        compiler_params=params(BIG),
        cost_estimate=cost(8 * steps * count / rows),
        name="atmos_block",
    )(*args)


def add_kernel(keep_ref, got_ref, *out_refs):
    for n, ref in enumerate(out_refs):
        k = n + keep_ref.shape[0] - len(out_refs)
        ref[...] = (keep_ref[k].astype(F32) + got_ref[k].astype(F32)).astype(BF)


def add_pairs(keep, got, skip):
    count = keep.shape[0] - skip
    return pl.pallas_call(
        add_kernel,
        out_shape=[jax.ShapeDtypeStruct(keep.shape[1:], BF)] * count,
        in_specs=[VMEM] * 2,
        out_specs=[VMEM] * count,
        compiler_params=params(24),
        name="add_pairs",
    )(keep, got)


def send_xor(value, bits):
    members = lax.axis_size("member")
    return lax.ppermute(value, "member", [(i, i ^ bits) for i in range(members)])


def force_kernel(members, *refs):
    near_refs, flux_refs = refs[:2], refs[2 : members // 2 + 1]
    win_ref, land_ref, ice_ref, lift_ref, mid_ref, p_ref = refs[members // 2 + 1 :]
    lanes = land_ref.shape[1]
    rows = land_ref.shape[0]
    chans = mid_ref.shape[1]
    blocks = p_ref.shape[0]
    span, first, start = window(members, rows)
    total = near_refs[0][0].astype(F32) + near_refs[1][0].astype(F32)
    for ref in flux_refs:
        total = total + ref[...].astype(F32)
    low = (total / members).astype(BF)
    columns = jnp.concatenate([low[r] for r in range(span)], axis=1)
    terms = jnp.dot(lift_ref[...], columns, preferred_element_type=F32)
    keep = edge_lanes((chans, lanes)).astype(F32).astype(BF)
    packed = [None] * blocks
    for r in range(span):
        row = first + r
        safe = jnp.clip(row, 0, rows - 1)
        sea = (1 - land_ref[pl.ds(safe, 1), :]).astype(F32)
        ice = ice_ref[pl.ds(safe, 1), :].astype(F32)
        at = slice(r * lanes, (r + 1) * lanes)
        forcing = sea * ((1.0 - ice) * terms[:chans, at] + ice * terms[chans:, at])
        mid = win_ref[jnp.clip(row - start, 0, span - 1)].astype(F32) + forcing
        inside = (row >= 0) & (row < rows)
        mid = jnp.where(inside, mid, 0.0).astype(BF)
        mid_ref[r] = mid
        q, slot = r % blocks, r // blocks
        moved = mid * keep
        if slot:
            moved = pltpu.roll(moved, SLOT * slot, 1)
        packed[q] = moved if packed[q] is None else packed[q] + moved
    for q in range(blocks):
        p_ref[q] = packed[q]


def force(members, chunks, win, land, ice, lift):
    span, chans, lanes = win.shape
    return pl.pallas_call(
        functools.partial(force_kernel, members),
        out_shape=[
            jax.ShapeDtypeStruct((span, chans, lanes), BF),
            jax.ShapeDtypeStruct((OCEAN_BLOCKS, chans, lanes), BF),
        ],
        in_specs=[VMEM] * (len(chunks) + 4),
        out_specs=[VMEM] * 2,
        compiler_params=params(24),
        name="ocean_forcing",
    )(*chunks, win, land, ice, lift)


def ocean_kernel(mid_ref, a_ref, first_ref, second_ref, band_ref, land_ref, mat_ref, upt_ref, gain_ref, scale_ref, dn_ref, sw_ref, new_ref, surf_ref, xe, halo, normed):
    share, chans, lanes = new_ref.shape
    halo_conv(first_ref, second_ref, band_ref, False, mat_ref[...], xe, halo)
    scale = scale_ref[...]
    norm_rows(a_ref, 0, 0, share, halo, gain_ref[...], normed)
    branch = branch_of(normed[...], upt_ref[...], halved(dn_ref[...]))
    first = lax.axis_index("member") * share
    made = []
    for r in range(share):
        sea = (1 - land_ref[pl.ds(first + r, 1), :]).astype(F32)
        y = mid_ref[HALO + r].astype(F32) + scale * branch[:, r * lanes : (r + 1) * lanes]
        made.append((y * sea).astype(BF))
        new_ref[r] = made[r]
    surf = jnp.dot(
        sw_ref[...], jnp.concatenate(made, axis=1), preferred_element_type=F32
    )
    for r in range(share):
        surf_ref[r] = surf[:, r * lanes : (r + 1) * lanes].astype(BF)


def ocean_block(mid, a, edges, band, land, ready, down, surf_weight):
    share, chans, lanes = a.shape
    blocks = edges[0].shape[0]
    return pl.pallas_call(
        ocean_kernel,
        out_shape=[
            jax.ShapeDtypeStruct((share, chans, lanes), BF),
            jax.ShapeDtypeStruct((share, surf_weight.shape[0], lanes), BF),
        ],
        in_specs=[VMEM] * 12,
        out_specs=[VMEM] * 2,
        scratch_shapes=[
            pltpu.VMEM((TAPS - 1, OCEAN_BLOCKS + 2 * HALO, chans, lanes), BF),
            pltpu.VMEM((blocks, chans, lanes), F32),
            pltpu.VMEM((chans, share * lanes), BF),
        ],
        compiler_params=params(24),
        name="ocean_block",
    )(mid, a, *edges, band, land, *ready, down, surf_weight)


def pair_kernel(own_ref, got_ref, out_ref):
    out_ref[0] = own_ref[...]
    out_ref[1] = got_ref[...]


def make_pair(own, got):
    return pl.pallas_call(
        pair_kernel,
        out_shape=jax.ShapeDtypeStruct((2,) + own.shape, BF),
        in_specs=[VMEM] * 2,
        out_specs=VMEM,
        compiler_params=params(24),
        name="surface_pair",
    )(own, got)


def couple_kernel(ks, y_ref, land_ref, bw_ref, *refs):
    pair_refs = refs[: len(ks)]
    o_ref, buf, sems = refs[-3:]
    chans, lanes = y_ref.shape[1:]
    share = pair_refs[0].shape[1]
    rank = lax.axis_index("member")
    parity = rank % 2
    copies = []
    for n, (k, pair_ref) in enumerate(zip(ks, pair_refs)):
        first = ((rank // 2) ^ k) * 2 * share
        surf = [pair_ref[side ^ parity, r] for side in range(2) for r in range(share)]
        back = jnp.dot(bw_ref[...], jnp.concatenate(surf, axis=1), preferred_element_type=F32)
        for r in range(2 * share):
            sea = (1 - land_ref[pl.ds(first + r, 1), :]).astype(F32)
            out = y_ref[first + r].astype(F32) + sea * back[:, r * lanes : (r + 1) * lanes]
            buf[n, r] = out.astype(BF)
        copies.append(
            pltpu.make_async_copy(buf.at[n], o_ref.at[pl.ds(first, 2 * share)], sems.at[n])
        )
        copies[n].start()
    for copy in copies:
        copy.wait()


def couple(ks, y, land, back_weight, pairs, earlier):
    _, chans, lanes = y.shape
    count = len(ks)
    return pl.pallas_call(
        functools.partial(couple_kernel, ks),
        out_shape=jax.ShapeDtypeStruct(y.shape, BF),
        in_specs=[VMEM] * (3 + count) + [HBM] * len(earlier),
        out_specs=HBM,
        scratch_shapes=[
            pltpu.VMEM((count, 2 * pairs[0].shape[1], chans, lanes), BF),
            pltpu.SemaphoreType.DMA((count,)),
        ],
        input_output_aliases={3 + count: 0} if earlier else {},
        compiler_params=params(24),
        name="couple",
    )(y, land, back_weight, *pairs, *earlier)


def local(
    atmos,
    ocean,
    land_mask,
    ice_mask,
    atm_kernel,
    atm_gain,
    atm_up,
    atm_down,
    atm_scale,
    flux_weight,
    flux_lift,
    ocn_kernel,
    ocn_gain,
    ocn_up,
    ocn_down,
    ocn_scale,
    surf_weight,
    back_weight,
):
    members = lax.axis_size("member")
    half = members // 2
    state = atmos[0]
    rows = state.shape[0]
    blocks = rows // SLOTS
    small = 2 * blocks
    atm = (atm_gain, atm_up, atm_down.transpose(0, 2, 1), atm_scale)
    taps = atm_kernel.transpose(1, 2, 0, 3)

    edges = neighbours(pack(state, 2 * small), True)
    a, band = convolve(0, state, taps, blocks)
    steps = rows // small
    near_steps = (rows // 2) // small - 1
    state, packed = atmos_block(0, False, members, state, a, atm, [*edges, band], small, steps)

    edges = neighbours(packed, True)
    a, band = convolve(1, state, taps, blocks)
    weights = (*atm, flux_weight.T)
    partly, far_keep, give, flux, halo = atmos_block(
        1, False, members, state, a, weights, [*edges, band], small, steps - near_steps
    )
    far_got = send_xor(give, 1)
    state, keep, give = atmos_block(
        1, True, members, state, a, weights, [partly, flux, halo], small, near_steps
    )
    far_got, give = lax.optimization_barrier((far_got, give))
    far_sums = add_pairs(far_keep, far_got, 0)
    give, *far_sums = lax.optimization_barrier((give, *far_sums))
    sent = [send_xor(far_sums[k], half + 2 * k) for k in reversed(range(len(far_sums)))]
    got = send_xor(give, 1)
    sums = add_pairs(keep, got, 1)
    sent += [send_xor(part, 2 * k + 2) for k, part in enumerate(sums)]
    band, *ready, lift, win = prepare_ocean(
        members, ocn_kernel, ocn_gain, ocn_up, ocn_scale, flux_lift, ocean, sums[0]
    )
    sent = [keep, got] + sent
    mid, packed = force(members, sent, win, land_mask, ice_mask, lift)
    edges = neighbours(packed, False)
    a = ocean_conv(mid, band)
    ocean_rows, surface = ocean_block(
        mid, a, edges, band, land_mask, ready, ocn_down.T, surf_weight.T
    )
    own = make_pair(surface, send_xor(surface, 1))
    rest = tuple(range(half - 1, 0, -1))
    pairs = [send_xor(own, 2 * k) for k in rest]
    out = couple((0,), state, land_mask, back_weight.T, [own], [])
    out = couple(rest, state, land_mask, back_weight.T, pairs, [out])
    return (out[None], ocean_rows)


def solution(mesh):
    in_specs = (
        P("member", None, None, "lon"),
        P(None, None, "lon"),
        P(None, "lon"),
        P(None, "lon"),
    ) + (P(),) * 14
    out_specs = (P("member", None, None, "lon"), P("member", None, "lon"))
    return jax.shard_map(local, mesh=mesh, in_specs=in_specs, out_specs=out_specs, check_vma=False)
```

```python
import functools

import jax
import jax.numpy as jnp
from jax import lax
from jax.experimental import pallas as pl
from jax.experimental.pallas import tpu as pltpu
from jax.sharding import PartitionSpec as P

BF = jnp.bfloat16
F32 = jnp.float32
TANH_A = 0.7978845608028654
TANH_B = TANH_A * 0.044715
TAPS = 7
HALO = 3
GROUP = 16
SPAN = 16
OUT = SPAN - TAPS + 1
DEPTH = GROUP * SPAN
SLOT = 8
SLOTS = 16
OCEAN_BLOCKS = 2
BIG = 32
VMEM = pl.BlockSpec(memory_space=pltpu.VMEM)
ANY = pl.BlockSpec(memory_space=pl.ANY)
HBM = pl.BlockSpec(memory_space=pltpu.HBM)


def params(mib):
    return pltpu.CompilerParams(vmem_limit_bytes=mib * 2**20)


def cost(gflop):
    return pl.CostEstimate(flops=int(gflop * 1e9), bytes_accessed=0, transcendentals=0)


def twice_gelu(z):
    return z + z * jnp.tanh(z * (TANH_A + TANH_B * (z * z)))


def transposed(value):
    return value.astype(F32).T.astype(BF)


def halved(value):
    return (0.5 * value.astype(F32)).astype(BF)


def spread(row, lanes):
    return jnp.broadcast_to(row.T, (row.shape[1], lanes))


def edge_lanes(shape):
    lane = lax.broadcasted_iota(jnp.int32, shape, len(shape) - 1)
    return (lane < HALO) | (lane >= shape[-1] - HALO)


def pack_kernel(step, src_ref, p_ref, x_ref, sems):
    rows, chans, lanes = x_ref.shape
    blocks = p_ref.shape[0]
    copies = []
    for n in range(rows // step):
        at = slice(n * step, (n + 1) * step)
        copies.append(pltpu.make_async_copy(src_ref.at[at], x_ref.at[at], sems.at[n]))
        copies[n].start()
    keep = edge_lanes((chans, lanes)).astype(F32).astype(BF)
    for n in range(rows // step):
        copies[n].wait()
        for q in range(blocks):
            total = None if n == 0 else p_ref[q]
            for slot in range(n * step // blocks, (n + 1) * step // blocks):
                moved = x_ref[slot * blocks + q] * keep
                if slot:
                    moved = pltpu.roll(moved, SLOT * slot, 1)
                total = moved if total is None else total + moved
            p_ref[q] = total


def pack(x, step):
    rows, chans, lanes = x.shape
    return pl.pallas_call(
        functools.partial(pack_kernel, step),
        out_shape=jax.ShapeDtypeStruct((rows // SLOTS, chans, lanes), BF),
        in_specs=[HBM],
        out_specs=VMEM,
        scratch_shapes=[pltpu.VMEM(x.shape, BF), pltpu.SemaphoreType.DMA((rows // step,))],
        compiler_params=params(60),
        name="pack_edges",
    )(x)


def neighbours(packed, wrap_first):
    count = lax.axis_size("lon")
    inner = [(i, i ^ 1) for i in range(count)]
    outer = [(i, (i - 1) % count if i % 2 == 0 else (i + 1) % count) for i in range(count)]
    return [
        lax.ppermute(packed, "lon", pairs)
        for pairs in ((outer, inner) if wrap_first else (inner, outer))
    ]


def by_side(first, second, wrap_first):
    swap = (lax.axis_index("lon") % 2 == 0) != wrap_first
    return jnp.where(swap, second, first), jnp.where(swap, first, second)


def fill_base(taps, base):
    groups, _, wide = base.shape
    chans = groups * GROUP
    tall = TAPS * SLOT
    t = lax.broadcasted_iota(jnp.int32, (tall, wide), 0)
    n = lax.broadcasted_iota(jnp.int32, (tall, wide), 1)
    hit = (t % SLOT == n // DEPTH) & (t // SLOT == (n % DEPTH) // GROUP)
    columns = []
    for i in range(TAPS):
        columns.append(taps(i).T)
        columns.append(jnp.zeros((chans, SLOT - TAPS), F32))
    columns = jnp.concatenate(columns, axis=1).astype(BF)
    total = jnp.dot(columns, hit.astype(F32).astype(BF), preferred_element_type=F32)
    r = lax.broadcasted_iota(jnp.int32, (GROUP, wide), 0)
    c = lax.broadcasted_iota(jnp.int32, (GROUP, wide), 1)
    same = r == c % GROUP
    for g in range(groups):
        base[g] = jnp.where(same, total[GROUP * g : GROUP * (g + 1)], 0.0)


def fill_band(base, g, band):
    for j in range(TAPS):
        one = base[g, :, j * DEPTH : (j + 1) * DEPTH]
        for r in range(OUT):
            moved = pltpu.roll(one, GROUP * r, 1) if r else one
            band[GROUP * r : GROUP * (r + 1), j * DEPTH : (j + 1) * DEPTH] = moved.astype(BF)


def fill_shifts(x, pad, xj):
    count, _, lanes = x.shape
    lane = lax.broadcasted_iota(jnp.int32, (GROUP, lanes), 1)
    for j in range(TAPS):
        d = j - HALO
        if d:
            keep = ((lane < lanes - d) if d > 0 else (lane >= -d)).astype(F32).astype(BF)
            xj[j, pad : pad + count] = pltpu.roll(x, (-d) % lanes, 2) * keep[None]
        else:
            xj[j, pad : pad + count] = x


def clear_pads(pad, count, xj):
    tall, _, lanes = xj.shape[1:]
    for j in range(TAPS):
        if pad:
            xj[j, :pad] = jnp.zeros((pad, GROUP, lanes), BF)
        if tall > pad + count:
            xj[j, pad + count :] = jnp.zeros((tall - pad - count, GROUP, lanes), BF)


def apply_band(band, xj, a_ref):
    rows, _, lanes = a_ref.shape
    starts = [min(OUT * i, max(rows - OUT, 0)) for i in range(-(-rows // OUT))]
    field = jnp.concatenate(
        [
            jnp.concatenate([xj[j, s : s + SPAN].reshape(DEPTH, lanes) for j in range(TAPS)], axis=0)
            for s in starts
        ],
        axis=1,
    )
    out = jnp.dot(band, field, preferred_element_type=F32)
    take = min(OUT, rows)
    for n, s in enumerate(starts):
        part = out[: take * GROUP, n * lanes : (n + 1) * lanes]
        a_ref[s : s + take] = part.reshape(take, GROUP, lanes)


def conv_kernel(layer, x_ref, k_ref, a_ref, band_ref, base, even_xj, odd_xj, even_band, odd_band):
    rows, chans, lanes = x_ref.shape
    groups = chans // GROUP
    fill_base(lambda i: k_ref[i, :, layer, :], base)
    clear_pads(HALO, rows, even_xj)
    clear_pads(HALO, rows, odd_xj)

    def at(g):
        return pl.ds(pl.multiple_of(GROUP * g, GROUP), GROUP)

    def prepare(g, xj, band):
        fill_band(base, g, band)
        band_ref[g] = band[: band_ref.shape[1]]
        fill_shifts(x_ref[:, at(g), :], HALO, xj)

    prepare(0, even_xj, even_band)

    def pair(i, carry):
        prepare(2 * i + 1, odd_xj, odd_band)
        apply_band(even_band[...], even_xj, a_ref.at[:, at(2 * i), :])
        prepare(jnp.minimum(2 * i + 2, groups - 1), even_xj, even_band)
        apply_band(odd_band[...], odd_xj, a_ref.at[:, at(2 * i + 1), :])
        return carry

    lax.fori_loop(0, groups // 2, pair, 0)


def convolve(layer, x, taps, blocks):
    rows, chans, lanes = x.shape
    groups = chans // GROUP
    wide = TAPS * DEPTH
    return pl.pallas_call(
        functools.partial(conv_kernel, layer),
        out_shape=[
            jax.ShapeDtypeStruct((rows, chans, lanes), F32),
            jax.ShapeDtypeStruct((groups, blocks * GROUP, wide), BF),
        ],
        in_specs=[VMEM, VMEM],
        out_specs=[VMEM, VMEM],
        scratch_shapes=[
            pltpu.VMEM((groups, GROUP, wide), F32),
        ]
        + [pltpu.VMEM((TAPS, rows + 2 * HALO, GROUP, lanes), BF)] * 2
        + [pltpu.VMEM((GROUP * OUT, wide), BF)] * 2,
        compiler_params=params(BIG),
        cost_estimate=cost(8),
        name="conv",
    )(x, taps)


def window(members, rows):
    share = rows // members
    span = share + 2 * HALO
    first = lax.axis_index("member") * share - HALO
    return span, first, jnp.clip(first, 0, rows - span)


def prepare_kernel(members, k_ref, g_ref, up_ref, s_ref, lift_ref, ocean_ref, _, *refs):
    band_ref, mat_ref, upt_ref, gain_ref, scale_ref, lift_out, win_ref, base, sem = refs
    lanes = gain_ref.shape[1]
    span, _, start = window(members, ocean_ref.shape[0])
    copy = pltpu.make_async_copy(ocean_ref.at[pl.ds(start, span)], win_ref, sem)
    copy.start()
    mat_ref[...] = halo_matrix(lanes)
    upt_ref[...] = transposed(up_ref[...])
    gain_ref[...] = spread(g_ref[...], lanes)
    scale_ref[...] = spread(s_ref[...], lanes)
    lift_out[...] = jnp.concatenate([transposed(lift_ref[0]), transposed(lift_ref[1])], axis=0)
    fill_base(lambda i: k_ref[i], base)
    for g in range(base.shape[0]):
        fill_band(base, g, band_ref.at[g])
    copy.wait()


def prepare_ocean(members, taps, gain, up, scale, lift, ocean, after):
    chans, hid = up.shape
    rows, _, lanes = ocean.shape
    flux = lift.shape[1]
    groups = chans // GROUP
    wide = TAPS * DEPTH
    span = rows // members + 2 * HALO
    return pl.pallas_call(
        functools.partial(prepare_kernel, members),
        out_shape=[
            jax.ShapeDtypeStruct((groups, GROUP * OUT, wide), BF),
            jax.ShapeDtypeStruct((2 * lanes, (TAPS - 1) * lanes), BF),
            jax.ShapeDtypeStruct((hid, chans), BF),
            jax.ShapeDtypeStruct((chans, lanes), F32),
            jax.ShapeDtypeStruct((chans, lanes), F32),
            jax.ShapeDtypeStruct((2 * chans, flux), BF),
            jax.ShapeDtypeStruct((span, chans, lanes), BF),
        ],
        in_specs=[VMEM] * 5 + [HBM, ANY],
        out_specs=[VMEM] * 7,
        scratch_shapes=[pltpu.VMEM((groups, GROUP, wide), F32), pltpu.SemaphoreType.DMA(())],
        compiler_params=params(24),
        cost_estimate=cost(3),
        name="prepare_ocean",
    )(taps, gain[None], up, scale[None], lift, ocean, after)


def ocean_conv_kernel(x_ref, band_ref, a_ref, xj):
    count, chans, lanes = x_ref.shape
    for g in range(chans // GROUP):
        at = slice(GROUP * g, GROUP * (g + 1))
        clear_pads(0, count, xj.at[g])
        fill_shifts(x_ref[:, at, :], 0, xj.at[g])
        apply_band(band_ref[g], xj.at[g], a_ref.at[:, at, :])


def ocean_conv(x, band):
    count, chans, lanes = x.shape
    return pl.pallas_call(
        ocean_conv_kernel,
        out_shape=jax.ShapeDtypeStruct((count - 2 * HALO, chans, lanes), F32),
        in_specs=[VMEM, VMEM],
        out_specs=VMEM,
        scratch_shapes=[pltpu.VMEM((chans // GROUP, TAPS, max(count, SPAN), GROUP, lanes), BF)],
        compiler_params=params(24),
        cost_estimate=cost(2),
        name="ocean_conv",
    )(x, band)


def halo_matrix(lanes):
    shape = (lanes, lanes)
    src = lax.broadcasted_iota(jnp.int32, shape, 0)
    dst = lax.broadcasted_iota(jnp.int32, shape, 1)
    ahead = (src - dst + lanes) % lanes
    right = (src % SLOT < HALO) & (dst % SLOT >= SLOT - HALO)
    left = (src % SLOT >= SLOT - HALO) & (dst % SLOT < HALO)
    right = jnp.where(right, ahead, -1)
    left = jnp.where(left, ahead, -1)
    none = jnp.zeros(shape, BF)
    upper, lower = [], []
    for j in range(TAPS):
        d = j - HALO
        if d > 0:
            upper.append((right == d).astype(F32).astype(BF))
            lower.append(none)
        elif d < 0:
            upper.append(none)
            lower.append((left == lanes + d).astype(F32).astype(BF))
    return jnp.concatenate(
        [jnp.concatenate(upper, axis=1), jnp.concatenate(lower, axis=1)], axis=0
    )


def halo_conv(first, second, band, wrapped, matrix, xe, halo):
    blocks, chans, lanes = halo.shape
    both = []
    for q in range(blocks):
        left, right = by_side(first[q], second[q], wrapped)
        both.append(jnp.concatenate([right, left], axis=1))
    lane = lax.broadcasted_iota(jnp.int32, (chans, lanes), 1)
    slot = (lane + HALO) // SLOT % SLOTS

    def turned(value, shift, drop):
        parts = [pltpu.roll(value[:, n * lanes : (n + 1) * lanes], shift, 1) for n in range(2)]
        if drop >= 0:
            keep = (slot != drop).astype(F32).astype(BF)
            parts = [part * keep for part in parts]
        return jnp.concatenate(parts, axis=1)

    if wrapped:
        tall = (
            [turned(both[q], SLOT, 0) for q in range(blocks - HALO, blocks)]
            + both
            + [turned(both[q], lanes - SLOT, SLOTS - 1) for q in range(HALO)]
        )
    else:
        tall = both + [
            turned(both[e % blocks], lanes - SLOT * (e // blocks), -1)
            for e in range(blocks, blocks + 2 * HALO)
        ]
    field = jnp.concatenate(tall, axis=0)
    moved = jnp.dot(field, matrix, preferred_element_type=F32)
    count = len(tall)
    span = xe.shape[1]
    for a in range(TAPS - 1):
        part = moved[:, a * lanes : (a + 1) * lanes].astype(BF)
        xe[a, :count] = part.reshape(count, chans, lanes)
        if count < span:
            xe[a, count:] = jnp.zeros((span - count, chans, lanes), BF)
    tops = slice(0, blocks * GROUP)
    side = [j for j in range(TAPS) if j != HALO]
    for g in range(chans // GROUP):
        at = slice(GROUP * g, GROUP * (g + 1))
        rhs = jnp.concatenate(
            [xe[a, :, at, :].reshape(span * GROUP, lanes) for a in range(TAPS - 1)], axis=0
        )
        lhs = jnp.concatenate(
            [band[g, tops, j * DEPTH : j * DEPTH + span * GROUP] for j in side], axis=1
        )
        out = jnp.dot(lhs, rhs, preferred_element_type=F32)
        halo[:, at, :] = out.reshape(blocks, GROUP, lanes)


def turned_by(value, slots):
    lanes = value.shape[-1]
    if isinstance(slots, int):
        shift = SLOT * slots % lanes
        return pltpu.roll(value, shift, 1) if shift else value
    return pltpu.roll(value, lax.rem(SLOT * slots + lanes, lanes), 1)


def norm_rows(a_ref, base, off, count, halo, gain, out):
    _, chans, lanes = a_ref.shape
    blocks = halo.shape[0]
    edge = edge_lanes((chans, lanes))
    for r in range(count):
        extra = turned_by(halo[(off + r) % blocks], -(base // blocks + (off + r) // blocks))
        a = a_ref[base + off + r] + jnp.where(edge, extra, 0.0)
        center = a - jnp.mean(a, axis=0, keepdims=True)
        var = jnp.mean(center * center, axis=0, keepdims=True)
        normed = (center * lax.rsqrt(var + 1e-06) * gain).astype(BF)
        out[:, r * lanes : (r + 1) * lanes] = normed


def branch_of(normed, up_t, down_t):
    z = jnp.dot(up_t, normed, preferred_element_type=F32)
    h = twice_gelu(z.astype(BF))
    return jnp.dot(down_t, h, preferred_element_type=F32)


def atmos_kernel(layer, near, members, count, steps, *refs):
    x_ref, a_ref, g_ref, up_ref, dn_ref, s_ref = refs[:6]
    refs = refs[6:]
    even, odd = refs[-2:]
    rows, chans, lanes = x_ref.shape
    base = 0
    if layer == 0:
        first_ref, second_ref, band_ref, y_ref, p_ref, xe, halo = refs[:-2]
        blocks = halo.shape[0]
        packed = [None] * blocks
        keep = edge_lanes((chans, lanes)).astype(F32).astype(BF)
    else:
        rank = lax.axis_index("member")
        half = members // 2
        upper = (rank >= half) if near else (rank < half)
        base = jnp.where(upper, rows - steps * count, 0)
        if near:
            fw_ref, _, old_ref, halo, y_ref, keep_ref, give_ref, flux = refs[:-2]
        else:
            fw_ref, first_ref, second_ref, band_ref = refs[:4]
            y_ref, keep_ref, give_ref, flux, halo, xe = refs[4:-2]
    if near:
        flux[...] = old_ref[...]
    else:
        halo_conv(first_ref, second_ref, band_ref, True, halo_matrix(lanes), xe, halo)
        if layer == 1:
            blank = jnp.zeros((HALO,) + flux.shape[1:], BF)
            flux[0:HALO] = blank
            flux[rows + HALO : rows + 2 * HALO] = blank
    up_t = transposed(up_ref[layer])
    dn_t = halved(dn_ref[layer])
    gain = spread(g_ref[layer : layer + 1], lanes)
    scale = spread(s_ref[layer : layer + 1], lanes)
    norm_rows(a_ref, base, 0, count, halo, gain, even)
    for step in range(steps):
        off = step * count
        now, later = (even, odd) if step % 2 == 0 else (odd, even)
        if step + 1 < steps:
            norm_rows(a_ref, base, off + count, count, halo, gain, later)
        branch = branch_of(now[...], up_t, dn_t)
        made = []
        for r in range(count):
            y = x_ref[base + off + r].astype(F32) + scale * branch[:, r * lanes : (r + 1) * lanes]
            made.append(y.astype(BF))
            y_ref[base + off + r] = made[r]
        if layer == 0:
            for r in range(count):
                q, slot = (off + r) % blocks, (off + r) // blocks
                moved = turned_by(made[r] * keep, slot)
                packed[q] = moved if packed[q] is None else packed[q] + moved
            if step % 4 == 3 or step + 1 == steps:
                for q in range(blocks):
                    p_ref[q] = packed[q] if step < 4 else p_ref[q] + packed[q]
                packed = [None] * blocks
        else:
            z = jnp.dot(fw_ref[...], jnp.concatenate(made, axis=1), preferred_element_type=F32)
            f = (0.5 * twice_gelu(z)).astype(BF)
            for r in range(count):
                flux[base + off + HALO + r] = f[:, r * lanes : (r + 1) * lanes]
    if layer == 1:
        share = rows // members
        for k in range(half):
            dst = rank ^ (k if near else half + k)
            chunk = flux[pl.ds(dst * share, share + 2 * HALO)]
            if k % 2:
                give_ref[k // 2] = chunk
            else:
                keep_ref[k // 2] = chunk


def atmos_block(layer, near, members, x, a, weights, others, count, steps):
    rows, chans, lanes = x.shape
    blocks = rows // SLOTS
    args = [x, a, *weights, *others]
    outs = [jax.ShapeDtypeStruct(x.shape, BF)]
    halo = jax.ShapeDtypeStruct((blocks, chans, lanes), F32)
    shifts = pltpu.VMEM((TAPS - 1, SPAN, chans, lanes), BF)
    if layer == 0:
        outs.append(jax.ShapeDtypeStruct((blocks, chans, lanes), BF))
        scratch = [shifts, pltpu.VMEM(halo.shape, F32)]
    else:
        flux = weights[-1].shape[0]
        share = rows // members
        field = (rows + 2 * HALO, flux, lanes)
        outs += [jax.ShapeDtypeStruct((members // 4, share + 2 * HALO, flux, lanes), BF)] * 2
        if near:
            scratch = [pltpu.VMEM(field, BF)]
        else:
            outs += [jax.ShapeDtypeStruct(field, BF), halo]
            scratch = [shifts]
    return pl.pallas_call(
        functools.partial(atmos_kernel, layer, near, members, count, steps),
        out_shape=outs,
        in_specs=[VMEM] * len(args),
        out_specs=[VMEM] * len(outs),
        scratch_shapes=scratch + [pltpu.VMEM((chans, count * lanes), BF)] * 2,
        input_output_aliases={7: 0} if near else {},
        compiler_params=params(BIG),
        cost_estimate=cost(8 * steps * count / rows),
        name="atmos_block",
    )(*args)


def add_kernel(keep_ref, got_ref, *out_refs):
    for n, ref in enumerate(out_refs):
        k = n + keep_ref.shape[0] - len(out_refs)
        ref[...] = (keep_ref[k].astype(F32) + got_ref[k].astype(F32)).astype(BF)


def add_pairs(keep, got, skip):
    count = keep.shape[0] - skip
    return pl.pallas_call(
        add_kernel,
        out_shape=[jax.ShapeDtypeStruct(keep.shape[1:], BF)] * count,
        in_specs=[VMEM] * 2,
        out_specs=[VMEM] * count,
        compiler_params=params(24),
        name="add_pairs",
    )(keep, got)


def send_xor(value, bits):
    members = lax.axis_size("member")
    return lax.ppermute(value, "member", [(i, i ^ bits) for i in range(members)])


def force_kernel(members, *refs):
    near_refs, flux_refs = refs[:2], refs[2 : members // 2 + 1]
    win_ref, land_ref, ice_ref, lift_ref, mid_ref, p_ref = refs[members // 2 + 1 :]
    lanes = land_ref.shape[1]
    rows = land_ref.shape[0]
    chans = mid_ref.shape[1]
    blocks = p_ref.shape[0]
    span, first, start = window(members, rows)
    total = near_refs[0][0].astype(F32) + near_refs[1][0].astype(F32)
    for ref in flux_refs:
        total = total + ref[...].astype(F32)
    low = (total / members).astype(BF)
    columns = jnp.concatenate([low[r] for r in range(span)], axis=1)
    terms = jnp.dot(lift_ref[...], columns, preferred_element_type=F32)
    keep = edge_lanes((chans, lanes)).astype(F32).astype(BF)
    packed = [None] * blocks
    for r in range(span):
        row = first + r
        safe = jnp.clip(row, 0, rows - 1)
        sea = (1 - land_ref[pl.ds(safe, 1), :]).astype(F32)
        ice = ice_ref[pl.ds(safe, 1), :].astype(F32)
        at = slice(r * lanes, (r + 1) * lanes)
        forcing = sea * ((1.0 - ice) * terms[:chans, at] + ice * terms[chans:, at])
        mid = win_ref[jnp.clip(row - start, 0, span - 1)].astype(F32) + forcing
        inside = (row >= 0) & (row < rows)
        mid = jnp.where(inside, mid, 0.0).astype(BF)
        mid_ref[r] = mid
        q, slot = r % blocks, r // blocks
        moved = mid * keep
        if slot:
            moved = pltpu.roll(moved, SLOT * slot, 1)
        packed[q] = moved if packed[q] is None else packed[q] + moved
    for q in range(blocks):
        p_ref[q] = packed[q]


def force(members, chunks, win, land, ice, lift):
    span, chans, lanes = win.shape
    return pl.pallas_call(
        functools.partial(force_kernel, members),
        out_shape=[
            jax.ShapeDtypeStruct((span, chans, lanes), BF),
            jax.ShapeDtypeStruct((OCEAN_BLOCKS, chans, lanes), BF),
        ],
        in_specs=[VMEM] * (len(chunks) + 4),
        out_specs=[VMEM] * 2,
        compiler_params=params(24),
        name="ocean_forcing",
    )(*chunks, win, land, ice, lift)


def ocean_kernel(mid_ref, a_ref, first_ref, second_ref, band_ref, land_ref, mat_ref, upt_ref, gain_ref, scale_ref, dn_ref, sw_ref, new_ref, surf_ref, xe, halo, normed):
    share, chans, lanes = new_ref.shape
    halo_conv(first_ref, second_ref, band_ref, False, mat_ref[...], xe, halo)
    scale = scale_ref[...]
    norm_rows(a_ref, 0, 0, share, halo, gain_ref[...], normed)
    branch = branch_of(normed[...], upt_ref[...], halved(dn_ref[...]))
    first = lax.axis_index("member") * share
    made = []
    for r in range(share):
        sea = (1 - land_ref[pl.ds(first + r, 1), :]).astype(F32)
        y = mid_ref[HALO + r].astype(F32) + scale * branch[:, r * lanes : (r + 1) * lanes]
        made.append((y * sea).astype(BF))
        new_ref[r] = made[r]
    surf = jnp.dot(
        sw_ref[...], jnp.concatenate(made, axis=1), preferred_element_type=F32
    )
    for r in range(share):
        surf_ref[r] = surf[:, r * lanes : (r + 1) * lanes].astype(BF)


def ocean_block(mid, a, edges, band, land, ready, down, surf_weight):
    share, chans, lanes = a.shape
    blocks = edges[0].shape[0]
    return pl.pallas_call(
        ocean_kernel,
        out_shape=[
            jax.ShapeDtypeStruct((share, chans, lanes), BF),
            jax.ShapeDtypeStruct((share, surf_weight.shape[0], lanes), BF),
        ],
        in_specs=[VMEM] * 12,
        out_specs=[VMEM] * 2,
        scratch_shapes=[
            pltpu.VMEM((TAPS - 1, OCEAN_BLOCKS + 2 * HALO, chans, lanes), BF),
            pltpu.VMEM((blocks, chans, lanes), F32),
            pltpu.VMEM((chans, share * lanes), BF),
        ],
        compiler_params=params(24),
        name="ocean_block",
    )(mid, a, *edges, band, land, *ready, down, surf_weight)


def pair_kernel(own_ref, got_ref, out_ref):
    out_ref[0] = own_ref[...]
    out_ref[1] = got_ref[...]


def make_pair(own, got):
    return pl.pallas_call(
        pair_kernel,
        out_shape=jax.ShapeDtypeStruct((2,) + own.shape, BF),
        in_specs=[VMEM] * 2,
        out_specs=VMEM,
        compiler_params=params(24),
        name="surface_pair",
    )(own, got)


def couple_kernel(ks, y_ref, land_ref, bw_ref, *refs):
    pair_refs = refs[: len(ks)]
    o_ref, buf, sems = refs[-3:]
    chans, lanes = y_ref.shape[1:]
    share = pair_refs[0].shape[1]
    rank = lax.axis_index("member")
    parity = rank % 2
    back_t = transposed(bw_ref[...])
    copies = []
    for n, (k, pair_ref) in enumerate(zip(ks, pair_refs)):
        first = ((rank // 2) ^ k) * 2 * share
        surf = [pair_ref[side ^ parity, r] for side in range(2) for r in range(share)]
        back = jnp.dot(back_t, jnp.concatenate(surf, axis=1), preferred_element_type=F32)
        for r in range(2 * share):
            sea = (1 - land_ref[pl.ds(first + r, 1), :]).astype(F32)
            out = y_ref[first + r].astype(F32) + sea * back[:, r * lanes : (r + 1) * lanes]
            buf[n, r] = out.astype(BF)
        copies.append(
            pltpu.make_async_copy(buf.at[n], o_ref.at[pl.ds(first, 2 * share)], sems.at[n])
        )
        copies[n].start()
    for copy in copies:
        copy.wait()


def couple(ks, y, land, back_weight, pairs, earlier):
    _, chans, lanes = y.shape
    count = len(ks)
    return pl.pallas_call(
        functools.partial(couple_kernel, ks),
        out_shape=jax.ShapeDtypeStruct(y.shape, BF),
        in_specs=[VMEM] * (3 + count) + [HBM] * len(earlier),
        out_specs=HBM,
        scratch_shapes=[
            pltpu.VMEM((count, 2 * pairs[0].shape[1], chans, lanes), BF),
            pltpu.SemaphoreType.DMA((count,)),
        ],
        input_output_aliases={3 + count: 0} if earlier else {},
        compiler_params=params(24),
        name="couple",
    )(y, land, back_weight, *pairs, *earlier)


def local(
    atmos,
    ocean,
    land_mask,
    ice_mask,
    atm_kernel,
    atm_gain,
    atm_up,
    atm_down,
    atm_scale,
    flux_weight,
    flux_lift,
    ocn_kernel,
    ocn_gain,
    ocn_up,
    ocn_down,
    ocn_scale,
    surf_weight,
    back_weight,
):
    members = lax.axis_size("member")
    half = members // 2
    state = atmos[0]
    rows = state.shape[0]
    blocks = rows // SLOTS
    small = 2 * blocks
    atm = (atm_gain, atm_up, atm_down.transpose(0, 2, 1), atm_scale)
    taps = atm_kernel.transpose(1, 2, 0, 3)

    edges = neighbours(pack(state, 2 * small), True)
    a, band = convolve(0, state, taps, blocks)
    steps = rows // small
    near_steps = (rows // 2) // small - 1
    state, packed = atmos_block(0, False, members, state, a, atm, [*edges, band], small, steps)

    edges = neighbours(packed, True)
    a, band = convolve(1, state, taps, blocks)
    weights = (*atm, flux_weight.T)
    partly, far_keep, give, flux, halo = atmos_block(
        1, False, members, state, a, weights, [*edges, band], small, steps - near_steps
    )
    far_got = send_xor(give, 1)
    state, keep, give = atmos_block(
        1, True, members, state, a, weights, [partly, flux, halo], small, near_steps
    )
    far_got, give = lax.optimization_barrier((far_got, give))
    far_sums = add_pairs(far_keep, far_got, 0)
    give, *far_sums = lax.optimization_barrier((give, *far_sums))
    sent = [send_xor(far_sums[k], half + 2 * k) for k in reversed(range(len(far_sums)))]
    got = send_xor(give, 1)
    sums = add_pairs(keep, got, 1)
    sent += [send_xor(part, 2 * k + 2) for k, part in enumerate(sums)]
    band, *ready, lift, win = prepare_ocean(
        members, ocn_kernel, ocn_gain, ocn_up, ocn_scale, flux_lift, ocean, sums[0]
    )
    sent = [keep, got] + sent
    mid, packed = force(members, sent, win, land_mask, ice_mask, lift)
    edges = neighbours(packed, False)
    a = ocean_conv(mid, band)
    ocean_rows, surface = ocean_block(
        mid, a, edges, band, land_mask, ready, ocn_down.T, surf_weight.T
    )
    own = make_pair(surface, send_xor(surface, 1))
    rest = tuple(range(half - 1, 0, -1))
    pairs = [send_xor(own, 2 * k) for k in rest]
    out = couple((0,), state, land_mask, back_weight, [own], [])
    out = couple(rest[:1], state, land_mask, back_weight, pairs[:1], [out])
    out = couple(rest[1:], state, land_mask, back_weight, pairs[1:], [out])
    return (out[None], ocean_rows)


def solution(mesh):
    in_specs = (
        P("member", None, None, "lon"),
        P(None, None, "lon"),
        P(None, "lon"),
        P(None, "lon"),
    ) + (P(),) * 14
    out_specs = (P("member", None, None, "lon"), P("member", None, "lon"))
    return jax.shard_map(local, mesh=mesh, in_specs=in_specs, out_specs=out_specs, check_vma=False)
```
